256 devices in a mesh: tile: 32 (over y_hi, z, core), sub: 2 (over y_lo), rep: 4 (over x).
Axes of the slice: x: 4, y: 4 (y_hi: 2, y_lo: 2; y = y_hi * 2 + y_lo), z: 8, core: 2. Of those that a mesh axis runs over, the one named last changes fastest.
Arguments:
- initial_state: bfloat16 [24, 64, 64, 128], P('rep', ('tile', 'sub')), parts along dimension 0, may hold values from -6 to 6
- state_tangent: bfloat16 [24, 64, 64, 128], P('rep', ('tile', 'sub')), parts along dimension 0, may hold values from -6 to 6
- cotangent: bfloat16 [24, 64, 64, 128], P('rep', ('tile', 'sub')), parts along dimension 0, may hold values from -6 to 6
- weight_first: bfloat16 [9, 128, 128], replicated, may hold values from -0.1875 to 0.1875
- weight_second: bfloat16 [9, 128, 128], replicated, may hold values from -0.1875 to 0.1875
- tangent_first: bfloat16 [9, 128, 128], replicated, may hold values from -0.1875 to 0.1875
- tangent_second: bfloat16 [9, 128, 128], replicated, may hold values from -0.1875 to 0.1875
- neighbour: int32 [6, 4], replicated, may hold values from 0 to 23, as said below
Outputs:
- next_state: bfloat16 [24, 64, 64, 128], P('rep', ('tile', 'sub')), parts along dimension 0
- adjoint: bfloat16 [24, 64, 64, 128], P('rep', ('tile', 'sub')), parts along dimension 0
- adjoint_tangent: bfloat16 [24, 64, 64, 128], P('rep', ('tile', 'sub')), parts along dimension 0
- weight_gradient: float32 [8, 9, 128, 128], P('rep'), parts along dimension 0
- hessian_product: float32 [8, 9, 128, 128], P('rep'), parts along dimension 0
The draws below stay inside these ranges and needn't reach their ends.
There are 4 independent parts, one for each index of `rep`. The reference program is written for one: setup_inputs(seed, part) draws one part's arguments, and reference() takes and returns one part's arrays. A program takes and returns all parts, laid end to end along the dimension named above; an argument that names none is the same for every part. Nothing has to cross between parts.
Inputs may be any that keep to these rules, and one draw needn't show every extreme that they name: neighbour[f, s] = 4 g + t means that side s of face f meets side t of face g; the relation is symmetric, each value appears once, no face meets itself, and the six faces close into the surface of a cube, every face seen from outside.
All inputs are finite; a program needn't handle non-finite values.
Results may differ from the reference program's by a relative error of at most 0.0049.
Values may be sent and summed in bfloat16 or wider, within the bound.
A program may use at most 128 MiB of HBM per device.

```python
import jax
import jax.numpy as jnp

C = 128
FACE = 64


cube_gluing = [[18, 7, 20, 13], [17, 11, 21, 1], [16, 15, 22, 5], [19, 3, 23, 9], [8, 4, 0, 12], [2, 6, 10, 14]]


def draw_neighbour(key, part):
    key = jax.random.fold_in(key, 11)
    label_key, turn_key = jax.random.split(key)
    relabel = jax.random.permutation(label_key, 6).astype(jnp.int32)
    turns = jax.random.randint(turn_key, (6,), 0, 4).astype(jnp.int32)
    gluing = jnp.asarray(cube_gluing, dtype=jnp.int32)
    old_face = jnp.arange(6, dtype=jnp.int32)[:, None]
    old_side = jnp.arange(4, dtype=jnp.int32)[None, :]
    target_face = gluing // 4
    target_side = gluing % 4
    new_slot = relabel[old_face] * 4 + (old_side + turns[old_face]) % 4
    new_value = relabel[target_face] * 4 + (target_side + turns[target_face]) % 4
    table = jnp.zeros((24,), jnp.int32).at[new_slot.reshape(24)].set(new_value.reshape(24))
    return table.reshape(6, 4)


def levels(key, extent, pieces, smallest, largest):
    loudness = 1.0
    for axis_at, blocks in pieces:
        heights = jax.random.uniform(jax.random.fold_in(jax.random.fold_in(key, 6), axis_at), (blocks,), jnp.float32, smallest / len(pieces), largest / len(pieces))
        loudness = loudness * jnp.repeat(jnp.exp(heights), extent[axis_at] // blocks).reshape((-1,) + (1,) * (len(extent) - 1 - axis_at))
    return loudness


def gaussian(own_key, shape, deviation, limit, cuts=(), kind=jnp.bfloat16):
    result = jax.random.normal(own_key, shape, jnp.float32) * deviation
    if len(cuts) > 0:
        result = levels(own_key, shape, cuts, -0.22, 0.18) * result
    return jnp.clip(result, min=-limit, max=limit).astype(kind)


def setup_inputs(seed: int = 0, part: int = 0) -> dict:
    splits = jax.random.split(jax.random.key(seed), 9)
    part_keys = jax.random.split(jax.random.fold_in(splits[8], part), 9)
    return {
        "initial_state": gaussian(part_keys[0], (6, FACE, FACE, C), 1.0, 6.0, ((1, 64),)),
        "state_tangent": gaussian(part_keys[1], (6, FACE, FACE, C), 1.0, 6.0, ((1, 64),)),
        "cotangent": gaussian(part_keys[2], (6, FACE, FACE, C), 1.0, 6.0, ((1, 64),)),
        "weight_first": gaussian(splits[3], (9, C, C), (9 * C) ** -0.5, 0.1875),
        "weight_second": gaussian(splits[4], (9, C, C), (9 * C) ** -0.5, 0.1875),
        "tangent_first": gaussian(splits[5], (9, C, C), (9 * C) ** -0.5, 0.1875),
        "tangent_second": gaussian(splits[6], (9, C, C), (9 * C) ** -0.5, 0.1875),
        "neighbour": draw_neighbour(jax.random.fold_in(splits[8], 71), part),
    }


step_size = 0.5

def side_flips(neighbour):
    other_side = neighbour % 4
    own_side = jnp.arange(4, dtype=jnp.int32)[None, :]
    return (own_side < 2) == (other_side < 2)

def pad_faces(face_field, neighbour):
    face_width = face_field.shape[1]
    edge_table = jnp.stack([face_field[:, 0], face_field[:, :, face_width - 1], face_field[:, face_width - 1], face_field[:, :, 0]], axis=1)
    flat_edges = edge_table.reshape((24,) + edge_table.shape[2:])
    margins = jnp.take(flat_edges, neighbour.reshape(24).astype(jnp.int32), axis=0).reshape(edge_table.shape)
    margins = jnp.where(side_flips(neighbour)[:, :, None, None], margins[:, :, ::-1], margins)
    middle = jnp.concatenate([margins[:, 3][:, :, None], face_field, margins[:, 1][:, :, None]], axis=2)
    upper_row = jnp.pad(margins[:, 0], ((0, 0), (1, 1), (0, 0)))
    lower_row = jnp.pad(margins[:, 2], ((0, 0), (1, 1), (0, 0)))
    return jnp.concatenate([upper_row[:, None], middle, lower_row[:, None]], axis=1)

def conv_valid(padded, kernel):
    height = padded.shape[1] - 2
    face_width = padded.shape[2] - 2
    total_sum = jnp.zeros((padded.shape[0], height, face_width, kernel.shape[2]), jnp.float32)
    for tap_row in range(3):
        for tap_col in range(3):
            window = padded[:, tap_row:tap_row + height, tap_col:tap_col + face_width].astype(jnp.float32)
            total_sum = total_sum + jnp.einsum('fijc,cd->fijd', window, kernel[3 * tap_row + tap_col].astype(jnp.float32))
    return total_sum

def spread(gradient, kernel, neighbour):
    zero_field = jnp.zeros(gradient.shape[:3] + (kernel.shape[1],), jnp.float32)
    _, pullback = jax.vjp(lambda source_field: conv_valid(pad_faces(source_field, neighbour), kernel), zero_field)
    return pullback(gradient.astype(jnp.float32))[0]

def weight_term(padded, gradient):
    height = gradient.shape[1]
    face_width = gradient.shape[2]
    tap_terms = []
    for tap_row in range(3):
        for tap_col in range(3):
            window = padded[:, tap_row:tap_row + height, tap_col:tap_col + face_width].astype(jnp.float32)
            tap_terms.append(jnp.einsum('fijc,fijd->cd', window, gradient.astype(jnp.float32)))
    return jnp.stack(tap_terms)

def reference(initial_state, state_tangent, cotangent, weight_first, weight_second, tangent_first, tangent_second, neighbour):
    face_width = initial_state.shape[1]
    padded_state = pad_faces(initial_state, neighbour)
    padded_tangent = pad_faces(state_tangent, neighbour)
    hidden = conv_valid(padded_state, weight_first)
    squash = jnp.tanh(hidden)
    derivative = 1.0 - squash * squash
    activated = squash.astype(jnp.bfloat16)
    hidden_tangent = conv_valid(padded_tangent, weight_first) + conv_valid(padded_state, tangent_first)
    activated_tangent = (derivative * hidden_tangent).astype(jnp.bfloat16)
    padded_act = pad_faces(activated, neighbour)
    padded_act_tangent = pad_faces(activated_tangent, neighbour)
    next_state = (initial_state.astype(jnp.float32) + step_size * conv_valid(padded_act, weight_second)).astype(jnp.bfloat16)
    seed_field = (step_size * cotangent.astype(jnp.float32)).astype(jnp.bfloat16)
    backward = spread(seed_field, weight_second, neighbour)
    backward_tangent = spread(seed_field, tangent_second, neighbour)
    delta_field = (derivative * backward).astype(jnp.bfloat16)
    delta_tangent = (derivative * backward_tangent - 2.0 * squash * derivative * hidden_tangent * backward).astype(jnp.bfloat16)
    adjoint = (cotangent.astype(jnp.float32) + spread(delta_field, weight_first, neighbour)).astype(jnp.bfloat16)
    adjoint_tangent = (spread(delta_tangent, weight_first, neighbour) + spread(delta_field, tangent_first, neighbour)).astype(jnp.bfloat16)
    grad_first = weight_term(padded_state, delta_field)
    grad_second = weight_term(padded_act, seed_field)
    curve_first = weight_term(padded_tangent, delta_field) + weight_term(padded_state, delta_tangent)
    curve_second = weight_term(padded_act_tangent, seed_field)
    weight_gradient = jnp.stack([grad_first, grad_second]) / face_width
    hessian_product = jnp.stack([curve_first, curve_second]) / face_width
    return (next_state, adjoint, adjoint_tangent, weight_gradient, hessian_product)
```

```python
import functools

import jax
import jax.numpy as jnp
from jax import lax
from jax.experimental import pallas as pl
from jax.experimental.pallas import tpu as pltpu
from jax.sharding import PartitionSpec as P

MESH = pl.DeviceIdType.MESH
BF = jnp.bfloat16
F32 = jnp.float32
C = 128
K9 = 9 * C
SIDES = 16


def dot(a, b):
    return jnp.dot(a, b, preferred_element_type=F32)


def dot_t(a, b):
    return lax.dot_general(a, b, (((0,), (0,)), ((), ())), preferred_element_type=F32)


def iota(shape, dim):
    return lax.broadcasted_iota(jnp.int32, shape, dim)


def onehot(mask):
    return jnp.where(mask, 1.0, 0.0).astype(BF)


def kernel(
    n,
    ny,
    nz,
    u_ref,
    v_ref,
    c_ref,
    w1_ref,
    w2_ref,
    t1_ref,
    t2_ref,
    nb_ref,
    next_ref,
    adj_ref,
    adt_ref,
    out_ref,
    rb,
    mb,
    ebuf,
    hm,
    zs,
    rx,
    mt,
    sel,
    selh,
    amat,
    bmat,
    c0mat,
    c2mat,
    wraw,
    wf1,
    ws1,
    ws2,
    padf,
    padz,
    tu,
    tv,
    ts,
    tx,
    ty,
    sq,
    aext,
    dd,
    field,
    gsum,
    gs,
    gr,
    yf,
    ys,
    yr,
    zf,
    zst,
    zr,
    lsem,
    bulk_s,
    bulk_r,
    e_s,
    e_r,
    hm_s,
    rx_r,
    z_s,
    z_r,
    mt_s,
    mt_r,
    c_s,
    c_r,
    y_s,
    y_r,
    zz_s,
    zz_r,
    gz_s,
    gz_r,
    gy_s,
    gy_r,
    gc_s,
    gc_r,
):
    F = n
    cells = 6 * F
    rep = lax.axis_index("rep")
    r = lax.axis_index("tile") * 2 + lax.axis_index("sub")
    core = lax.rem(lax.div(r, 2), 2)
    z = lax.rem(lax.div(r, 4), nz)
    yhi = lax.div(r, 4 * nz)
    ylo = lax.rem(r, 2)
    y = yhi * 2 + ylo

    def dev(p):
        return (lax.div(p, 2), lax.rem(p, 2), rep)

    def make(hi, zc, co, lo):
        return ((hi * nz + zc) * 2 + co) * 2 + lo

    up = lax.rem(r + n - 1, n)
    dn = lax.rem(r + 1, n)
    mirror = n - 1 - r
    partner = make(yhi, z, 1 - core, ylo)

    def ypeer(d):
        q = lax.rem(y + d, ny)
        return q, make(lax.div(q, 2), z, core, lax.rem(q, 2))

    def zpeer(d):
        q = lax.rem(z + d, nz)
        return q, make(yhi, q, core, ylo)

    is0 = r == 0
    is1 = r == n - 1
    ishub = jnp.logical_or(is0, is1)

    def rcopy(src, dst, ssem, rsem, p):
        return pltpu.make_async_remote_copy(
            src_ref=src,
            dst_ref=dst,
            send_sem=ssem,
            recv_sem=rsem,
            device_id=dev(p),
            device_id_type=MESH,
        )

    loads = [pltpu.make_async_copy(ref, rb.at[0, i, 1], lsem.at[i]) for i, ref in enumerate((u_ref, v_ref, c_ref))]
    wloads = [pltpu.make_async_copy(ref, wraw.at[i], lsem.at[3 + i]) for i, ref in enumerate((w1_ref, t1_ref, w2_ref, t2_ref))]
    for cp in loads + wloads:
        cp.start()

    barrier = pltpu.get_barrier_semaphore()

    def greet(p):
        pl.semaphore_signal(barrier, inc=1, device_id=dev(p), device_id_type=MESH)

    @pl.when(ishub)
    def _():
        def body(i, carry):
            greet(lax.rem(r + i, n))
            return carry

        lax.fori_loop(1, n, body, 0)

    @pl.when(r != 0)
    def _():
        greet(0)

    @pl.when(r != n - 1)
    def _():
        greet(n - 1)

    for p in (up, dn, mirror, partner):
        greet(p)
    for d in range(1, ny):
        greet(ypeer(d)[1])
    for d in range(1, nz):
        greet(zpeer(d)[1])

    nbs = [[nb_ref[f, s] for s in range(4)] for f in range(6)]
    x = iota((48, 160), 0)
    yy = iota((48, 160), 1)
    xs = x & 15
    xsd = jnp.where(xs < 8, 1, 3)
    xnb = jnp.full((48, 160), -1, jnp.int32)
    for f in range(6):
        xnb = jnp.where(xs == f, nbs[f][1], xnb)
        xnb = jnp.where(xs == 8 + f, nbs[f][3], xnb)
    ym = jnp.where(yy >= 48, yy - 48, yy)
    ysd = jnp.where((ym & 15) < 8, 1, 3)
    yz = (yy - 96) & 31
    isz = yy >= 96
    yg = jnp.where(isz, yz & 7, ym & 7)
    yt = jnp.where(isz, jnp.where(yy >= 128, 2, 0), ysd)
    yfield = jnp.where(isz, yz >> 3, ym >> 4)
    way = jnp.where(isz, 1, jnp.where(yy >= 48, jnp.where(xsd == ysd, 1, 0), jnp.where(xsd == ysd, 0, 1)))
    sel[...] = onehot((xnb == 4 * yg + yt) & ((x >> 4) == yfield) & (yg < 6) & (way == 1))
    x = iota((64, 48), 0)
    yy = iota((64, 48), 1)
    xnb = jnp.full((64, 48), -1, jnp.int32)
    for f in range(6):
        xnb = jnp.where((x & 7) == f, jnp.where(x < 32, nbs[f][0], nbs[f][2]), xnb)
    yt = jnp.where((yy & 15) < 8, 1, 3)
    selh[...] = onehot((xnb == 4 * (yy & 7) + yt) & (((x & 31) >> 3) == (yy >> 4)) & ((yy & 7) < 6))

    def chosen(s, code, offset):
        t = code & 3
        flipped = (s < 2) == (t < 2)
        along = jnp.where(flipped, 1 - offset, offset - 1)
        row_tap = jnp.where(t == 0, 0, jnp.where(t == 2, 2, 1 - along))
        col_tap = jnp.where(t == 1, 2, jnp.where(t == 3, 0, 1 - along))
        return 3 * row_tap + col_tap

    xs = iota((SIDES, C), 0)
    code = jnp.full((SIDES, C), 0, jnp.int32)
    for f in range(6):
        code = jnp.where(xs == f, nbs[f][1], code)
        code = jnp.where(xs == 8 + f, nbs[f][3], code)
    side_taps = [chosen(jnp.where(xs < 8, 1, 3), code, o) for o in range(3)]

    hub_side = jnp.where(is0, 0, 2)
    hub_nb = [jnp.where(is0, nbs[f][0], nbs[f][2]) for f in range(6)]
    hub_flip = [((hub_side < 2) == ((code_f & 3) < 2)).astype(jnp.int32) for code_f in hub_nb]

    def per_face(face, values, start):
        result = jnp.full(face.shape, start, jnp.int32)
        for f in range(6):
            result = jnp.where(face == f, values[f], result)
        return result

    @pl.when(ishub)
    def _():
        a = iota((8 * F, cells), 0)
        b = iota((8 * F, cells), 1)
        g = a & 7
        pos = a >> 3
        target = g * F + jnp.where(per_face(g, hub_flip, 0) == 1, F - 1 - pos, pos)
        amat[...] = onehot((b == target) & (g < 6))

    def edges(ph, i):
        row = rb[ph, i, 1].astype(F32)
        zero = jnp.zeros((2, C), F32)
        return jnp.concatenate([row[:, F - 1], zero, row[:, 0], zero], axis=0).astype(BF)

    def prepare(ph):
        for i in range(3):
            ebuf[ph, 16 * i : 16 * i + 16] = edges(ph, i)
        hm[ph] = dot(selh[...], ebuf[ph, 0:48]).astype(BF)

        @pl.when(ishub)
        def _():
            parts = []
            for i in range(3):
                parts.append(dot(amat[...], rb[ph, i, 1].reshape(cells, C)).reshape(F, 8, C))
            parts.append(jnp.zeros((F, 8, C), F32))
            zs[ph] = jnp.concatenate(parts, axis=1).astype(BF)

        @pl.when(is0)
        def _():
            rx[ph, 0] = hm[ph, 0:32]
            ebuf[ph, 96:128] = zs[ph, 0]

        @pl.when(is1)
        def _():
            rx[ph, n - 1] = hm[ph, 32:64]
            ebuf[ph, 128:160] = zs[ph, n - 1]

    def e_copy(ph):
        return rcopy(ebuf.at[ph, pl.ds(0, 48)], ebuf.at[ph, pl.ds(48, 48)], e_s.at[ph], e_r.at[ph], mirror)

    def hm_copy(ph, h):
        return rcopy(
            hm.at[ph, pl.ds(32 * h, 32)],
            rx.at[ph, r],
            hm_s.at[ph, h],
            rx_r.at[ph, r],
            (n - 1) * h,
        )

    def z_copy(ph, h, p):
        return rcopy(zs.at[ph, p], ebuf.at[ph, pl.ds(96 + 32 * h, 32)], z_s.at[ph, p], z_r.at[ph, h], p)

    def bulk_copy(ph, i, way):
        return rcopy(
            rb.at[ph, i, 1],
            rb.at[ph, i, 2 if way == 0 else 0],
            bulk_s.at[ph, i, way],
            bulk_r.at[ph, i, way],
            up if way == 0 else dn,
        )

    def mt_copy(ph, way):
        return rcopy(
            mt.at[ph, 1],
            mt.at[ph, 2 if way == 0 else 0],
            mt_s.at[ph, way],
            mt_r.at[ph, way],
            up if way == 0 else dn,
        )

    def hub_loop(step):
        def body(i, carry):
            step(lax.rem(r + i, n))
            return carry

        lax.fori_loop(1, n, body, 0)

    def send(ph):
        for h, here in ((0, is0), (1, is1)):

            @pl.when(here)
            def _():
                hub_loop(lambda p: z_copy(ph, h, p).start())

            @pl.when(jnp.logical_not(here))
            def _():
                hm_copy(ph, h).start()

        e_copy(ph).start()
        for i in range(3):
            for way in range(2):
                bulk_copy(ph, i, way).start()

    def margins(ph):
        e_copy(ph).wait()
        for h, here in ((0, is0), (1, is1)):

            @pl.when(jnp.logical_not(here))
            def _():
                z_copy(ph, h, 0).wait_recv()

        mt[ph, 1] = dot(sel[...], ebuf[ph]).astype(BF)
        for way in range(2):
            mt_copy(ph, way).start()

    def hub_row(ph, spreads):
        @pl.when(ishub)
        def _():
            hub_loop(lambda p: rcopy(hm.at[ph, pl.ds(0, 32)], rx.at[ph, p], hm_s.at[ph, 0], rx_r.at[ph, p], p).wait_recv())
            slot = jnp.where(is0, 0, 2)
            got = rx[ph].astype(F32)
            for i in range(3):
                piece = got[:, 8 * i : 8 * i + 8].reshape(8 * F, C).astype(BF)
                row = dot(bmat[...], piece)
                row = row + dot(c0mat[...], rb[ph, i, 1].reshape(cells, C))
                row = row + dot(c2mat[...], rb[ph, i, slot].reshape(cells, C))
                row = row.astype(BF).reshape(6, F, C)
                if i in spreads:
                    mb[ph, i] = row
                    rb[ph, i, slot] = jnp.zeros((6, F, C), BF)
                else:
                    rb[ph, i, slot] = row

        @pl.when(is0)
        def _():
            mt[ph, 0] = jnp.zeros((48, C), BF)

        @pl.when(is1)
        def _():
            mt[ph, 2] = jnp.zeros((48, C), BF)

    def receive(ph, spreads):
        for way in range(2):
            for i in range(3):
                bulk_copy(ph, i, way).wait()
            mt_copy(ph, way).wait()
        hub_row(ph, spreads)

    def finish_sends(ph):
        for h, here in ((0, is0), (1, is1)):

            @pl.when(here)
            def _():
                hub_loop(lambda p: z_copy(ph, h, p).wait_send())

            @pl.when(jnp.logical_not(here))
            def _():
                hm_copy(ph, h).wait_send()

    def forward_taps(ph, i, dst):
        for a in range(3):
            padf[:, 8 : 8 + F] = rb[ph, i, a].astype(F32)
            line = mt[ph, a, 16 * i : 16 * i + 16].astype(F32)
            for f in range(6):
                padf[f, 7:8] = line[8 + f : 9 + f]
                padf[f, 8 + F : 9 + F] = line[f : f + 1]
            for b in range(3):
                k = 3 * a + b
                dst[0:cells, k * C : k * C + C] = padf[:, 7 + b : 7 + b + F].reshape(cells, C).astype(BF)

    def spread_taps(ph, i, dst, extra, scale):
        for a in range(3):
            padz[:, 8 : 8 + F] = rb[ph, i, a].astype(F32) * scale
            for b in range(3):
                k = 8 - (3 * a + b)
                dst[0:cells, k * C : k * C + C] = padz[:, 7 + b : 7 + b + F].reshape(cells, C).astype(BF)
        lines = [mt[ph, o, 16 * i : 16 * i + 16].astype(F32) * scale for o in range(3)]
        for k in range(9):
            total = jnp.zeros((SIDES, C), F32)
            for o in range(3):
                total = jnp.where(side_taps[o] == k, lines[o], total)
            dst[cells : cells + SIDES, k * C : k * C + C] = total.astype(BF)

        @pl.when(ishub)
        def _():
            padz[:, 8 : 8 + F] = mb[ph, i].astype(F32) * scale
            for f in range(6):
                picks = [chosen(hub_side, hub_nb[f], o) for o in range(3)]
                shifted = [padz[f, 7 + o : 7 + o + F] for o in range(3)]
                for k in range(9):
                    total = jnp.zeros((F, C), F32)
                    for o in range(3):
                        total = jnp.where(picks[o] == k, shifted[o], total)
                    extra[f * F : f * F + F, k * C : k * C + C] = total.astype(BF)

    def spread(dst, extra, weights, width):
        result = dot(dst[...], weights)
        field[:, :, 0:width] = result[0:cells].reshape(6, F, width)
        for f in range(6):
            field[f, F - 1 : F, 0:width] += result[cells + f : cells + f + 1]
            field[f, 0:1, 0:width] += result[cells + 8 + f : cells + 9 + f]

        @pl.when(ishub)
        def _():
            field[:, :, 0:width] += dot(extra[...], weights).reshape(6, F, width)

        return field[:, :, 0:width].reshape(cells, width)

    for cp in loads:
        cp.wait()
    prepare(0)
    base = 2 + 1 + 1 + (ny - 1) + (nz - 1)
    pl.semaphore_wait(barrier, base + 2 + jnp.where(ishub, n - 2, 0))
    send(0)

    padz[...] = jnp.zeros(padz.shape, F32)
    for cp in wloads:
        cp.wait()
    wf1[:, 0:C] = wraw[0]
    wf1[:, C : 2 * C] = wraw[1]
    for k in range(9):
        rows = slice(k * C, k * C + C)
        ws1[rows, 0:C] = wraw[0, rows].astype(F32).T.astype(BF)
        ws1[rows, C : 2 * C] = wraw[1, rows].astype(F32).T.astype(BF)
        ws2[rows, 0:C] = wraw[2, rows].astype(F32).T.astype(BF)
        ws2[rows, C : 2 * C] = wraw[3, rows].astype(F32).T.astype(BF)

    @pl.when(ishub)
    def _():
        a = iota((cells, 8 * F), 0)
        b = iota((cells, 8 * F), 1)
        face = lax.div(a, F)
        pos = a - face * F
        pos = jnp.where(per_face(face, hub_flip, 0) == 1, F - 1 - pos, pos)
        column = per_face(face, [code_f & 1 for code_f in hub_nb], 0)
        bmat[...] = onehot((b == 8 * pos + face) & (column == 1))
        a = iota((cells, cells), 0)
        b = iota((cells, cells), 1)
        face = lax.div(a, F)
        pos = a - face * F
        code_a = per_face(face, hub_nb, 0)
        other = (code_a >> 2) * F
        c0mat[...] = onehot(((code_a & 3) == hub_side) & (b == other + F - 1 - pos))
        c2mat[...] = onehot(((code_a & 3) == 2 - hub_side) & (b == other + pos))

    margins(0)
    receive(0, (2,))

    forward_taps(0, 0, tu)
    forward_taps(0, 1, tv)
    spread_taps(0, 2, ts, tx, 0.5)
    joined = dot(tu[...], wf1[...])
    hidden = joined[:, 0:C]
    hidden_tangent = joined[:, C : 2 * C] + dot(tv[...], wraw[0])
    squash = jnp.tanh(hidden)
    derivative = 1.0 - squash * squash
    act = squash.astype(BF)
    act_tangent = (derivative * hidden_tangent).astype(BF)
    aext[0:cells, 0:C] = act
    aext[0:cells, C : 2 * C] = act_tangent
    sq[...] = squash.reshape(6, F, C)
    dd[0:cells, 0:C] = (-2.0 * squash * derivative * hidden_tangent)
    back = spread(ts, tx, ws2[...], 2 * C)
    squash = sq[...].reshape(cells, C)
    derivative = 1.0 - squash * squash
    delta = (derivative * back[:, 0:C]).astype(BF)
    delta_tangent = (derivative * back[:, C : 2 * C] + dd[...] * back[:, 0:C]).astype(BF)
    rb[1, 0, 1] = aext[0:cells, 0:C].reshape(6, F, C)
    rb[1, 1, 1] = delta.reshape(6, F, C)
    rb[1, 2, 1] = delta_tangent.reshape(6, F, C)
    prepare(1)
    send(1)

    pair = jnp.concatenate([delta, delta_tangent], axis=1)
    first = dot_t(tu[...], pair)
    gsum[0, 0:K9] = first[:, 0:C]
    gsum[0, K9 : 2 * K9] = first[:, C : 2 * C] + dot_t(tv[...], delta)
    zero = jnp.zeros((2, C), F32)
    tangent = aext[0:cells, C : 2 * C].astype(F32).reshape(6, F, C)
    aext[cells : cells + SIDES, 0:C] = ebuf[1, 0:16]
    aext[cells : cells + SIDES, C : 2 * C] = jnp.concatenate(
        [tangent[:, F - 1], zero, tangent[:, 0], zero], axis=0
    ).astype(BF)
    second = dot_t(aext[...], ts[...])
    for k in range(9):
        gsum[1, k * C : k * C + C] = second[0:C, k * C : k * C + C]
        gsum[1, K9 + k * C : K9 + k * C + C] = second[C : 2 * C, k * C : k * C + C]

    @pl.when(ishub)
    def _():
        more = dot_t(aext[0:cells], tx[...])
        for k in range(9):
            gsum[1, k * C : k * C + C] += more[0:C, k * C : k * C + C]
            gsum[1, K9 + k * C : K9 + k * C + C] += more[C : 2 * C, k * C : k * C + C]

    rows_y = 2 * K9 // ny
    rows_z = rows_y // nz
    gs[...] = gsum[1 - core].astype(BF)
    core_copy = rcopy(gs, gr, c_s.at[0], c_r.at[0], partner)
    core_copy.start()
    core_copy.wait()
    total = gsum[core] + gr[...].astype(F32)
    yf[...] = total
    ys[...] = total.astype(BF)

    def y_copy(d):
        q, p = ypeer(d)
        return rcopy(ys.at[pl.ds(pl.multiple_of(q * rows_y, 16), rows_y)], yr.at[y], y_s.at[d], y_r.at[y], p)

    def y_wait(d):
        q, p = ypeer(d)
        return rcopy(ys.at[pl.ds(0, rows_y)], yr.at[q], y_s.at[d], y_r.at[q], p)

    for d in range(1, ny):
        y_copy(d).start()
    margins(1)
    for d in range(1, ny):
        y_copy(d).wait_send()
        y_wait(d).wait_recv()
    total = yf[pl.ds(pl.multiple_of(y * rows_y, 8), rows_y)]
    for d in range(1, ny):
        total = total + yr[ypeer(d)[0]].astype(F32)
    total = total.reshape(nz, rows_z, C)
    zf[...] = total
    zst[:, 0:rows_z] = total.astype(BF)
    if zst.shape[1] > rows_z:
        zst[:, rows_z:] = jnp.zeros((nz, zst.shape[1] - rows_z, C), BF)

    def z_sum_copy(d):
        q, p = zpeer(d)
        return rcopy(zst.at[q], zr.at[z], zz_s.at[d], zz_r.at[z], p)

    def z_sum_wait(d):
        q, p = zpeer(d)
        return rcopy(zst.at[q], zr.at[q], zz_s.at[d], zz_r.at[q], p)

    for d in range(1, nz):
        z_sum_copy(d).start()

    receive(1, (1, 2))
    forward_taps(1, 0, tu)
    change = dot(tu[...], wraw[2])
    next_ref[...] = (rb[0, 0, 1].astype(F32).reshape(cells, C) + 0.5 * change).astype(BF).reshape(6, F, C)
    spread_taps(1, 1, ts, tx, 1.0)
    back = spread(ts, tx, ws1[...], 2 * C)
    adj_ref[...] = (rb[0, 2, 1].astype(F32).reshape(cells, C) + back[:, 0:C]).astype(BF).reshape(6, F, C)
    dd[...] = back[:, C : 2 * C]
    spread_taps(1, 2, ty, tx, 1.0)
    back = spread(ty, tx, ws1[:, 0:C], C)
    adt_ref[...] = (dd[...] + back).astype(BF).reshape(6, F, C)

    for d in range(1, nz):
        z_sum_copy(d).wait_send()
        z_sum_wait(d).wait_recv()
    total = zf[z]
    for d in range(1, nz):
        total = total + zr[zpeer(d)[0], 0:rows_z].astype(F32)
    out_ref[core, y, z, 0:rows_z] = (total * (1.0 / F)).astype(BF)
    if zst.shape[1] > rows_z:
        out_ref[core, y, z, rows_z:] = jnp.zeros((zst.shape[1] - rows_z, C), BF)

    def gz_copy(d, q):
        return rcopy(out_ref.at[core, y, q], out_ref.at[core, y, q], gz_s.at[d], gz_r.at[q], zpeer(d)[1])

    for d in range(1, nz):
        gz_copy(d, z).start()
    for d in range(1, nz):
        gz_copy(d, z).wait_send()
        gz_copy(d, zpeer(d)[0]).wait_recv()

    def gy_copy(d, q):
        return rcopy(out_ref.at[core, q], out_ref.at[core, q], gy_s.at[d], gy_r.at[q], ypeer(d)[1])

    for d in range(1, ny):
        gy_copy(d, y).start()
    for d in range(1, ny):
        gy_copy(d, y).wait_send()
        gy_copy(d, ypeer(d)[0]).wait_recv()
    rcopy(out_ref.at[core], out_ref.at[core], gc_s.at[0], gc_r.at[0], partner).start()
    rcopy(out_ref.at[core], out_ref.at[core], gc_s.at[0], gc_r.at[0], partner).wait_send()
    rcopy(out_ref.at[1 - core], out_ref.at[1 - core], gc_s.at[0], gc_r.at[0], partner).wait_recv()
    finish_sends(0)
    finish_sends(1)


def on_device(n, ny, nz, u, v, c, w1, w2, t1, t2, nb):
    F = n
    cells = 6 * F
    rows_y = 2 * K9 // ny
    rows_z = rows_y // nz
    zp = -(-rows_z // 16) * 16
    u, v, c = (a.reshape(6, F, C) for a in (u, v, c))
    w1, w2, t1, t2 = (a.reshape(K9, C) for a in (w1, w2, t1, t2))
    vm = pltpu.VMEM
    dma = pltpu.SemaphoreType.DMA
    anywhere = pl.BlockSpec(memory_space=pl.ANY)
    inside = pl.BlockSpec(memory_space=pltpu.VMEM)
    row = jax.ShapeDtypeStruct((6, F, C), BF)
    nxt, adj, adt, out = pl.pallas_call(
        functools.partial(kernel, n, ny, nz),
        out_shape=(row, row, row, jax.ShapeDtypeStruct((2, ny, nz, zp, C), BF)),
        in_specs=[anywhere] * 7 + [pl.BlockSpec(memory_space=pltpu.SMEM)],
        out_specs=(inside,) * 4,
        scratch_shapes=[
            vm((2, 3, 3, 6, F, C), BF),
            vm((2, 3, 6, F, C), BF),
            vm((2, 160, C), BF),
            vm((2, 64, C), BF),
            vm((2, F, 32, C), BF),
            vm((2, F, 32, C), BF),
            vm((2, 3, 48, C), BF),
            vm((48, 160), BF),
            vm((64, 48), BF),
            vm((8 * F, cells), BF),
            vm((cells, 8 * F), BF),
            vm((cells, cells), BF),
            vm((cells, cells), BF),
            vm((4, K9, C), BF),
            vm((K9, 2 * C), BF),
            vm((K9, 2 * C), BF),
            vm((K9, 2 * C), BF),
            vm((6, F + 16, C), F32),
            vm((6, F + 16, C), F32),
            vm((cells, K9), BF),
            vm((cells, K9), BF),
            vm((cells + SIDES, K9), BF),
            vm((cells, K9), BF),
            vm((cells + SIDES, K9), BF),
            vm((6, F, C), F32),
            vm((cells + SIDES, 2 * C), BF),
            vm((cells, C), F32),
            vm((6, F, 2 * C), F32),
            vm((2, 2 * K9, C), F32),
            vm((2 * K9, C), BF),
            vm((2 * K9, C), BF),
            vm((2 * K9, C), F32),
            vm((2 * K9, C), BF),
            vm((ny, rows_y, C), BF),
            vm((nz, rows_z, C), F32),
            vm((nz, zp, C), BF),
            vm((nz, zp, C), BF),
            dma((7,)),
            dma((2, 3, 2)),
            dma((2, 3, 2)),
            dma((2,)),
            dma((2,)),
            dma((2, 2)),
            dma((2, n)),
            dma((2, n)),
            dma((2, 2)),
            dma((2, 2)),
            dma((2, 2)),
            dma((1,)),
            dma((1,)),
            dma((ny,)),
            dma((ny,)),
            dma((nz,)),
            dma((nz,)),
            dma((nz,)),
            dma((nz,)),
            dma((ny,)),
            dma((ny,)),
            dma((1,)),
            dma((1,)),
        ],
        compiler_params=pltpu.CompilerParams(
            collective_id=0, has_side_effects=True, vmem_limit_bytes=56 * 2**20
        ),
    )(u, v, c, w1, w2, t1, t2, nb)
    rows = out[:, :, :, :rows_z].astype(F32).reshape(2, 2, 9, C, C)
    shape = (6, 1, F, C)
    return nxt.reshape(shape), adj.reshape(shape), adt.reshape(shape), rows[:, 0], rows[:, 1]


def solution(mesh):
    n = mesh.shape["tile"] * mesh.shape["sub"]
    nz = 8 if n == 64 else 2
    ny = n // (2 * nz)
    field = P("rep", ("tile", "sub"), None, None)
    grads = P("rep", None, None, None)
    return jax.shard_map(
        functools.partial(on_device, n, ny, nz),
        mesh=mesh,
        in_specs=(field, field, field, P(), P(), P(), P(), P()),
        out_specs=(field, field, field, grads, grads),
        check_vma=False,
    )
```

```python
import functools

import jax
import jax.numpy as jnp
from jax import lax
from jax.experimental import pallas as pl
from jax.experimental.pallas import tpu as pltpu
from jax.sharding import PartitionSpec as P

MESH = pl.DeviceIdType.MESH
BF = jnp.bfloat16
F32 = jnp.float32
C = 128
K9 = 9 * C
SIDES = 16


def dot(a, b):
    return jnp.dot(a, b, preferred_element_type=F32)


def dot_t(a, b):
    return lax.dot_general(a, b, (((0,), (0,)), ((), ())), preferred_element_type=F32)


def iota(shape, dim):
    return lax.broadcasted_iota(jnp.int32, shape, dim)


def onehot(mask):
    return jnp.where(mask, 1.0, 0.0).astype(BF)


def kernel(
    n,
    ny,
    nz,
    u_ref,
    v_ref,
    c_ref,
    w1_ref,
    w2_ref,
    t1_ref,
    t2_ref,
    nb_ref,
    next_ref,
    adj_ref,
    adt_ref,
    out_ref,
    rb,
    mb,
    ebuf,
    hm,
    zs,
    rx,
    mt,
    sel,
    selh,
    amat,
    bmat,
    c0mat,
    c2mat,
    wraw,
    wf1,
    ws1,
    ws2,
    padf,
    padz,
    tu,
    tv,
    ts,
    tx,
    ty,
    sq,
    aext,
    dd,
    field,
    gsum,
    gs,
    gr,
    pf,
    ps,
    pr,
    qf,
    qs,
    qr,
    pz,
    pzf,
    pzr,
    qy,
    qyf,
    qyr,
    nbm,
    lsem,
    bulk_s,
    bulk_r,
    e_s,
    e_r,
    hm_s,
    rx_r,
    z_s,
    z_r,
    mt_s,
    mt_r,
    ar_s,
    ar_r,
):
    F = n
    cells = 6 * F
    rep = lax.axis_index("rep")
    r = lax.axis_index("tile") * 2 + lax.axis_index("sub")
    core = lax.rem(lax.div(r, 2), 2)
    z = lax.rem(lax.div(r, 4), nz)
    yhi = lax.div(r, 4 * nz)
    ylo = lax.rem(r, 2)
    y = yhi * 2 + ylo

    def dev(p):
        return (lax.div(p, 2), lax.rem(p, 2), rep)

    def make(hi, zc, co, lo):
        return ((hi * nz + zc) * 2 + co) * 2 + lo

    up = lax.rem(r + n - 1, n)
    dn = lax.rem(r + 1, n)
    mirror = n - 1 - r
    partner = make(yhi, z, 1 - core, ylo)

    def ypeer(d):
        q = lax.rem(y + d, ny)
        return q, make(lax.div(q, 2), z, core, lax.rem(q, 2))

    def zpeer(d):
        q = lax.rem(z + d, nz)
        return q, make(yhi, q, core, ylo)

    is0 = r == 0
    is1 = r == n - 1
    ishub = jnp.logical_or(is0, is1)

    def rcopy(src, dst, ssem, rsem, p):
        return pltpu.make_async_remote_copy(
            src_ref=src,
            dst_ref=dst,
            send_sem=ssem,
            recv_sem=rsem,
            device_id=dev(p),
            device_id_type=MESH,
        )

    nbload = pltpu.make_async_copy(nb_ref, nbm, lsem.at[7])
    nbload.start()
    loads = [pltpu.make_async_copy(ref, rb.at[0, i, 1], lsem.at[i]) for i, ref in enumerate((u_ref, v_ref, c_ref))]
    wloads = [pltpu.make_async_copy(ref, wraw.at[i], lsem.at[3 + i]) for i, ref in enumerate((w1_ref, t1_ref, w2_ref, t2_ref))]
    for cp in loads + wloads:
        cp.start()

    barrier = pltpu.get_barrier_semaphore()

    def greet(p):
        pl.semaphore_signal(barrier, inc=1, device_id=dev(p), device_id_type=MESH)

    @pl.when(ishub)
    def _():
        def body(i, carry):
            greet(lax.rem(r + i, n))
            return carry

        lax.fori_loop(1, n, body, 0)

    @pl.when(r != 0)
    def _():
        greet(0)

    @pl.when(r != n - 1)
    def _():
        greet(n - 1)

    for p in (up, dn, mirror, partner):
        greet(p)
    for d in range(1, ny):
        greet(ypeer(d)[1])
    for d in range(1, nz):
        greet(zpeer(d)[1])

    nbload.wait()
    nbs = [[nbm[f, s] for s in range(4)] for f in range(6)]
    x = iota((48, 160), 0)
    yy = iota((48, 160), 1)
    xs = x & 15
    xsd = jnp.where(xs < 8, 1, 3)
    xnb = jnp.full((48, 160), -1, jnp.int32)
    for f in range(6):
        xnb = jnp.where(xs == f, nbs[f][1], xnb)
        xnb = jnp.where(xs == 8 + f, nbs[f][3], xnb)
    ym = jnp.where(yy >= 48, yy - 48, yy)
    ysd = jnp.where((ym & 15) < 8, 1, 3)
    yz = (yy - 96) & 31
    isz = yy >= 96
    yg = jnp.where(isz, yz & 7, ym & 7)
    yt = jnp.where(isz, jnp.where(yy >= 128, 2, 0), ysd)
    yfield = jnp.where(isz, yz >> 3, ym >> 4)
    way = jnp.where(isz, 1, jnp.where(yy >= 48, jnp.where(xsd == ysd, 1, 0), jnp.where(xsd == ysd, 0, 1)))
    sel[...] = onehot((xnb == 4 * yg + yt) & ((x >> 4) == yfield) & (yg < 6) & (way == 1))
    x = iota((64, 48), 0)
    yy = iota((64, 48), 1)
    xnb = jnp.full((64, 48), -1, jnp.int32)
    for f in range(6):
        xnb = jnp.where((x & 7) == f, jnp.where(x < 32, nbs[f][0], nbs[f][2]), xnb)
    yt = jnp.where((yy & 15) < 8, 1, 3)
    selh[...] = onehot((xnb == 4 * (yy & 7) + yt) & (((x & 31) >> 3) == (yy >> 4)) & ((yy & 7) < 6))

    def chosen(s, code, offset):
        t = code & 3
        flipped = (s < 2) == (t < 2)
        along = jnp.where(flipped, 1 - offset, offset - 1)
        row_tap = jnp.where(t == 0, 0, jnp.where(t == 2, 2, 1 - along))
        col_tap = jnp.where(t == 1, 2, jnp.where(t == 3, 0, 1 - along))
        return 3 * row_tap + col_tap

    xs = iota((SIDES, C), 0)
    code = jnp.full((SIDES, C), 0, jnp.int32)
    for f in range(6):
        code = jnp.where(xs == f, nbs[f][1], code)
        code = jnp.where(xs == 8 + f, nbs[f][3], code)
    side_taps = [chosen(jnp.where(xs < 8, 1, 3), code, o) for o in range(3)]

    hub_side = jnp.where(is0, 0, 2)
    hub_nb = [jnp.where(is0, nbs[f][0], nbs[f][2]) for f in range(6)]
    hub_flip = [((hub_side < 2) == ((code_f & 3) < 2)).astype(jnp.int32) for code_f in hub_nb]

    def per_face(face, values, start):
        result = jnp.full(face.shape, start, jnp.int32)
        for f in range(6):
            result = jnp.where(face == f, values[f], result)
        return result

    @pl.when(ishub)
    def _():
        a = iota((8 * F, cells), 0)
        b = iota((8 * F, cells), 1)
        g = a & 7
        pos = a >> 3
        target = g * F + jnp.where(per_face(g, hub_flip, 0) == 1, F - 1 - pos, pos)
        amat[...] = onehot((b == target) & (g < 6))

    def edges(ph, i):
        row = rb[ph, i, 1].astype(F32)
        zero = jnp.zeros((2, C), F32)
        return jnp.concatenate([row[:, F - 1], zero, row[:, 0], zero], axis=0).astype(BF)

    def prepare(ph):
        for i in range(3):
            ebuf[ph, 16 * i : 16 * i + 16] = edges(ph, i)
        hm[ph] = dot(selh[...], ebuf[ph, 0:48]).astype(BF)

        @pl.when(ishub)
        def _():
            parts = []
            for i in range(3):
                parts.append(dot(amat[...], rb[ph, i, 1].reshape(cells, C)).reshape(F, 8, C))
            parts.append(jnp.zeros((F, 8, C), F32))
            zs[ph] = jnp.concatenate(parts, axis=1).astype(BF)

        @pl.when(is0)
        def _():
            rx[ph, 0] = hm[ph, 0:32]
            ebuf[ph, 96:128] = zs[ph, 0]

        @pl.when(is1)
        def _():
            rx[ph, n - 1] = hm[ph, 32:64]
            ebuf[ph, 128:160] = zs[ph, n - 1]

    def e_copy(ph):
        return rcopy(ebuf.at[ph, pl.ds(0, 48)], ebuf.at[ph, pl.ds(48, 48)], e_s.at[ph], e_r.at[ph], mirror)

    def hm_copy(ph, h):
        return rcopy(
            hm.at[ph, pl.ds(32 * h, 32)],
            rx.at[ph, r],
            hm_s.at[ph, h],
            rx_r.at[ph, r],
            (n - 1) * h,
        )

    def z_copy(ph, h, p):
        return rcopy(zs.at[ph, p], ebuf.at[ph, pl.ds(96 + 32 * h, 32)], z_s.at[ph, p], z_r.at[ph, h], p)

    def bulk_copy(ph, i, way):
        return rcopy(
            rb.at[ph, i, 1],
            rb.at[ph, i, 2 if way == 0 else 0],
            bulk_s.at[ph, i, way],
            bulk_r.at[ph, i, way],
            up if way == 0 else dn,
        )

    def mt_copy(ph, way):
        return rcopy(
            mt.at[ph, 1],
            mt.at[ph, 2 if way == 0 else 0],
            mt_s.at[ph, way],
            mt_r.at[ph, way],
            up if way == 0 else dn,
        )

    def hub_loop(step):
        def body(i, carry):
            step(lax.rem(r + i, n))
            return carry

        lax.fori_loop(1, n, body, 0)

    def send(ph):
        for h, here in ((0, is0), (1, is1)):

            @pl.when(here)
            def _():
                hub_loop(lambda p: z_copy(ph, h, p).start())

            @pl.when(jnp.logical_not(here))
            def _():
                hm_copy(ph, h).start()

        e_copy(ph).start()
        for i in range(3):
            for way in range(2):
                bulk_copy(ph, i, way).start()

    def margins(ph):
        e_copy(ph).wait()
        for h, here in ((0, is0), (1, is1)):

            @pl.when(jnp.logical_not(here))
            def _():
                z_copy(ph, h, 0).wait_recv()

        mt[ph, 1] = dot(sel[...], ebuf[ph]).astype(BF)
        for way in range(2):
            mt_copy(ph, way).start()

    def hub_row(ph, spreads):
        @pl.when(ishub)
        def _():
            hub_loop(lambda p: rcopy(hm.at[ph, pl.ds(0, 32)], rx.at[ph, p], hm_s.at[ph, 0], rx_r.at[ph, p], p).wait_recv())
            slot = jnp.where(is0, 0, 2)
            got = rx[ph].astype(F32)
            for i in range(3):
                piece = got[:, 8 * i : 8 * i + 8].reshape(8 * F, C).astype(BF)
                row = dot(bmat[...], piece)
                row = row + dot(c0mat[...], rb[ph, i, 1].reshape(cells, C))
                row = row + dot(c2mat[...], rb[ph, i, slot].reshape(cells, C))
                row = row.astype(BF).reshape(6, F, C)
                if i in spreads:
                    mb[ph, i] = row
                    rb[ph, i, slot] = jnp.zeros((6, F, C), BF)
                else:
                    rb[ph, i, slot] = row

        @pl.when(is0)
        def _():
            mt[ph, 0] = jnp.zeros((48, C), BF)

        @pl.when(is1)
        def _():
            mt[ph, 2] = jnp.zeros((48, C), BF)

    def receive(ph, spreads):
        for way in range(2):
            for i in range(3):
                bulk_copy(ph, i, way).wait()
            mt_copy(ph, way).wait()
        hub_row(ph, spreads)

    def finish_sends(ph):
        for h, here in ((0, is0), (1, is1)):

            @pl.when(here)
            def _():
                hub_loop(lambda p: z_copy(ph, h, p).wait_send())

            @pl.when(jnp.logical_not(here))
            def _():
                hm_copy(ph, h).wait_send()

    def forward_taps(ph, i, dst):
        for a in range(3):
            padf[:, 8 : 8 + F] = rb[ph, i, a].astype(F32)
            line = mt[ph, a, 16 * i : 16 * i + 16].astype(F32)
            for f in range(6):
                padf[f, 7:8] = line[8 + f : 9 + f]
                padf[f, 8 + F : 9 + F] = line[f : f + 1]
            for b in range(3):
                k = 3 * a + b
                dst[0:cells, k * C : k * C + C] = padf[:, 7 + b : 7 + b + F].reshape(cells, C).astype(BF)

    def spread_taps(ph, i, dst, extra, scale):
        for a in range(3):
            padz[:, 8 : 8 + F] = rb[ph, i, a].astype(F32) * scale
            for b in range(3):
                k = 8 - (3 * a + b)
                dst[0:cells, k * C : k * C + C] = padz[:, 7 + b : 7 + b + F].reshape(cells, C).astype(BF)
        lines = [mt[ph, o, 16 * i : 16 * i + 16].astype(F32) * scale for o in range(3)]
        for k in range(9):
            total = jnp.zeros((SIDES, C), F32)
            for o in range(3):
                total = jnp.where(side_taps[o] == k, lines[o], total)
            dst[cells : cells + SIDES, k * C : k * C + C] = total.astype(BF)

        @pl.when(ishub)
        def _():
            padz[:, 8 : 8 + F] = mb[ph, i].astype(F32) * scale
            for f in range(6):
                picks = [chosen(hub_side, hub_nb[f], o) for o in range(3)]
                shifted = [padz[f, 7 + o : 7 + o + F] for o in range(3)]
                for k in range(9):
                    total = jnp.zeros((F, C), F32)
                    for o in range(3):
                        total = jnp.where(picks[o] == k, shifted[o], total)
                    extra[f * F : f * F + F, k * C : k * C + C] = total.astype(BF)

    def spread(dst, extra, weights, width):
        result = dot(dst[...], weights)
        field[:, :, 0:width] = result[0:cells].reshape(6, F, width)
        for f in range(6):
            field[f, F - 1 : F, 0:width] += result[cells + f : cells + f + 1]
            field[f, 0:1, 0:width] += result[cells + 8 + f : cells + 9 + f]

        @pl.when(ishub)
        def _():
            field[:, :, 0:width] += dot(extra[...], weights).reshape(6, F, width)

        return field[:, :, 0:width].reshape(cells, width)

    for cp in loads:
        cp.wait()
    prepare(0)
    base = 2 + 1 + 1 + (ny - 1) + (nz - 1)
    pl.semaphore_wait(barrier, base + 2 + jnp.where(ishub, n - 2, 0))
    send(0)

    padz[...] = jnp.zeros(padz.shape, F32)
    for cp in wloads:
        cp.wait()
    wf1[:, 0:C] = wraw[0]
    wf1[:, C : 2 * C] = wraw[1]
    for k in range(9):
        rows = slice(k * C, k * C + C)
        ws1[rows, 0:C] = wraw[0, rows].astype(F32).T.astype(BF)
        ws1[rows, C : 2 * C] = wraw[1, rows].astype(F32).T.astype(BF)
        ws2[rows, 0:C] = wraw[2, rows].astype(F32).T.astype(BF)
        ws2[rows, C : 2 * C] = wraw[3, rows].astype(F32).T.astype(BF)

    @pl.when(ishub)
    def _():
        a = iota((cells, 8 * F), 0)
        b = iota((cells, 8 * F), 1)
        face = lax.div(a, F)
        pos = a - face * F
        pos = jnp.where(per_face(face, hub_flip, 0) == 1, F - 1 - pos, pos)
        column = per_face(face, [code_f & 1 for code_f in hub_nb], 0)
        bmat[...] = onehot((b == 8 * pos + face) & (column == 1))
        a = iota((cells, cells), 0)
        b = iota((cells, cells), 1)
        face = lax.div(a, F)
        pos = a - face * F
        code_a = per_face(face, hub_nb, 0)
        other = (code_a >> 2) * F
        c0mat[...] = onehot(((code_a & 3) == hub_side) & (b == other + F - 1 - pos))
        c2mat[...] = onehot(((code_a & 3) == 2 - hub_side) & (b == other + pos))

    margins(0)
    receive(0, (2,))

    forward_taps(0, 0, tu)
    forward_taps(0, 1, tv)
    spread_taps(0, 2, ts, tx, 0.5)
    joined = dot(tu[...], wf1[...])
    hidden = joined[:, 0:C]
    hidden_tangent = joined[:, C : 2 * C] + dot(tv[...], wraw[0])
    squash = jnp.tanh(hidden)
    derivative = 1.0 - squash * squash
    act = squash.astype(BF)
    act_tangent = (derivative * hidden_tangent).astype(BF)
    aext[0:cells, 0:C] = act
    aext[0:cells, C : 2 * C] = act_tangent
    sq[...] = squash.reshape(6, F, C)
    dd[0:cells, 0:C] = (-2.0 * squash * derivative * hidden_tangent)
    back = spread(ts, tx, ws2[...], 2 * C)
    squash = sq[...].reshape(cells, C)
    derivative = 1.0 - squash * squash
    delta = (derivative * back[:, 0:C]).astype(BF)
    delta_tangent = (derivative * back[:, C : 2 * C] + dd[...] * back[:, 0:C]).astype(BF)
    rb[1, 0, 1] = aext[0:cells, 0:C].reshape(6, F, C)
    rb[1, 1, 1] = delta.reshape(6, F, C)
    rb[1, 2, 1] = delta_tangent.reshape(6, F, C)
    prepare(1)
    send(1)

    pair = jnp.concatenate([delta, delta_tangent], axis=1)
    first = dot_t(tu[...], pair)
    gsum[0:K9] = first[:, 0:C]
    gsum[2 * K9 : 3 * K9] = first[:, C : 2 * C] + dot_t(tv[...], delta)
    zero = jnp.zeros((2, C), F32)
    tangent = aext[0:cells, C : 2 * C].astype(F32).reshape(6, F, C)
    aext[cells : cells + SIDES, 0:C] = ebuf[1, 0:16]
    aext[cells : cells + SIDES, C : 2 * C] = jnp.concatenate(
        [tangent[:, F - 1], zero, tangent[:, 0], zero], axis=0
    ).astype(BF)
    second = dot_t(aext[...], ts[...])
    for k in range(9):
        gsum[K9 + k * C : K9 + k * C + C] = second[0:C, k * C : k * C + C]
        gsum[3 * K9 + k * C : 3 * K9 + k * C + C] = second[C : 2 * C, k * C : k * C + C]

    @pl.when(ishub)
    def _():
        more = dot_t(aext[0:cells], tx[...])
        for k in range(9):
            gsum[K9 + k * C : K9 + k * C + C] += more[0:C, k * C : k * C + C]
            gsum[3 * K9 + k * C : 3 * K9 + k * C + C] += more[C : 2 * C, k * C : k * C + C]

    shard, p0, p1, qn = split_rows(ny, nz)
    qoff = p0 + p1 + qn * core
    qother = p0 + p1 + qn * (1 - core)
    slots = {}
    for name, count in PHASES:
        slots[name] = sum(ny if c == "y" else nz if c == "z" else 1 for _, c in PHASES[: len(slots)])

    def by_core(fn):
        @pl.when(core == 0)
        def _():
            fn(0, p0, p0, p1)

        @pl.when(core == 1)
        def _():
            fn(p0, p1, 0, p0)

    def ar(name, slot_s, slot_r, src, dst, p):
        return rcopy(src, dst, ar_s.at[slots[name] + slot_s], ar_r.at[slots[name] + slot_r], p)

    ypeers = [ypeer(d) for d in range(1, ny)]
    zpeers = [zpeer(d) for d in range(1, nz)]
    whole = gsum[...].reshape(ny, nz, shard, C)
    gs[...] = whole.astype(BF)

    def core_p(off, size, ooff, osize):
        return ar("cp", 0, 0, gs.at[:, :, pl.ds(ooff, osize)], gr.at[:, :, pl.ds(ooff, osize)], partner)

    def core_p_in(off, size, ooff, osize):
        return ar("cp", 0, 0, gs.at[:, :, pl.ds(off, size)], gr.at[:, :, pl.ds(off, size)], partner)

    def core_q(o):
        return ar("cq", 0, 0, gs.at[:, :, pl.ds(o, qn)], gr.at[:, :, pl.ds(o, qn)], partner)

    core_q(qother).start()
    by_core(lambda *a: core_p(*a).start())

    def q1(d, out):
        q, p = zpeers[d]
        return ar("q1", q, z if out else q, qs.at[:, q], qr.at[z if out else q], p)

    def p1_copy(d, size, out):
        q, p = ypeers[d]
        return ar("p1", q, y if out else q, ps.at[q, :, pl.ds(0, size)], pr.at[y if out else q, :, pl.ds(0, size)], p)

    core_q(qother).wait_send()
    core_q(qoff).wait_recv()

    def stage(qo):
        part = gsum[...].reshape(ny, nz, shard, C)[:, :, qo : qo + qn] + gr[:, :, qo : qo + qn].astype(F32)
        qf[...] = part
        qs[...] = part.astype(BF)

    by_core(lambda off, size, ooff, osize: stage(p0 + p1 if off == 0 else p0 + p1 + qn))
    for d in range(nz - 1):
        q1(d, True).start()

    def stage(off, size, ooff, osize):
        core_p(off, size, ooff, osize).wait_send()
        core_p_in(off, size, ooff, osize).wait_recv()
        part = gsum[...].reshape(ny, nz, shard, C)[:, :, off : off + size] + gr[:, :, off : off + size].astype(F32)
        pf[:, :, 0:size] = part
        ps[:, :, 0:size] = part.astype(BF)
        for d in range(ny - 1):
            p1_copy(d, size, True).start()

    by_core(stage)
    margins(1)

    def p2_copy(d, size, out):
        q, p = zpeers[d]
        return ar("p2", q, z if out else q, pz.at[q, pl.ds(0, size)], pzr.at[z if out else q, pl.ds(0, size)], p)

    def stage(off, size, ooff, osize):
        for d in range(ny - 1):
            p1_copy(d, size, True).wait_send()
            p1_copy(d, size, False).wait_recv()
        part = pf[y, :, 0:size]
        for q, p in ypeers:
            part = part + pr[q, :, 0:size].astype(F32)
        pzf[:, 0:size] = part
        pz[:, 0:size] = part.astype(BF)
        for d in range(nz - 1):
            p2_copy(d, size, True).start()

    by_core(stage)

    def q2(d, out):
        q, p = ypeers[d]
        return ar("q2", q, y if out else q, qy.at[q], qyr.at[y if out else q], p)

    for d in range(nz - 1):
        q1(d, True).wait_send()
        q1(d, False).wait_recv()
    part = qf[:, z]
    for q, p in zpeers:
        part = part + qr[q].astype(F32)
    qyf[...] = part
    qy[...] = part.astype(BF)
    for d in range(ny - 1):
        q2(d, True).start()

    receive(1, (1, 2))
    forward_taps(1, 0, tu)
    change = dot(tu[...], wraw[2])
    next_ref[...] = (rb[0, 0, 1].astype(F32).reshape(cells, C) + 0.5 * change).astype(BF).reshape(6, F, C)

    scale = 1.0 / F

    def p3(d, size, off, out):
        q, p = zpeers[d]
        zz = z if out else q
        ref = out_ref.at[y, zz, pl.ds(off, size)]
        return ar("p3", q, zz, ref, ref, p)

    def stage(off, size, ooff, osize):
        for d in range(nz - 1):
            p2_copy(d, size, True).wait_send()
            p2_copy(d, size, False).wait_recv()
        part = pzf[z, 0:size]
        for q, p in zpeers:
            part = part + pzr[q, 0:size].astype(F32)
        out_ref[y, z, off : off + size] = (part * scale).astype(BF)
        for d in range(nz - 1):
            p3(d, size, off, True).start()

    by_core(stage)

    def q3(d, out):
        q, p = ypeers[d]
        qq = y if out else q
        ref = out_ref.at[qq, z, pl.ds(qoff, qn)]
        return ar("q3", q, qq, ref, ref, p)

    for d in range(ny - 1):
        q2(d, True).wait_send()
        q2(d, False).wait_recv()
    part = qyf[y]
    for q, p in ypeers:
        part = part + qyr[q].astype(F32)
    out_ref[y, z, pl.ds(pl.multiple_of(qoff, 16), qn)] = (part * scale).astype(BF)
    for d in range(ny - 1):
        q3(d, True).start()

    spread_taps(1, 1, ts, tx, 1.0)
    back = spread(ts, tx, ws1[...], 2 * C)
    adj_ref[...] = (rb[0, 2, 1].astype(F32).reshape(cells, C) + back[:, 0:C]).astype(BF).reshape(6, F, C)
    dd[...] = back[:, C : 2 * C]

    def p4(d, size, off, out):
        q, p = ypeers[d]
        qq = y if out else q
        ref = out_ref.at[qq, :, pl.ds(off, size)]
        return ar("p4", q, qq, ref, ref, p)

    def cpy_p(q, size, off):
        ref = out_ref.at[q, :, pl.ds(off, size)]
        return ar("c4", q, q, ref, ref, partner)

    def stage(off, size, ooff, osize):
        for d in range(nz - 1):
            p3(d, size, off, True).wait_send()
            p3(d, size, off, False).wait_recv()
        for d in range(ny - 1):
            p4(d, size, off, True).start()
        cpy_p(y, size, off).start()

    by_core(stage)

    def q4(d, out):
        q, p = zpeers[d]
        qq = z if out else q
        ref = out_ref.at[:, qq, pl.ds(qoff, qn)]
        return ar("q4", q, qq, ref, ref, p)

    def cpy_q(q, o):
        ref = out_ref.at[:, q, pl.ds(o, qn)]
        return ar("d4", q, q, ref, ref, partner)

    for d in range(ny - 1):
        q3(d, True).wait_send()
        q3(d, False).wait_recv()
    for d in range(nz - 1):
        q4(d, True).start()
    cpy_q(z, qoff).start()

    spread_taps(1, 2, ty, tx, 1.0)
    back = spread(ty, tx, ws1[:, 0:C], C)
    adt_ref[...] = (dd[...] + back).astype(BF).reshape(6, F, C)

    def stage(off, size, ooff, osize):
        for d in range(ny - 1):
            p4(d, size, off, False).wait_recv()
            cpy_p(ypeers[d][0], size, off).start()

    by_core(stage)
    for d in range(nz - 1):
        q4(d, False).wait_recv()
        cpy_q(zpeers[d][0], qoff).start()

    def stage(off, size, ooff, osize):
        for d in range(ny - 1):
            p4(d, size, off, True).wait_send()
        for q in range(ny):
            cpy_p(q, size, off).wait_send()
            cpy_p(q, osize, ooff).wait_recv()

    by_core(stage)
    for d in range(nz - 1):
        q4(d, True).wait_send()
    for q in range(nz):
        cpy_q(q, qoff).wait_send()
        cpy_q(q, qother).wait_recv()
    finish_sends(0)
    finish_sends(1)


PHASES = (
    ("cp", "1"),
    ("cq", "1"),
    ("q1", "z"),
    ("p1", "y"),
    ("p2", "z"),
    ("q2", "y"),
    ("p3", "z"),
    ("q3", "y"),
    ("p4", "y"),
    ("c4", "y"),
    ("q4", "z"),
    ("d4", "z"),
)


def split_rows(ny, nz):
    tiles = 4 * K9 // (16 * ny * nz)
    qn = 2 * tiles // 9
    p1 = (tiles - 2 * qn) // 2
    return 16 * tiles, 16 * (tiles - 2 * qn - p1), 16 * p1, 16 * qn


def on_device(n, ny, nz, u, v, c, w1, w2, t1, t2, nb):
    F = n
    cells = 6 * F
    shard, p0, p1, qn = split_rows(ny, nz)
    arrived = sum(ny if c == "y" else nz if c == "z" else 1 for _, c in PHASES)
    u, v, c = (a.reshape(6, F, C) for a in (u, v, c))
    w1, w2, t1, t2 = (a.reshape(K9, C) for a in (w1, w2, t1, t2))
    vm = pltpu.VMEM
    dma = pltpu.SemaphoreType.DMA
    anywhere = pl.BlockSpec(memory_space=pl.ANY)
    inside = pl.BlockSpec(memory_space=pltpu.VMEM)
    row = jax.ShapeDtypeStruct((6, F, C), BF)
    nxt, adj, adt, out = pl.pallas_call(
        functools.partial(kernel, n, ny, nz),
        out_shape=(row, row, row, jax.ShapeDtypeStruct((ny, nz, shard, C), BF)),
        in_specs=[anywhere] * 8,
        out_specs=(inside,) * 4,
        scratch_shapes=[
            vm((2, 3, 3, 6, F, C), BF),
            vm((2, 3, 6, F, C), BF),
            vm((2, 160, C), BF),
            vm((2, 64, C), BF),
            vm((2, F, 32, C), BF),
            vm((2, F, 32, C), BF),
            vm((2, 3, 48, C), BF),
            vm((48, 160), BF),
            vm((64, 48), BF),
            vm((8 * F, cells), BF),
            vm((cells, 8 * F), BF),
            vm((cells, cells), BF),
            vm((cells, cells), BF),
            vm((4, K9, C), BF),
            vm((K9, 2 * C), BF),
            vm((K9, 2 * C), BF),
            vm((K9, 2 * C), BF),
            vm((6, F + 16, C), F32),
            vm((6, F + 16, C), F32),
            vm((cells, K9), BF),
            vm((cells, K9), BF),
            vm((cells + SIDES, K9), BF),
            vm((cells, K9), BF),
            vm((cells + SIDES, K9), BF),
            vm((6, F, C), F32),
            vm((cells + SIDES, 2 * C), BF),
            vm((cells, C), F32),
            vm((6, F, 2 * C), F32),
            vm((4 * K9, C), F32),
            vm((ny, nz, shard, C), BF),
            vm((ny, nz, shard, C), BF),
            vm((ny, nz, p0, C), F32),
            vm((ny, nz, p0, C), BF),
            vm((ny, nz, p0, C), BF),
            vm((ny, nz, qn, C), F32),
            vm((ny, nz, qn, C), BF),
            vm((nz, ny, qn, C), BF),
            vm((nz, p0, C), BF),
            vm((nz, p0, C), F32),
            vm((nz, p0, C), BF),
            vm((ny, qn, C), BF),
            vm((ny, qn, C), F32),
            vm((ny, qn, C), BF),
            pltpu.SMEM((6, 4), jnp.int32),
            dma((8,)),
            dma((2, 3, 2)),
            dma((2, 3, 2)),
            dma((2,)),
            dma((2,)),
            dma((2, 2)),
            dma((2, n)),
            dma((2, n)),
            dma((2, 2)),
            dma((2, 2)),
            dma((2, 2)),
            dma((arrived,)),
            dma((arrived,)),
        ],
        compiler_params=pltpu.CompilerParams(
            collective_id=0, has_side_effects=True, vmem_limit_bytes=56 * 2**20
        ),
    )(u, v, c, w1, w2, t1, t2, nb)
    grads = out.reshape(2, 2, 9, C, C).astype(F32)
    shape = (6, 1, F, C)
    return nxt.reshape(shape), adj.reshape(shape), adt.reshape(shape), grads[0], grads[1]


def solution(mesh):
    n = mesh.shape["tile"] * mesh.shape["sub"]
    nz = 8 if n == 64 else 2
    ny = n // (2 * nz)
    field = P("rep", ("tile", "sub"), None, None)
    grads = P("rep", None, None, None)
    return jax.shard_map(
        functools.partial(on_device, n, ny, nz),
        mesh=mesh,
        in_specs=(field, field, field, P(), P(), P(), P(), P()),
        out_specs=(field, field, field, grads, grads),
        check_vma=False,
    )
```

```python
import functools

import jax
import jax.numpy as jnp
from jax import lax
from jax.experimental import pallas as pl
from jax.experimental.pallas import tpu as pltpu
from jax.sharding import PartitionSpec as P

MESH = pl.DeviceIdType.MESH
BF = jnp.bfloat16
F32 = jnp.float32
C = 128
K9 = 9 * C
SIDES = 16


def dot(a, b):
    return jnp.dot(a, b, preferred_element_type=F32)


def dot_t(a, b):
    return lax.dot_general(a, b, (((0,), (0,)), ((), ())), preferred_element_type=F32)


def iota(shape, dim):
    return lax.broadcasted_iota(jnp.int32, shape, dim)


def onehot(mask):
    return jnp.where(mask, 1.0, 0.0).astype(BF)


def kernel(
    n,
    ny,
    nz,
    u_ref,
    v_ref,
    c_ref,
    w1_ref,
    w2_ref,
    t1_ref,
    t2_ref,
    nb_ref,
    next_ref,
    adj_ref,
    adt_ref,
    out_ref,
    rb,
    mb,
    ebuf,
    hm,
    zs,
    rx,
    mt,
    sel,
    selh,
    amat,
    bmat,
    c0mat,
    c2mat,
    wraw,
    wf1,
    ws1,
    ws2,
    padz,
    tu,
    tv,
    ts,
    tx,
    aext,
    pext,
    front,
    field,
    gsum,
    gs,
    gr,
    pf,
    ps,
    pr,
    qf,
    qs,
    qr,
    pz,
    pzf,
    pzr,
    qy,
    qyf,
    qyr,
    nbm,
    res,
    fin_p,
    fin_q,
    osem,
    lsem,
    bulk_s,
    bulk_r,
    e_s,
    e_r,
    hm_s,
    rx_r,
    z_s,
    z_r,
    mt_s,
    mt_r,
    ar_s,
    ar_r,
):
    F = n
    cells = 6 * F
    rep = lax.axis_index("rep")
    r = lax.axis_index("tile") * 2 + lax.axis_index("sub")
    core = lax.rem(lax.div(r, 2), 2)
    z = lax.rem(lax.div(r, 4), nz)
    yhi = lax.div(r, 4 * nz)
    ylo = lax.rem(r, 2)
    y = yhi * 2 + ylo

    def dev(p):
        return (lax.div(p, 2), lax.rem(p, 2), rep)

    def make(hi, zc, co, lo):
        return ((hi * nz + zc) * 2 + co) * 2 + lo

    up = lax.rem(r + n - 1, n)
    dn = lax.rem(r + 1, n)
    mirror = n - 1 - r
    partner = make(yhi, z, 1 - core, ylo)

    def ypeer(d):
        q = lax.rem(y + d, ny)
        return q, make(lax.div(q, 2), z, core, lax.rem(q, 2))

    def zpeer(d):
        q = lax.rem(z + d, nz)
        return q, make(yhi, q, core, ylo)

    is0 = r == 0
    is1 = r == n - 1
    ishub = jnp.logical_or(is0, is1)

    def rcopy(src, dst, ssem, rsem, p):
        return pltpu.make_async_remote_copy(
            src_ref=src,
            dst_ref=dst,
            send_sem=ssem,
            recv_sem=rsem,
            device_id=dev(p),
            device_id_type=MESH,
        )

    nbload = pltpu.make_async_copy(nb_ref, nbm, lsem.at[7])
    nbload.start()
    loads = [pltpu.make_async_copy(ref, rb.at[0, i, 1], lsem.at[i]) for i, ref in enumerate((u_ref, v_ref, c_ref))]
    wloads = [pltpu.make_async_copy(ref, wraw.at[i], lsem.at[3 + i]) for i, ref in enumerate((w1_ref, t1_ref, w2_ref, t2_ref))]
    for cp in loads + wloads:
        cp.start()

    barrier = pltpu.get_barrier_semaphore()

    def greet(p):
        pl.semaphore_signal(barrier, inc=1, device_id=dev(p), device_id_type=MESH)

    @pl.when(ishub)
    def _():
        def body(i, carry):
            greet(lax.rem(r + i, n))
            return carry

        lax.fori_loop(1, n, body, 0)

    @pl.when(r != 0)
    def _():
        greet(0)

    @pl.when(r != n - 1)
    def _():
        greet(n - 1)

    for p in (up, dn, mirror, partner):
        greet(p)
    for d in range(1, ny):
        greet(ypeer(d)[1])
    for d in range(1, nz):
        greet(zpeer(d)[1])

    nbload.wait()
    nbs = [[nbm[s, f] for s in range(4)] for f in range(6)]
    x = iota((48, 160), 0)
    yy = iota((48, 160), 1)
    xs = x & 15
    xsd = jnp.where(xs < 8, 1, 3)
    xnb = jnp.full((48, 160), -1, jnp.int32)
    for f in range(6):
        xnb = jnp.where(xs == f, nbs[f][1], xnb)
        xnb = jnp.where(xs == 8 + f, nbs[f][3], xnb)
    ym = jnp.where(yy >= 48, yy - 48, yy)
    ysd = jnp.where((ym & 15) < 8, 1, 3)
    yz = (yy - 96) & 31
    isz = yy >= 96
    yg = jnp.where(isz, yz & 7, ym & 7)
    yt = jnp.where(isz, jnp.where(yy >= 128, 2, 0), ysd)
    yfield = jnp.where(isz, yz >> 3, ym >> 4)
    way = jnp.where(isz, 1, jnp.where(yy >= 48, jnp.where(xsd == ysd, 1, 0), jnp.where(xsd == ysd, 0, 1)))
    sel[...] = onehot((xnb == 4 * yg + yt) & ((x >> 4) == yfield) & (yg < 6) & (way == 1))
    x = iota((64, 48), 0)
    yy = iota((64, 48), 1)
    xnb = jnp.full((64, 48), -1, jnp.int32)
    for f in range(6):
        xnb = jnp.where((x & 7) == f, jnp.where(x < 32, nbs[f][0], nbs[f][2]), xnb)
    yt = jnp.where((yy & 15) < 8, 1, 3)
    selh[...] = onehot((xnb == 4 * (yy & 7) + yt) & (((x & 31) >> 3) == (yy >> 4)) & ((yy & 7) < 6))

    def chosen(s, code, offset):
        t = code & 3
        flipped = (s < 2) == (t < 2)
        along = jnp.where(flipped, 1 - offset, offset - 1)
        row_tap = jnp.where(t == 0, 0, jnp.where(t == 2, 2, 1 - along))
        col_tap = jnp.where(t == 1, 2, jnp.where(t == 3, 0, 1 - along))
        return 3 * row_tap + col_tap

    xs = iota((SIDES, C), 0)
    code = jnp.full((SIDES, C), 0, jnp.int32)
    for f in range(6):
        code = jnp.where(xs == f, nbs[f][1], code)
        code = jnp.where(xs == 8 + f, nbs[f][3], code)
    side_taps = [chosen(jnp.where(xs < 8, 1, 3), code, o) for o in range(3)]

    hub_side = jnp.where(is0, 0, 2)
    hub_nb = [jnp.where(is0, nbs[f][0], nbs[f][2]) for f in range(6)]
    hub_flip = [((hub_side < 2) == ((code_f & 3) < 2)).astype(jnp.int32) for code_f in hub_nb]

    def per_face(face, values, start):
        result = jnp.full(face.shape, start, jnp.int32)
        for f in range(6):
            result = jnp.where(face == f, values[f], result)
        return result

    @pl.when(ishub)
    def _():
        a = iota((8 * F, cells), 0)
        b = iota((8 * F, cells), 1)
        g = a & 7
        pos = a >> 3
        target = g * F + jnp.where(per_face(g, hub_flip, 0) == 1, F - 1 - pos, pos)
        amat[...] = onehot((b == target) & (g < 6))

    def edges(ph, i):
        row = rb[ph, i, 1].astype(F32)
        zero = jnp.zeros((2, C), F32)
        return jnp.concatenate([row[:, F - 1], zero, row[:, 0], zero], axis=0).astype(BF)

    def prepare(ph):
        for i in range(3):
            ebuf[ph, 16 * i : 16 * i + 16] = edges(ph, i)
        hm[ph] = dot(selh[...], ebuf[ph, 0:48]).astype(BF)

        @pl.when(ishub)
        def _():
            parts = []
            for i in range(3):
                parts.append(dot(amat[...], rb[ph, i, 1].reshape(cells, C)).reshape(F, 8, C))
            parts.append(jnp.zeros((F, 8, C), F32))
            zs[ph] = jnp.concatenate(parts, axis=1).astype(BF)

        @pl.when(is0)
        def _():
            rx[ph, 0] = hm[ph, 0:32]
            ebuf[ph, 96:128] = zs[ph, 0]

        @pl.when(is1)
        def _():
            rx[ph, n - 1] = hm[ph, 32:64]
            ebuf[ph, 128:160] = zs[ph, n - 1]

    def e_copy(ph):
        return rcopy(ebuf.at[ph, pl.ds(0, 48)], ebuf.at[ph, pl.ds(48, 48)], e_s.at[ph], e_r.at[ph], mirror)

    def hm_copy(ph, h):
        return rcopy(
            hm.at[ph, pl.ds(32 * h, 32)],
            rx.at[ph, r],
            hm_s.at[ph, h],
            rx_r.at[ph, r],
            (n - 1) * h,
        )

    def z_copy(ph, h, p):
        return rcopy(zs.at[ph, p], ebuf.at[ph, pl.ds(96 + 32 * h, 32)], z_s.at[ph, p], z_r.at[ph, h], p)

    def bulk_copy(ph, i, way):
        return rcopy(
            rb.at[ph, i, 1],
            rb.at[ph, i, 2 if way == 0 else 0],
            bulk_s.at[ph, i, way],
            bulk_r.at[ph, i, way],
            up if way == 0 else dn,
        )

    def send_rows(ph):
        for i in range(3):
            for way in range(2):
                bulk_copy(ph, i, way).start()

    def mt_copy(ph, way):
        return rcopy(
            mt.at[ph, 1],
            mt.at[ph, 2 if way == 0 else 0],
            mt_s.at[ph, way],
            mt_r.at[ph, way],
            up if way == 0 else dn,
        )

    def hub_loop(step):
        def body(i, carry):
            step(lax.rem(r + i, n))
            return carry

        lax.fori_loop(1, n, body, 0)

    def send(ph):
        for h, here in ((0, is0), (1, is1)):

            @pl.when(here)
            def _():
                hub_loop(lambda p: z_copy(ph, h, p).start())

            @pl.when(jnp.logical_not(here))
            def _():
                hm_copy(ph, h).start()

        e_copy(ph).start()

    def margins(ph):
        e_copy(ph).wait()
        for h, here in ((0, is0), (1, is1)):

            @pl.when(jnp.logical_not(here))
            def _():
                z_copy(ph, h, 0).wait_recv()

        mt[ph, 1] = dot(sel[...], ebuf[ph]).astype(BF)
        for way in range(2):
            mt_copy(ph, way).start()

    def hub_row(ph, spreads):
        @pl.when(ishub)
        def _():
            hub_loop(lambda p: rcopy(hm.at[ph, pl.ds(0, 32)], rx.at[ph, p], hm_s.at[ph, 0], rx_r.at[ph, p], p).wait_recv())
            slot = jnp.where(is0, 0, 2)
            got = rx[ph].astype(F32)
            for i in range(3):
                piece = got[:, 8 * i : 8 * i + 8].reshape(8 * F, C).astype(BF)
                row = dot(bmat[...], piece)
                row = row + dot(c0mat[...], rb[ph, i, 1].reshape(cells, C))
                row = row + dot(c2mat[...], rb[ph, i, slot].reshape(cells, C))
                row = row.astype(BF).reshape(6, F, C)
                if i in spreads:
                    mb[ph, i] = row
                    rb[ph, i, slot] = jnp.zeros((6, F, C), BF)
                else:
                    rb[ph, i, slot] = row

    def receive(ph, spreads):
        for i in range(3):
            for way in range(2):
                bulk_copy(ph, i, way).wait()
        hub_row(ph, spreads)

    def receive_margins(ph):
        for way in range(2):
            mt_copy(ph, way).wait()

        @pl.when(is0)
        def _():
            mt[ph, 0] = jnp.zeros((48, C), BF)

        @pl.when(is1)
        def _():
            mt[ph, 2] = jnp.zeros((48, C), BF)

    def finish_sends(ph):
        for h, here in ((0, is0), (1, is1)):

            @pl.when(here)
            def _():
                hub_loop(lambda p: z_copy(ph, h, p).wait_send())

            @pl.when(jnp.logical_not(here))
            def _():
                hm_copy(ph, h).wait_send()

    def row_taps(ph, i, a, dst, spreads, scale):
        padz[:, 8 : 8 + F] = rb[ph, i, a].astype(F32) * scale
        for b in range(3):
            k = 3 * a + b
            k = 8 - k if spreads else k
            dst[0:cells, k * C : k * C + C] = padz[:, 7 + b : 7 + b + F].reshape(cells, C).astype(BF)

    def forward_sides(ph, i, dst):
        for a in range(3):
            line = mt[ph, a, 16 * i : 16 * i + 16].astype(F32)
            zero = jnp.zeros((SIDES, C), F32)
            for b, part in enumerate((jnp.where(xs < 8, zero, line), zero, jnp.where(xs < 8, line, zero))):
                k = 3 * a + b
                dst[cells : cells + SIDES, k * C : k * C + C] = part.astype(BF)

    def spread_sides(ph, i, dst, scale):
        lines = [mt[ph, o, 16 * i : 16 * i + 16].astype(F32) * scale for o in range(3)]
        for k in range(9):
            total = jnp.zeros((SIDES, C), F32)
            for o in range(3):
                total = jnp.where(side_taps[o] == k, lines[o], total)
            dst[cells : cells + SIDES, k * C : k * C + C] = total.astype(BF)

    def hub_taps(ph, i, extra, scale):
        padz[:, 8 : 8 + F] = mb[ph, i].astype(F32) * scale
        for f in range(6):
            picks = [chosen(hub_side, hub_nb[f], o) for o in range(3)]
            shifted = [padz[f, 7 + o : 7 + o + F] for o in range(3)]
            for k in range(9):
                total = jnp.zeros((F, C), F32)
                for o in range(3):
                    total = jnp.where(picks[o] == k, shifted[o], total)
                extra[f * F : f * F + F, k * C : k * C + C] = total.astype(BF)

    def add_sides(ref, lanes, side):
        for f in range(6):
            ref[f, F - 1 : F, lanes] += side[f : f + 1]
            ref[f, 0:1, lanes] += side[8 + f : 9 + f]

    def main_spread(ph, i, dst, extra, weights, scale, ref, lanes):
        width = lanes.stop - lanes.start
        ref[:, :, lanes] = dot(dst[0:cells], weights).reshape(6, F, width)

        @pl.when(ishub)
        def _():
            hub_taps(ph, i, extra, scale)
            ref[:, :, lanes] += dot(extra[...], weights).reshape(6, F, width)

    for cp in loads:
        cp.wait()
    prepare(0)
    base = 4 + (ny - 1) + (nz - 1)
    pl.semaphore_wait(barrier, base + 2 + jnp.where(ishub, n - 2, 0))
    send(0)
    send_rows(0)

    padz[...] = jnp.zeros(padz.shape, F32)
    for cp in wloads:
        cp.wait()
    wf1[:, 0:C] = wraw[0]
    wf1[:, C : 2 * C] = wraw[1]
    for k in range(9):
        rows = slice(k * C, k * C + C)
        ws1[rows, 0:C] = wraw[0, rows].astype(F32).T.astype(BF)
        ws1[rows, C : 2 * C] = wraw[1, rows].astype(F32).T.astype(BF)
        ws2[rows, 0:C] = wraw[2, rows].astype(F32).T.astype(BF)
        ws2[rows, C : 2 * C] = wraw[3, rows].astype(F32).T.astype(BF)

    @pl.when(ishub)
    def _():
        a = iota((cells, 8 * F), 0)
        b = iota((cells, 8 * F), 1)
        face = lax.div(a, F)
        pos = a - face * F
        pos = jnp.where(per_face(face, hub_flip, 0) == 1, F - 1 - pos, pos)
        column = per_face(face, [code_f & 1 for code_f in hub_nb], 0)
        bmat[...] = onehot((b == 8 * pos + face) & (column == 1))
        a = iota((cells, cells), 0)
        b = iota((cells, cells), 1)
        face = lax.div(a, F)
        pos = a - face * F
        code_a = per_face(face, hub_nb, 0)
        other = (code_a >> 2) * F
        c0mat[...] = onehot(((code_a & 3) == hub_side) & (b == other + F - 1 - pos))
        c2mat[...] = onehot(((code_a & 3) == 2 - hub_side) & (b == other + pos))

    inputs = ((0, tu, False, 1.0), (1, tv, False, 1.0), (2, ts, True, 0.5))
    for i, dst, spreads, scale in inputs:
        row_taps(0, i, 1, dst, spreads, scale)
    margins(0)
    receive(0, (2,))

    for i, dst, spreads, scale in inputs:
        row_taps(0, i, 0, dst, spreads, scale)
        row_taps(0, i, 2, dst, spreads, scale)
    both = slice(0, 2 * C)
    left = slice(0, C)
    right = slice(C, 2 * C)
    front[...] = dot(tu[0:cells], wf1[...]).reshape(6, F, 2 * C)
    front[:, :, right] += dot(tv[0:cells], wraw[0]).reshape(6, F, C)
    main_spread(0, 2, ts, tx, ws2[...], 0.5, field, both)
    receive_margins(0)
    forward_sides(0, 0, tu)
    forward_sides(0, 1, tv)
    spread_sides(0, 2, ts, 0.5)
    side = dot(tu[cells:], wf1[...])
    more = dot(tv[cells:], wraw[0])
    add_sides(front, both, side)
    add_sides(front, right, more)
    add_sides(field, both, dot(ts[cells:], ws2[...]))
    squash = jnp.tanh(front[:, :, left])
    derivative = 1.0 - squash * squash
    hidden_tangent = front[:, :, right]
    act_tangent = (derivative * hidden_tangent).astype(BF)
    backward = field[:, :, left]
    scaled = derivative * backward
    rb[1, 0, 1] = squash.astype(BF)
    rb[1, 1, 1] = scaled.astype(BF)
    rb[1, 2, 1] = (derivative * field[:, :, right] - 2.0 * squash * scaled * hidden_tangent).astype(BF)
    aext[0:cells, right] = act_tangent.reshape(cells, C)

    aext[0:cells, left] = rb[1, 0, 1].reshape(cells, C)
    aext[cells:, left] = edges(1, 0)
    zero = jnp.zeros((2, C), F32)
    wide = act_tangent.astype(F32)
    aext[cells:, right] = jnp.concatenate([wide[:, F - 1], zero, wide[:, 0], zero], axis=0).astype(BF)
    for i, lanes in ((1, left), (2, right)):
        pext[0:cells, lanes] = rb[1, i, 1].reshape(cells, C)
        pext[cells:, lanes] = edges(1, i)
    first = dot_t(tu[...], pext[...])
    gsum[0:K9] = first[:, 0:C]
    gsum[2 * K9 : 3 * K9] = first[:, C : 2 * C] + dot_t(tv[...], pext[:, left])
    second = dot_t(aext[...], ts[...])
    for k in range(9):
        gsum[K9 + k * C : K9 + k * C + C] = second[0:C, k * C : k * C + C]
        gsum[3 * K9 + k * C : 3 * K9 + k * C + C] = second[C : 2 * C, k * C : k * C + C]

    @pl.when(ishub)
    def _():
        more = dot_t(aext[0:cells], tx[...])
        for k in range(9):
            gsum[K9 + k * C : K9 + k * C + C] += more[0:C, k * C : k * C + C]
            gsum[3 * K9 + k * C : 3 * K9 + k * C + C] += more[C : 2 * C, k * C : k * C + C]

    outs = [pltpu.make_async_copy(res.at[i], ref, osem.at[i]) for i, ref in enumerate((next_ref, adj_ref, adt_ref))]

    shard, p0, p1, qn = split_rows(ny, nz)
    qoff = p0 + p1 + qn * core
    qother = p0 + p1 + qn * (1 - core)
    slots = {}
    for name, count in PHASES:
        slots[name] = sum(ny if c == "y" else nz if c == "z" else 1 for _, c in PHASES[: len(slots)])

    def by_core(fn):
        @pl.when(core == 0)
        def _():
            fn(0, p0, p0, p1)

        @pl.when(core == 1)
        def _():
            fn(p0, p1, 0, p0)

    def ar(name, slot_s, slot_r, src, dst, p):
        return rcopy(src, dst, ar_s.at[slots[name] + slot_s], ar_r.at[slots[name] + slot_r], p)

    ypeers = [ypeer(d) for d in range(1, ny)]
    zpeers = [zpeer(d) for d in range(1, nz)]
    whole = gsum[...].reshape(ny, nz, shard, C)
    gs[...] = whole.astype(BF)

    def core_p(off, size, ooff, osize):
        return ar("cp", 0, 0, gs.at[:, :, pl.ds(ooff, osize)], gr.at[:, :, pl.ds(ooff, osize)], partner)

    def core_p_in(off, size, ooff, osize):
        return ar("cp", 0, 0, gs.at[:, :, pl.ds(off, size)], gr.at[:, :, pl.ds(off, size)], partner)

    def core_q(o):
        return ar("cq", 0, 0, gs.at[:, :, pl.ds(o, qn)], gr.at[:, :, pl.ds(o, qn)], partner)

    core_q(qother).start()
    by_core(lambda *a: core_p(*a).start())

    def q1(d, out):
        q, p = zpeers[d]
        return ar("q1", q, z if out else q, qs.at[:, q], qr.at[z if out else q], p)

    def p1_copy(d, size, out):
        q, p = ypeers[d]
        return ar("p1", q, y if out else q, ps.at[q, :, pl.ds(0, size)], pr.at[y if out else q, :, pl.ds(0, size)], p)

    core_q(qother).wait_send()
    core_q(qoff).wait_recv()

    def stage(qo):
        part = gsum[...].reshape(ny, nz, shard, C)[:, :, qo : qo + qn] + gr[:, :, qo : qo + qn].astype(F32)
        qf[...] = part
        qs[...] = part.astype(BF)

    by_core(lambda off, size, ooff, osize: stage(p0 + p1 if off == 0 else p0 + p1 + qn))
    for d in range(nz - 1):
        q1(d, True).start()

    def stage(off, size, ooff, osize):
        core_p(off, size, ooff, osize).wait_send()
        core_p_in(off, size, ooff, osize).wait_recv()
        part = gsum[...].reshape(ny, nz, shard, C)[:, :, off : off + size] + gr[:, :, off : off + size].astype(F32)
        pf[:, :, 0:size] = part
        ps[:, :, 0:size] = part.astype(BF)
        for d in range(ny - 1):
            p1_copy(d, size, True).start()

    by_core(stage)
    prepare(1)
    send(1)
    send_rows(1)

    def p2_copy(d, size, out):
        q, p = zpeers[d]
        return ar("p2", q, z if out else q, pz.at[q, pl.ds(0, size)], pzr.at[z if out else q, pl.ds(0, size)], p)

    def stage(off, size, ooff, osize):
        for d in range(ny - 1):
            p1_copy(d, size, True).wait_send()
            p1_copy(d, size, False).wait_recv()
        part = pf[y, :, 0:size]
        for q, p in ypeers:
            part = part + pr[q, :, 0:size].astype(F32)
        pzf[:, 0:size] = part
        pz[:, 0:size] = part.astype(BF)
        for d in range(nz - 1):
            p2_copy(d, size, True).start()

    by_core(stage)

    def q2(d, out):
        q, p = ypeers[d]
        return ar("q2", q, y if out else q, qy.at[q], qyr.at[y if out else q], p)

    for d in range(nz - 1):
        q1(d, True).wait_send()
        q1(d, False).wait_recv()
    part = qf[:, z]
    for q, p in zpeers:
        part = part + qr[q].astype(F32)
    qyf[...] = part
    qy[...] = part.astype(BF)
    for d in range(ny - 1):
        q2(d, True).start()

    scale = 1.0 / F

    def p3(d, size, off, out):
        q, p = zpeers[d]
        zz = z if out else q
        return ar("p3", q, zz, fin_p.at[pl.ds(0, size)], out_ref.at[y, zz, pl.ds(off, size)], p)

    def own_p(size, off):
        return pltpu.make_async_copy(fin_p.at[pl.ds(0, size)], out_ref.at[y, z, pl.ds(off, size)], osem.at[3])

    own_q = pltpu.make_async_copy(fin_q, out_ref.at[y, z, pl.ds(qoff, qn)], osem.at[4])

    def stage(off, size, ooff, osize):
        for d in range(nz - 1):
            p2_copy(d, size, True).wait_send()
            p2_copy(d, size, False).wait_recv()
        part = pzf[z, 0:size]
        for q, p in zpeers:
            part = part + pzr[q, 0:size].astype(F32)
        fin_p[0:size] = (part * scale).astype(BF)
        own_p(size, off).start()
        for d in range(nz - 1):
            p3(d, size, off, True).start()

    by_core(stage)

    def q3(d, out):
        q, p = ypeers[d]
        qq = y if out else q
        return ar("q3", q, qq, fin_q, out_ref.at[qq, z, pl.ds(qoff, qn)], p)

    for d in range(ny - 1):
        q2(d, True).wait_send()
        q2(d, False).wait_recv()
    part = qyf[y]
    for q, p in ypeers:
        part = part + qyr[q].astype(F32)
    fin_q[...] = (part * scale).astype(BF)
    own_q.start()
    for d in range(ny - 1):
        q3(d, True).start()

    margins(1)
    receive(1, (1, 2))
    for a in range(3):
        row_taps(1, 0, a, tu, False, 1.0)
    field[:, :, left] = dot(tu[0:cells], wraw[2]).reshape(6, F, C)

    def p4(d, size, off, out):
        q, p = ypeers[d]
        qq = y if out else q
        ref = out_ref.at[qq, :, pl.ds(off, size)]
        return ar("p4", q, qq, ref, ref, p)

    def cpy_p(q, size, off):
        ref = out_ref.at[q, :, pl.ds(off, size)]
        return ar("c4", q, q, ref, ref, partner)

    def stage(off, size, ooff, osize):
        for d in range(nz - 1):
            p3(d, size, off, True).wait_send()
            p3(d, size, off, False).wait_recv()
        own_p(size, off).wait()
        for d in range(ny - 1):
            p4(d, size, off, True).start()
        cpy_p(y, size, off).start()

    by_core(stage)

    def q4(d, out):
        q, p = zpeers[d]
        qq = z if out else q
        ref = out_ref.at[:, qq, pl.ds(qoff, qn)]
        return ar("q4", q, qq, ref, ref, p)

    def cpy_q(q, o):
        ref = out_ref.at[:, q, pl.ds(o, qn)]
        return ar("d4", q, q, ref, ref, partner)

    for d in range(ny - 1):
        q3(d, True).wait_send()
        q3(d, False).wait_recv()
    own_q.wait()
    for d in range(nz - 1):
        q4(d, True).start()
    cpy_q(z, qoff).start()

    receive_margins(1)
    forward_sides(1, 0, tu)
    add_sides(field, left, dot(tu[cells:], wraw[2]))
    res[0] = (rb[0, 0, 1].astype(F32) + 0.5 * field[:, :, left]).astype(BF)
    outs[0].start()

    def adjoint_of(i, dst, weights, ref, lanes):
        for a in range(3):
            row_taps(1, i, a, dst, True, 1.0)
        spread_sides(1, i, dst, 1.0)
        main_spread(1, i, dst, tx, weights, 1.0, ref, lanes)
        add_sides(ref, lanes, dot(dst[cells:], weights))

    adjoint_of(1, ts, ws1[...], front, both)
    res[1] = (rb[0, 2, 1].astype(F32) + front[:, :, left]).astype(BF)
    outs[1].start()

    adjoint_of(2, ts, ws1[:, 0:C], field, left)
    res[2] = (front[:, :, right] + field[:, :, left]).astype(BF)
    outs[2].start()

    def stage(off, size, ooff, osize):
        for d in range(ny - 1):
            p4(d, size, off, False).wait_recv()
            cpy_p(ypeers[d][0], size, off).start()

    by_core(stage)
    for d in range(nz - 1):
        q4(d, False).wait_recv()
        cpy_q(zpeers[d][0], qoff).start()

    def stage(off, size, ooff, osize):
        for d in range(ny - 1):
            p4(d, size, off, True).wait_send()
        for q in range(ny):
            cpy_p(q, size, off).wait_send()
            cpy_p(q, osize, ooff).wait_recv()

    by_core(stage)
    for d in range(nz - 1):
        q4(d, True).wait_send()
    for q in range(nz):
        cpy_q(q, qoff).wait_send()
        cpy_q(q, qother).wait_recv()
    for cp in outs:
        cp.wait()
    finish_sends(0)
    finish_sends(1)


PHASES = (
    ("cp", "1"),
    ("cq", "1"),
    ("q1", "z"),
    ("p1", "y"),
    ("p2", "z"),
    ("q2", "y"),
    ("p3", "z"),
    ("q3", "y"),
    ("p4", "y"),
    ("c4", "y"),
    ("q4", "z"),
    ("d4", "z"),
)


def split_rows(ny, nz):
    tiles = 4 * K9 // (16 * ny * nz)
    qn = 2 * tiles // 9
    p1 = (tiles - 2 * qn) // 2
    return 16 * tiles, 16 * (tiles - 2 * qn - p1), 16 * p1, 16 * qn


CHUNKS = 8


def finish(n_ref, a_ref, t_ref, g_ref, n_out, a_out, t_out, w_out, h_out, packed, wide, held, in_sem, out_sem, row_in, row_out):
    size = packed.shape[1]
    row_ins = [pltpu.make_async_copy(src, held.at[i], row_in.at[i]) for i, src in enumerate((n_ref, a_ref, t_ref))]
    row_outs = [pltpu.make_async_copy(held.at[i], dst, row_out.at[i]) for i, dst in enumerate((n_out, a_out, t_out))]
    half = CHUNKS // 2
    ins = [pltpu.make_async_copy(g_ref.at[pl.ds(i * size, size)], packed.at[i], in_sem.at[i]) for i in range(CHUNKS)]
    outs = [
        pltpu.make_async_copy(wide.at[i], (w_out, h_out)[i // half].at[pl.ds(i % half * size, size)], out_sem.at[i])
        for i in range(CHUNKS)
    ]
    for cp in ins + row_ins:
        cp.start()
    for i in range(CHUNKS):
        ins[i].wait()
        wide[i] = packed[i].astype(F32)
        outs[i].start()
    for i in range(3):
        row_ins[i].wait()
        row_outs[i].start()
    for cp in outs + row_outs:
        cp.wait()


def on_device(n, ny, nz, u, v, c, w1, w2, t1, t2, nb):
    F = n
    cells = 6 * F
    shard, p0, p1, qn = split_rows(ny, nz)
    arrived = sum(ny if c == "y" else nz if c == "z" else 1 for _, c in PHASES)
    u, v, c = (a.reshape(6, F, C) for a in (u, v, c))
    w1, w2, t1, t2 = (a.reshape(K9, C) for a in (w1, w2, t1, t2))
    vm = pltpu.VMEM
    dma = pltpu.SemaphoreType.DMA
    anywhere = pl.BlockSpec(memory_space=pl.ANY)
    inside = pl.BlockSpec(memory_space=pltpu.VMEM)
    row = jax.ShapeDtypeStruct((6, F, C), BF)
    nxt, adj, adt, out = pl.pallas_call(
        functools.partial(kernel, n, ny, nz),
        out_shape=(row, row, row, jax.ShapeDtypeStruct((ny, nz, shard, C), BF)),
        in_specs=[anywhere] * 8,
        out_specs=(anywhere,) * 4,
        scratch_shapes=[
            vm((2, 3, 3, 6, F, C), BF),
            vm((2, 3, 6, F, C), BF),
            vm((2, 160, C), BF),
            vm((2, 64, C), BF),
            vm((2, F, 32, C), BF),
            vm((2, F, 32, C), BF),
            vm((2, 3, 48, C), BF),
            vm((48, 160), BF),
            vm((64, 48), BF),
            vm((8 * F, cells), BF),
            vm((cells, 8 * F), BF),
            vm((cells, cells), BF),
            vm((cells, cells), BF),
            vm((4, K9, C), BF),
            vm((K9, 2 * C), BF),
            vm((K9, 2 * C), BF),
            vm((K9, 2 * C), BF),
            vm((6, F + 16, C), F32),
            vm((cells + SIDES, K9), BF),
            vm((cells + SIDES, K9), BF),
            vm((cells + SIDES, K9), BF),
            vm((cells, K9), BF),
            vm((cells + SIDES, 2 * C), BF),
            vm((cells + SIDES, 2 * C), BF),
            vm((6, F, 2 * C), F32),
            vm((6, F, 2 * C), F32),
            vm((4 * K9, C), F32),
            vm((ny, nz, shard, C), BF),
            vm((ny, nz, shard, C), BF),
            vm((ny, nz, p0, C), F32),
            vm((ny, nz, p0, C), BF),
            vm((ny, nz, p0, C), BF),
            vm((ny, nz, qn, C), F32),
            vm((ny, nz, qn, C), BF),
            vm((nz, ny, qn, C), BF),
            vm((nz, p0, C), BF),
            vm((nz, p0, C), F32),
            vm((nz, p0, C), BF),
            vm((ny, qn, C), BF),
            vm((ny, qn, C), F32),
            vm((ny, qn, C), BF),
            pltpu.SMEM((4, 6), jnp.int32),
            vm((3, 6, F, C), BF),
            vm((p0, C), BF),
            vm((qn, C), BF),
            dma((5,)),
            dma((8,)),
            dma((2, 3, 2)),
            dma((2, 3, 2)),
            dma((2,)),
            dma((2,)),
            dma((2, 2)),
            dma((2, n)),
            dma((2, n)),
            dma((2, 2)),
            dma((2, 2)),
            dma((2, 2)),
            dma((arrived,)),
            dma((arrived,)),
        ],
        compiler_params=pltpu.CompilerParams(
            collective_id=0, has_side_effects=True, vmem_limit_bytes=56 * 2**20
        ),
    )(u, v, c, w1, w2, t1, t2, nb.T)
    half = 2 * K9
    grad = jax.ShapeDtypeStruct((half, C), F32)
    nxt, adj, adt, wg, hp = pl.pallas_call(
        finish,
        out_shape=(row, row, row, grad, grad),
        in_specs=[anywhere] * 4,
        out_specs=(anywhere,) * 5,
        scratch_shapes=[vm((CHUNKS, 2 * half // CHUNKS, C), BF), vm((CHUNKS, 2 * half // CHUNKS, C), F32), vm((3, 6, F, C), BF), dma((CHUNKS,)), dma((CHUNKS,)), dma((3,)), dma((3,))],
        compiler_params=pltpu.CompilerParams(vmem_limit_bytes=56 * 2**20),
    )(nxt, adj, adt, out.reshape(2 * half, C))
    shape4 = (2, 9, C, C)
    shape = (6, 1, F, C)
    return nxt.reshape(shape), adj.reshape(shape), adt.reshape(shape), wg.reshape(shape4), hp.reshape(shape4)


def solution(mesh):
    n = mesh.shape["tile"] * mesh.shape["sub"]
    nz = 8 if n == 64 else 2
    ny = n // (2 * nz)
    field = P("rep", ("tile", "sub"), None, None)
    grads = P("rep", None, None, None)
    return jax.shard_map(
        functools.partial(on_device, n, ny, nz),
        mesh=mesh,
        in_specs=(field, field, field, P(), P(), P(), P(), P()),
        out_specs=(field, field, field, grads, grads),
        check_vma=False,
    )
```

```python
import functools

import jax
import jax.numpy as jnp
from jax import lax
from jax.experimental import pallas as pl
from jax.experimental.pallas import tpu as pltpu
from jax.sharding import PartitionSpec as P

MESH = pl.DeviceIdType.MESH
BF = jnp.bfloat16
F32 = jnp.float32
C = 128
K9 = 9 * C
SIDES = 16


def dot(a, b):
    return jnp.dot(a, b, preferred_element_type=F32)


def dot_t(a, b):
    return lax.dot_general(a, b, (((0,), (0,)), ((), ())), preferred_element_type=F32)


def iota(shape, dim):
    return lax.broadcasted_iota(jnp.int32, shape, dim)


def onehot(mask):
    return jnp.where(mask, 1.0, 0.0).astype(BF)


def kernel(
    n,
    ny,
    nz,
    u_ref,
    v_ref,
    c_ref,
    w1_ref,
    w2_ref,
    t1_ref,
    t2_ref,
    nb_ref,
    next_ref,
    adj_ref,
    adt_ref,
    out_ref,
    rb,
    mb,
    ebuf,
    hm,
    zs,
    rx,
    mt,
    sel,
    selh,
    amat,
    bmat,
    c0mat,
    c2mat,
    wraw,
    wf1,
    ws1,
    ws2,
    padz,
    tu,
    tv,
    ts,
    tx,
    aext,
    pext,
    front,
    field,
    gsum,
    gs,
    gr,
    pf,
    ps,
    pr,
    qf,
    qs,
    qr,
    pz,
    pzf,
    pzr,
    qy,
    qyf,
    qyr,
    nbm,
    res,
    fin_p,
    fin_q,
    osem,
    lsem,
    bulk_s,
    bulk_r,
    e_s,
    e_r,
    hm_s,
    rx_r,
    z_s,
    z_r,
    mt_s,
    mt_r,
    ar_s,
    ar_r,
):
    F = n
    cells = 6 * F
    rep = lax.axis_index("rep")
    r = lax.axis_index("tile") * 2 + lax.axis_index("sub")
    core = lax.rem(lax.div(r, 2), 2)
    z = lax.rem(lax.div(r, 4), nz)
    yhi = lax.div(r, 4 * nz)
    ylo = lax.rem(r, 2)
    y = yhi * 2 + ylo

    def dev(p):
        return (lax.div(p, 2), lax.rem(p, 2), rep)

    def make(hi, zc, co, lo):
        return ((hi * nz + zc) * 2 + co) * 2 + lo

    up = lax.rem(r + n - 1, n)
    dn = lax.rem(r + 1, n)
    mirror = n - 1 - r
    odd = lax.rem(r, 2)
    beside = r + 1 - 2 * odd
    beyond = lax.rem(r + n - 1 + 2 * odd, n)
    outer = jnp.logical_or(lax.rem(r, 4) == 0, lax.rem(r, 4) == 3)
    slot_in = 2 - 2 * odd
    slot_out = 2 * odd
    partner = make(yhi, z, 1 - core, ylo)

    def ypeer(d):
        q = lax.rem(y + d, ny)
        return q, make(lax.div(q, 2), z, core, lax.rem(q, 2))

    def zpeer(d):
        q = lax.rem(z + d, nz)
        return q, make(yhi, q, core, ylo)

    is0 = r == 0
    is1 = r == n - 1
    ishub = jnp.logical_or(is0, is1)

    def rcopy(src, dst, ssem, rsem, p):
        return pltpu.make_async_remote_copy(
            src_ref=src,
            dst_ref=dst,
            send_sem=ssem,
            recv_sem=rsem,
            device_id=dev(p),
            device_id_type=MESH,
        )

    nbload = pltpu.make_async_copy(nb_ref, nbm, lsem.at[7])
    nbload.start()
    loads = [pltpu.make_async_copy(ref, rb.at[0, i, 1], lsem.at[i]) for i, ref in enumerate((u_ref, v_ref, c_ref))]
    wloads = [pltpu.make_async_copy(ref, wraw.at[i], lsem.at[3 + i]) for i, ref in enumerate((w1_ref, t1_ref, w2_ref, t2_ref))]
    for cp in loads + wloads:
        cp.start()

    barrier = pltpu.get_barrier_semaphore()

    def greet(p):
        pl.semaphore_signal(barrier, inc=1, device_id=dev(p), device_id_type=MESH)

    @pl.when(ishub)
    def _():
        def body(i, carry):
            greet(lax.rem(r + i, n))
            return carry

        lax.fori_loop(1, n, body, 0)

    @pl.when(r != 0)
    def _():
        greet(0)

    @pl.when(r != n - 1)
    def _():
        greet(n - 1)

    for p in (up, dn, mirror, partner):
        greet(p)
    for d in range(1, ny):
        greet(ypeer(d)[1])
    for d in range(1, nz):
        greet(zpeer(d)[1])

    nbload.wait()
    nbs = [[nbm[s, f] for s in range(4)] for f in range(6)]
    x = iota((48, 160), 0)
    yy = iota((48, 160), 1)
    xs = x & 15
    xsd = jnp.where(xs < 8, 1, 3)
    xnb = jnp.full((48, 160), -1, jnp.int32)
    for f in range(6):
        xnb = jnp.where(xs == f, nbs[f][1], xnb)
        xnb = jnp.where(xs == 8 + f, nbs[f][3], xnb)
    ym = jnp.where(yy >= 48, yy - 48, yy)
    ysd = jnp.where((ym & 15) < 8, 1, 3)
    yz = (yy - 96) & 31
    isz = yy >= 96
    yg = jnp.where(isz, yz & 7, ym & 7)
    yt = jnp.where(isz, jnp.where(yy >= 128, 2, 0), ysd)
    yfield = jnp.where(isz, yz >> 3, ym >> 4)
    way = jnp.where(isz, 1, jnp.where(yy >= 48, jnp.where(xsd == ysd, 1, 0), jnp.where(xsd == ysd, 0, 1)))
    sel[...] = onehot((xnb == 4 * yg + yt) & ((x >> 4) == yfield) & (yg < 6) & (way == 1))
    x = iota((64, 48), 0)
    yy = iota((64, 48), 1)
    xnb = jnp.full((64, 48), -1, jnp.int32)
    for f in range(6):
        xnb = jnp.where((x & 7) == f, jnp.where(x < 32, nbs[f][0], nbs[f][2]), xnb)
    yt = jnp.where((yy & 15) < 8, 1, 3)
    selh[...] = onehot((xnb == 4 * (yy & 7) + yt) & (((x & 31) >> 3) == (yy >> 4)) & ((yy & 7) < 6))

    def chosen(s, code, offset):
        t = code & 3
        flipped = (s < 2) == (t < 2)
        along = jnp.where(flipped, 1 - offset, offset - 1)
        row_tap = jnp.where(t == 0, 0, jnp.where(t == 2, 2, 1 - along))
        col_tap = jnp.where(t == 1, 2, jnp.where(t == 3, 0, 1 - along))
        return 3 * row_tap + col_tap

    xs = iota((SIDES, C), 0)
    code = jnp.full((SIDES, C), 0, jnp.int32)
    for f in range(6):
        code = jnp.where(xs == f, nbs[f][1], code)
        code = jnp.where(xs == 8 + f, nbs[f][3], code)
    side_taps = [chosen(jnp.where(xs < 8, 1, 3), code, o) for o in range(3)]

    hub_side = jnp.where(is0, 0, 2)
    hub_nb = [jnp.where(is0, nbs[f][0], nbs[f][2]) for f in range(6)]
    hub_flip = [((hub_side < 2) == ((code_f & 3) < 2)).astype(jnp.int32) for code_f in hub_nb]

    def per_face(face, values, start):
        result = jnp.full(face.shape, start, jnp.int32)
        for f in range(6):
            result = jnp.where(face == f, values[f], result)
        return result

    @pl.when(ishub)
    def _():
        a = iota((8 * F, cells), 0)
        b = iota((8 * F, cells), 1)
        g = a & 7
        pos = a >> 3
        target = g * F + jnp.where(per_face(g, hub_flip, 0) == 1, F - 1 - pos, pos)
        amat[...] = onehot((b == target) & (g < 6))

    def edges(ph, i):
        row = rb[ph, i, 1].astype(F32)
        zero = jnp.zeros((2, C), F32)
        return jnp.concatenate([row[:, F - 1], zero, row[:, 0], zero], axis=0).astype(BF)

    def prepare(ph):
        for i in range(3):
            ebuf[ph, 16 * i : 16 * i + 16] = edges(ph, i)
        hm[ph] = dot(selh[...], ebuf[ph, 0:48]).astype(BF)

        @pl.when(ishub)
        def _():
            parts = []
            for i in range(3):
                parts.append(dot(amat[...], rb[ph, i, 1].reshape(cells, C)).reshape(F, 8, C))
            parts.append(jnp.zeros((F, 8, C), F32))
            zs[ph] = jnp.concatenate(parts, axis=1).astype(BF)

        @pl.when(is0)
        def _():
            rx[ph, 0] = hm[ph, 0:32]
            ebuf[ph, 96:128] = zs[ph, 0]

        @pl.when(is1)
        def _():
            rx[ph, n - 1] = hm[ph, 32:64]
            ebuf[ph, 128:160] = zs[ph, n - 1]

    def e_copy(ph):
        return rcopy(ebuf.at[ph, pl.ds(0, 48)], ebuf.at[ph, pl.ds(48, 48)], e_s.at[ph], e_r.at[ph], mirror)

    def hm_copy(ph, h):
        return rcopy(
            hm.at[ph, pl.ds(32 * h, 32)],
            rx.at[ph, r],
            hm_s.at[ph, h],
            rx_r.at[ph, r],
            (n - 1) * h,
        )

    def z_copy(ph, h, p):
        return rcopy(zs.at[ph, p], ebuf.at[ph, pl.ds(96 + 32 * h, 32)], z_s.at[ph, p], z_r.at[ph, h], p)

    def row_beside(ph, i, out):
        slot = slot_out if out else slot_in
        return rcopy(rb.at[ph, i, 1], rb.at[ph, i, slot], bulk_s.at[ph, i, 0], bulk_r.at[ph, i, 0], beside)

    def row_beyond(ph, i, out):
        slot = slot_in if out else slot_out
        return rcopy(rb.at[ph, i, 1], rb.at[ph, i, slot], bulk_s.at[ph, i, 1], bulk_r.at[ph, i, 1], beyond)

    def row_inward(ph, i):
        return rcopy(rb.at[ph, i, slot_in], rb.at[ph, i, slot_out], bulk_s.at[ph, i, 2], bulk_r.at[ph, i, 1], partner)

    def send_rows(ph, fields=(0, 1, 2)):
        for i in fields:
            row_beside(ph, i, True).start()

            @pl.when(outer)
            def _():
                row_beyond(ph, i, True).start()

    def hand_row(ph, i):
        @pl.when(outer)
        def _():
            row_beside(ph, i, False).wait_recv()
            row_inward(ph, i).start()

    def receive_row(ph, i):
        @pl.when(jnp.logical_not(outer))
        def _():
            row_beside(ph, i, False).wait_recv()

        row_beyond(ph, i, False).wait_recv()

    def finish_rows(ph):
        for i in range(3):
            row_beside(ph, i, True).wait_send()

            @pl.when(outer)
            def _():
                row_beyond(ph, i, True).wait_send()
                row_inward(ph, i).wait_send()

    def mt_copy(ph, way):
        return rcopy(
            mt.at[ph, 1],
            mt.at[ph, 2 if way == 0 else 0],
            mt_s.at[ph, way],
            mt_r.at[ph, way],
            up if way == 0 else dn,
        )

    def hub_loop(step):
        def body(i, carry):
            step(lax.rem(r + i, n))
            return carry

        lax.fori_loop(1, n, body, 0)

    def send(ph):
        for h, here in ((0, is0), (1, is1)):

            @pl.when(here)
            def _():
                hub_loop(lambda p: z_copy(ph, h, p).start())

            @pl.when(jnp.logical_not(here))
            def _():
                hm_copy(ph, h).start()

        e_copy(ph).start()

    def margins(ph):
        e_copy(ph).wait()
        for h, here in ((0, is0), (1, is1)):

            @pl.when(jnp.logical_not(here))
            def _():
                z_copy(ph, h, 0).wait_recv()

        mt[ph, 1] = dot(sel[...], ebuf[ph]).astype(BF)
        for way in range(2):
            mt_copy(ph, way).start()

    def hub_wait(ph):
        @pl.when(ishub)
        def _():
            hub_loop(lambda p: rcopy(hm.at[ph, pl.ds(0, 32)], rx.at[ph, p], hm_s.at[ph, 0], rx_r.at[ph, p], p).wait_recv())

    def hub_row(ph, i, spreads):
        @pl.when(ishub)
        def _():
            slot = jnp.where(is0, 0, 2)
            piece = rx[ph].astype(F32)[:, 8 * i : 8 * i + 8].reshape(8 * F, C).astype(BF)
            row = dot(bmat[...], piece)
            row = row + dot(c0mat[...], rb[ph, i, 1].reshape(cells, C))
            row = row + dot(c2mat[...], rb[ph, i, slot].reshape(cells, C))
            row = row.astype(BF).reshape(6, F, C)
            if spreads:
                mb[ph, i] = row
                rb[ph, i, slot] = jnp.zeros((6, F, C), BF)
            else:
                rb[ph, i, slot] = row

    def receive_margins(ph):
        for way in range(2):
            mt_copy(ph, way).wait()

        @pl.when(is0)
        def _():
            mt[ph, 0] = jnp.zeros((48, C), BF)

        @pl.when(is1)
        def _():
            mt[ph, 2] = jnp.zeros((48, C), BF)

    def finish_sends(ph):
        for h, here in ((0, is0), (1, is1)):

            @pl.when(here)
            def _():
                hub_loop(lambda p: z_copy(ph, h, p).wait_send())

            @pl.when(jnp.logical_not(here))
            def _():
                hm_copy(ph, h).wait_send()

    def row_taps(ph, i, a, dst, spreads, scale):
        padz[:, 8 : 8 + F] = rb[ph, i, a].astype(F32) * scale
        for b in range(3):
            k = 3 * a + b
            k = 8 - k if spreads else k
            dst[0:cells, k * C : k * C + C] = padz[:, 7 + b : 7 + b + F].reshape(cells, C).astype(BF)

    def forward_sides(ph, i, dst):
        for a in range(3):
            line = mt[ph, a, 16 * i : 16 * i + 16].astype(F32)
            zero = jnp.zeros((SIDES, C), F32)
            for b, part in enumerate((jnp.where(xs < 8, zero, line), zero, jnp.where(xs < 8, line, zero))):
                k = 3 * a + b
                dst[cells : cells + SIDES, k * C : k * C + C] = part.astype(BF)

    def spread_sides(ph, i, dst, scale):
        lines = [mt[ph, o, 16 * i : 16 * i + 16].astype(F32) * scale for o in range(3)]
        for k in range(9):
            total = jnp.zeros((SIDES, C), F32)
            for o in range(3):
                total = jnp.where(side_taps[o] == k, lines[o], total)
            dst[cells : cells + SIDES, k * C : k * C + C] = total.astype(BF)

    def hub_taps(ph, i, extra, scale):
        padz[:, 8 : 8 + F] = mb[ph, i].astype(F32) * scale
        for f in range(6):
            picks = [chosen(hub_side, hub_nb[f], o) for o in range(3)]
            shifted = [padz[f, 7 + o : 7 + o + F] for o in range(3)]
            for k in range(9):
                total = jnp.zeros((F, C), F32)
                for o in range(3):
                    total = jnp.where(picks[o] == k, shifted[o], total)
                extra[f * F : f * F + F, k * C : k * C + C] = total.astype(BF)

    def add_sides(ref, lanes, side):
        for f in range(6):
            ref[f, F - 1 : F, lanes] += side[f : f + 1]
            ref[f, 0:1, lanes] += side[8 + f : 9 + f]

    def main_spread(ph, i, dst, extra, weights, scale, ref, lanes):
        width = lanes.stop - lanes.start
        ref[:, :, lanes] = dot(dst[0:cells], weights).reshape(6, F, width)

        @pl.when(ishub)
        def _():
            hub_taps(ph, i, extra, scale)
            ref[:, :, lanes] += dot(extra[...], weights).reshape(6, F, width)

    for cp in loads:
        cp.wait()
    prepare(0)
    base = 4 + (ny - 1) + (nz - 1)
    pl.semaphore_wait(barrier, base + 2 + jnp.where(ishub, n - 2, 0))
    send(0)
    send_rows(0)

    padz[...] = jnp.zeros(padz.shape, F32)
    for cp in wloads:
        cp.wait()
    wf1[:, 0:C] = wraw[0]
    wf1[:, C : 2 * C] = wraw[1]
    for k in range(9):
        rows = slice(k * C, k * C + C)
        ws1[rows, 0:C] = wraw[0, rows].astype(F32).T.astype(BF)
        ws1[rows, C : 2 * C] = wraw[1, rows].astype(F32).T.astype(BF)
        ws2[rows, 0:C] = wraw[2, rows].astype(F32).T.astype(BF)
        ws2[rows, C : 2 * C] = wraw[3, rows].astype(F32).T.astype(BF)

    @pl.when(ishub)
    def _():
        a = iota((cells, 8 * F), 0)
        b = iota((cells, 8 * F), 1)
        face = lax.div(a, F)
        pos = a - face * F
        pos = jnp.where(per_face(face, hub_flip, 0) == 1, F - 1 - pos, pos)
        column = per_face(face, [code_f & 1 for code_f in hub_nb], 0)
        bmat[...] = onehot((b == 8 * pos + face) & (column == 1))
        a = iota((cells, cells), 0)
        b = iota((cells, cells), 1)
        face = lax.div(a, F)
        pos = a - face * F
        code_a = per_face(face, hub_nb, 0)
        other = (code_a >> 2) * F
        c0mat[...] = onehot(((code_a & 3) == hub_side) & (b == other + F - 1 - pos))
        c2mat[...] = onehot(((code_a & 3) == 2 - hub_side) & (b == other + pos))

    inputs = ((0, tu, False, 1.0), (1, tv, False, 1.0), (2, ts, True, 0.5))
    for i, dst, spreads, scale in inputs:
        row_taps(0, i, 1, dst, spreads, scale)
    both = slice(0, 2 * C)
    left = slice(0, C)
    right = slice(C, 2 * C)

    def field_rows(i):
        receive_row(0, i)
        _, dst, spreads, scale = inputs[i]
        hub_row(0, i, spreads)
        row_taps(0, i, 0, dst, spreads, scale)
        row_taps(0, i, 2, dst, spreads, scale)

    hand_row(0, 0)
    margins(0)
    hand_row(0, 1)
    hub_wait(0)
    field_rows(0)
    front[...] = dot(tu[0:cells], wf1[...]).reshape(6, F, 2 * C)
    hand_row(0, 2)
    field_rows(1)
    front[:, :, right] += dot(tv[0:cells], wraw[0]).reshape(6, F, C)
    field_rows(2)
    main_spread(0, 2, ts, tx, ws2[...], 0.5, field, both)
    receive_margins(0)
    forward_sides(0, 0, tu)
    forward_sides(0, 1, tv)
    spread_sides(0, 2, ts, 0.5)
    side = dot(tu[cells:], wf1[...])
    more = dot(tv[cells:], wraw[0])
    add_sides(front, both, side)
    add_sides(front, right, more)
    add_sides(field, both, dot(ts[cells:], ws2[...]))
    squash = jnp.tanh(front[:, :, left])
    derivative = 1.0 - squash * squash
    hidden_tangent = front[:, :, right]
    act_tangent = (derivative * hidden_tangent).astype(BF)
    backward = field[:, :, left]
    scaled = derivative * backward
    rb[1, 0, 1] = squash.astype(BF)
    rb[1, 1, 1] = scaled.astype(BF)
    rb[1, 2, 1] = (derivative * field[:, :, right] - 2.0 * squash * scaled * hidden_tangent).astype(BF)
    aext[0:cells, right] = act_tangent.reshape(cells, C)

    send_rows(1, (0,))

    aext[0:cells, left] = rb[1, 0, 1].reshape(cells, C)
    aext[cells:, left] = edges(1, 0)
    zero = jnp.zeros((2, C), F32)
    wide = act_tangent.astype(F32)
    aext[cells:, right] = jnp.concatenate([wide[:, F - 1], zero, wide[:, 0], zero], axis=0).astype(BF)
    for i, lanes in ((1, left), (2, right)):
        pext[0:cells, lanes] = rb[1, i, 1].reshape(cells, C)
        pext[cells:, lanes] = edges(1, i)
    first = dot_t(tu[...], pext[...])
    gsum[0:K9] = first[:, 0:C]
    gsum[2 * K9 : 3 * K9] = first[:, C : 2 * C] + dot_t(tv[...], pext[:, left])
    second = dot_t(aext[...], ts[...])
    for k in range(9):
        gsum[K9 + k * C : K9 + k * C + C] = second[0:C, k * C : k * C + C]
        gsum[3 * K9 + k * C : 3 * K9 + k * C + C] = second[C : 2 * C, k * C : k * C + C]

    @pl.when(ishub)
    def _():
        more = dot_t(aext[0:cells], tx[...])
        for k in range(9):
            gsum[K9 + k * C : K9 + k * C + C] += more[0:C, k * C : k * C + C]
            gsum[3 * K9 + k * C : 3 * K9 + k * C + C] += more[C : 2 * C, k * C : k * C + C]

    outs = [pltpu.make_async_copy(res.at[i], ref, osem.at[i]) for i, ref in enumerate((next_ref, adj_ref, adt_ref))]

    shard, p0, p1, qn = split_rows(ny, nz)
    qoff = p0 + p1 + qn * core
    qother = p0 + p1 + qn * (1 - core)
    slots = {}
    for name, count in PHASES:
        slots[name] = sum(ny if c == "y" else nz if c == "z" else 1 for _, c in PHASES[: len(slots)])

    def by_core(fn):
        @pl.when(core == 0)
        def _():
            fn(0, p0, p0, p1)

        @pl.when(core == 1)
        def _():
            fn(p0, p1, 0, p0)

    def ar(name, slot_s, slot_r, src, dst, p):
        return rcopy(src, dst, ar_s.at[slots[name] + slot_s], ar_r.at[slots[name] + slot_r], p)

    ypeers = [ypeer(d) for d in range(1, ny)]
    zpeers = [zpeer(d) for d in range(1, nz)]
    whole = gsum[...].reshape(ny, nz, shard, C)
    gs[...] = whole.astype(BF)

    def core_p(off, size, ooff, osize):
        return ar("cp", 0, 0, gs.at[:, :, pl.ds(ooff, osize)], gr.at[:, :, pl.ds(ooff, osize)], partner)

    def core_p_in(off, size, ooff, osize):
        return ar("cp", 0, 0, gs.at[:, :, pl.ds(off, size)], gr.at[:, :, pl.ds(off, size)], partner)

    def core_q(o):
        return ar("cq", 0, 0, gs.at[:, :, pl.ds(o, qn)], gr.at[:, :, pl.ds(o, qn)], partner)

    core_q(qother).start()
    by_core(lambda *a: core_p(*a).start())

    def q1(d, out):
        q, p = zpeers[d]
        return ar("q1", q, z if out else q, qs.at[:, q], qr.at[z if out else q], p)

    def p1_copy(d, size, out):
        q, p = ypeers[d]
        return ar("p1", q, y if out else q, ps.at[q, :, pl.ds(0, size)], pr.at[y if out else q, :, pl.ds(0, size)], p)

    core_q(qother).wait_send()
    core_q(qoff).wait_recv()

    def stage(qo):
        part = gsum[...].reshape(ny, nz, shard, C)[:, :, qo : qo + qn] + gr[:, :, qo : qo + qn].astype(F32)
        qf[...] = part
        qs[...] = part.astype(BF)

    by_core(lambda off, size, ooff, osize: stage(p0 + p1 if off == 0 else p0 + p1 + qn))
    for d in range(nz - 1):
        q1(d, True).start()

    def stage(off, size, ooff, osize):
        core_p(off, size, ooff, osize).wait_send()
        core_p_in(off, size, ooff, osize).wait_recv()
        part = gsum[...].reshape(ny, nz, shard, C)[:, :, off : off + size] + gr[:, :, off : off + size].astype(F32)
        pf[:, :, 0:size] = part
        ps[:, :, 0:size] = part.astype(BF)
        for d in range(ny - 1):
            p1_copy(d, size, True).start()

    by_core(stage)
    prepare(1)
    send(1)
    send_rows(1, (1, 2))

    def p2_copy(d, size, out):
        q, p = zpeers[d]
        return ar("p2", q, z if out else q, pz.at[q, pl.ds(0, size)], pzr.at[z if out else q, pl.ds(0, size)], p)

    def stage(off, size, ooff, osize):
        for d in range(ny - 1):
            p1_copy(d, size, True).wait_send()
            p1_copy(d, size, False).wait_recv()
        part = pf[y, :, 0:size]
        for q, p in ypeers:
            part = part + pr[q, :, 0:size].astype(F32)
        pzf[:, 0:size] = part
        pz[:, 0:size] = part.astype(BF)
        for d in range(nz - 1):
            p2_copy(d, size, True).start()

    by_core(stage)

    def q2(d, out):
        q, p = ypeers[d]
        return ar("q2", q, y if out else q, qy.at[q], qyr.at[y if out else q], p)

    for d in range(nz - 1):
        q1(d, True).wait_send()
        q1(d, False).wait_recv()
    part = qf[:, z]
    for q, p in zpeers:
        part = part + qr[q].astype(F32)
    qyf[...] = part
    qy[...] = part.astype(BF)
    for d in range(ny - 1):
        q2(d, True).start()

    scale = 1.0 / F

    def p3(d, size, off, out):
        q, p = zpeers[d]
        zz = z if out else q
        return ar("p3", q, zz, fin_p.at[pl.ds(0, size)], out_ref.at[y, zz, pl.ds(off, size)], p)

    def own_p(size, off):
        return pltpu.make_async_copy(fin_p.at[pl.ds(0, size)], out_ref.at[y, z, pl.ds(off, size)], osem.at[3])

    own_q = pltpu.make_async_copy(fin_q, out_ref.at[y, z, pl.ds(qoff, qn)], osem.at[4])

    def stage(off, size, ooff, osize):
        for d in range(nz - 1):
            p2_copy(d, size, True).wait_send()
            p2_copy(d, size, False).wait_recv()
        part = pzf[z, 0:size]
        for q, p in zpeers:
            part = part + pzr[q, 0:size].astype(F32)
        fin_p[0:size] = (part * scale).astype(BF)
        own_p(size, off).start()
        for d in range(nz - 1):
            p3(d, size, off, True).start()

    by_core(stage)

    def q3(d, out):
        q, p = ypeers[d]
        qq = y if out else q
        return ar("q3", q, qq, fin_q, out_ref.at[qq, z, pl.ds(qoff, qn)], p)

    for d in range(ny - 1):
        q2(d, True).wait_send()
        q2(d, False).wait_recv()
    part = qyf[y]
    for q, p in ypeers:
        part = part + qyr[q].astype(F32)
    fin_q[...] = (part * scale).astype(BF)
    own_q.start()
    for d in range(ny - 1):
        q3(d, True).start()

    for i in range(3):
        hand_row(1, i)
    margins(1)
    hub_wait(1)
    for i in range(3):
        receive_row(1, i)
        hub_row(1, i, i > 0)
    for a in range(3):
        row_taps(1, 0, a, tu, False, 1.0)
    field[:, :, left] = dot(tu[0:cells], wraw[2]).reshape(6, F, C)

    def p4(d, size, off, out):
        q, p = ypeers[d]
        qq = y if out else q
        ref = out_ref.at[qq, :, pl.ds(off, size)]
        return ar("p4", q, qq, ref, ref, p)

    def cpy_p(q, size, off):
        ref = out_ref.at[q, :, pl.ds(off, size)]
        return ar("c4", q, q, ref, ref, partner)

    def stage(off, size, ooff, osize):
        for d in range(nz - 1):
            p3(d, size, off, True).wait_send()
            p3(d, size, off, False).wait_recv()
        own_p(size, off).wait()
        for d in range(ny - 1):
            p4(d, size, off, True).start()
        cpy_p(y, size, off).start()

    by_core(stage)

    def q4(d, out):
        q, p = zpeers[d]
        qq = z if out else q
        ref = out_ref.at[:, qq, pl.ds(qoff, qn)]
        return ar("q4", q, qq, ref, ref, p)

    def cpy_q(q, o):
        ref = out_ref.at[:, q, pl.ds(o, qn)]
        return ar("d4", q, q, ref, ref, partner)

    for d in range(ny - 1):
        q3(d, True).wait_send()
        q3(d, False).wait_recv()
    own_q.wait()
    for d in range(nz - 1):
        q4(d, True).start()
    cpy_q(z, qoff).start()

    receive_margins(1)
    forward_sides(1, 0, tu)
    add_sides(field, left, dot(tu[cells:], wraw[2]))
    res[0] = (rb[0, 0, 1].astype(F32) + 0.5 * field[:, :, left]).astype(BF)
    outs[0].start()

    def adjoint_of(i, dst, weights, ref, lanes):
        for a in range(3):
            row_taps(1, i, a, dst, True, 1.0)
        spread_sides(1, i, dst, 1.0)
        main_spread(1, i, dst, tx, weights, 1.0, ref, lanes)
        add_sides(ref, lanes, dot(dst[cells:], weights))

    adjoint_of(1, ts, ws1[...], front, both)
    res[1] = (rb[0, 2, 1].astype(F32) + front[:, :, left]).astype(BF)
    outs[1].start()

    adjoint_of(2, ts, ws1[:, 0:C], field, left)
    res[2] = (front[:, :, right] + field[:, :, left]).astype(BF)
    outs[2].start()

    def stage(off, size, ooff, osize):
        for d in range(ny - 1):
            p4(d, size, off, False).wait_recv()
            cpy_p(ypeers[d][0], size, off).start()

    by_core(stage)
    for d in range(nz - 1):
        q4(d, False).wait_recv()
        cpy_q(zpeers[d][0], qoff).start()

    def stage(off, size, ooff, osize):
        for d in range(ny - 1):
            p4(d, size, off, True).wait_send()
        for q in range(ny):
            cpy_p(q, size, off).wait_send()
            cpy_p(q, osize, ooff).wait_recv()

    by_core(stage)
    for d in range(nz - 1):
        q4(d, True).wait_send()
    for q in range(nz):
        cpy_q(q, qoff).wait_send()
        cpy_q(q, qother).wait_recv()
    for cp in outs:
        cp.wait()
    for ph in range(2):
        finish_sends(ph)
        finish_rows(ph)


PHASES = (
    ("cp", "1"),
    ("cq", "1"),
    ("q1", "z"),
    ("p1", "y"),
    ("p2", "z"),
    ("q2", "y"),
    ("p3", "z"),
    ("q3", "y"),
    ("p4", "y"),
    ("c4", "y"),
    ("q4", "z"),
    ("d4", "z"),
)


def split_rows(ny, nz):
    tiles = 4 * K9 // (16 * ny * nz)
    qn = 2 * tiles // 9
    p1 = (tiles - 2 * qn) // 2
    return 16 * tiles, 16 * (tiles - 2 * qn - p1), 16 * p1, 16 * qn


CHUNKS = 8


def finish(n_ref, a_ref, t_ref, g_ref, n_out, a_out, t_out, w_out, h_out, packed, wide, held, in_sem, out_sem, row_in, row_out):
    size = packed.shape[1]
    row_ins = [pltpu.make_async_copy(src, held.at[i], row_in.at[i]) for i, src in enumerate((n_ref, a_ref, t_ref))]
    row_outs = [pltpu.make_async_copy(held.at[i], dst, row_out.at[i]) for i, dst in enumerate((n_out, a_out, t_out))]
    half = CHUNKS // 2
    ins = [pltpu.make_async_copy(g_ref.at[pl.ds(i * size, size)], packed.at[i], in_sem.at[i]) for i in range(CHUNKS)]
    outs = [
        pltpu.make_async_copy(wide.at[i], (w_out, h_out)[i // half].at[pl.ds(i % half * size, size)], out_sem.at[i])
        for i in range(CHUNKS)
    ]
    for cp in ins + row_ins:
        cp.start()
    for i in range(CHUNKS):
        ins[i].wait()
        wide[i] = packed[i].astype(F32)
        outs[i].start()
    for i in range(3):
        row_ins[i].wait()
        row_outs[i].start()
    for cp in outs + row_outs:
        cp.wait()


def on_device(n, ny, nz, u, v, c, w1, w2, t1, t2, nb):
    F = n
    cells = 6 * F
    shard, p0, p1, qn = split_rows(ny, nz)
    arrived = sum(ny if c == "y" else nz if c == "z" else 1 for _, c in PHASES)
    u, v, c = (a.reshape(6, F, C) for a in (u, v, c))
    w1, w2, t1, t2 = (a.reshape(K9, C) for a in (w1, w2, t1, t2))
    vm = pltpu.VMEM
    dma = pltpu.SemaphoreType.DMA
    anywhere = pl.BlockSpec(memory_space=pl.ANY)
    inside = pl.BlockSpec(memory_space=pltpu.VMEM)
    row = jax.ShapeDtypeStruct((6, F, C), BF)
    nxt, adj, adt, out = pl.pallas_call(
        functools.partial(kernel, n, ny, nz),
        out_shape=(row, row, row, jax.ShapeDtypeStruct((ny, nz, shard, C), BF)),
        in_specs=[anywhere] * 8,
        out_specs=(anywhere,) * 4,
        scratch_shapes=[
            vm((2, 3, 3, 6, F, C), BF),
            vm((2, 3, 6, F, C), BF),
            vm((2, 160, C), BF),
            vm((2, 64, C), BF),
            vm((2, F, 32, C), BF),
            vm((2, F, 32, C), BF),
            vm((2, 3, 48, C), BF),
            vm((48, 160), BF),
            vm((64, 48), BF),
            vm((8 * F, cells), BF),
            vm((cells, 8 * F), BF),
            vm((cells, cells), BF),
            vm((cells, cells), BF),
            vm((4, K9, C), BF),
            vm((K9, 2 * C), BF),
            vm((K9, 2 * C), BF),
            vm((K9, 2 * C), BF),
            vm((6, F + 16, C), F32),
            vm((cells + SIDES, K9), BF),
            vm((cells + SIDES, K9), BF),
            vm((cells + SIDES, K9), BF),
            vm((cells, K9), BF),
            vm((cells + SIDES, 2 * C), BF),
            vm((cells + SIDES, 2 * C), BF),
            vm((6, F, 2 * C), F32),
            vm((6, F, 2 * C), F32),
            vm((4 * K9, C), F32),
            vm((ny, nz, shard, C), BF),
            vm((ny, nz, shard, C), BF),
            vm((ny, nz, p0, C), F32),
            vm((ny, nz, p0, C), BF),
            vm((ny, nz, p0, C), BF),
            vm((ny, nz, qn, C), F32),
            vm((ny, nz, qn, C), BF),
            vm((nz, ny, qn, C), BF),
            vm((nz, p0, C), BF),
            vm((nz, p0, C), F32),
            vm((nz, p0, C), BF),
            vm((ny, qn, C), BF),
            vm((ny, qn, C), F32),
            vm((ny, qn, C), BF),
            pltpu.SMEM((4, 6), jnp.int32),
            vm((3, 6, F, C), BF),
            vm((p0, C), BF),
            vm((qn, C), BF),
            dma((5,)),
            dma((8,)),
            dma((2, 3, 3)),
            dma((2, 3, 2)),
            dma((2,)),
            dma((2,)),
            dma((2, 2)),
            dma((2, n)),
            dma((2, n)),
            dma((2, 2)),
            dma((2, 2)),
            dma((2, 2)),
            dma((arrived,)),
            dma((arrived,)),
        ],
        compiler_params=pltpu.CompilerParams(
            collective_id=0, has_side_effects=True, vmem_limit_bytes=56 * 2**20
        ),
    )(u, v, c, w1, w2, t1, t2, nb.T)
    half = 2 * K9
    grad = jax.ShapeDtypeStruct((half, C), F32)
    nxt, adj, adt, wg, hp = pl.pallas_call(
        finish,
        out_shape=(row, row, row, grad, grad),
        in_specs=[anywhere] * 4,
        out_specs=(anywhere,) * 5,
        scratch_shapes=[vm((CHUNKS, 2 * half // CHUNKS, C), BF), vm((CHUNKS, 2 * half // CHUNKS, C), F32), vm((3, 6, F, C), BF), dma((CHUNKS,)), dma((CHUNKS,)), dma((3,)), dma((3,))],
        compiler_params=pltpu.CompilerParams(vmem_limit_bytes=56 * 2**20),
    )(nxt, adj, adt, out.reshape(2 * half, C))
    shape4 = (2, 9, C, C)
    shape = (6, 1, F, C)
    return nxt.reshape(shape), adj.reshape(shape), adt.reshape(shape), wg.reshape(shape4), hp.reshape(shape4)


def solution(mesh):
    n = mesh.shape["tile"] * mesh.shape["sub"]
    nz = 8 if n == 64 else 2
    ny = n // (2 * nz)
    field = P("rep", ("tile", "sub"), None, None)
    grads = P("rep", None, None, None)
    return jax.shard_map(
        functools.partial(on_device, n, ny, nz),
        mesh=mesh,
        in_specs=(field, field, field, P(), P(), P(), P(), P()),
        out_specs=(field, field, field, grads, grads),
        check_vma=False,
    )
```

```python
import functools

import jax
import jax.numpy as jnp
from jax import lax
from jax.experimental import pallas as pl
from jax.experimental.pallas import tpu as pltpu
from jax.sharding import PartitionSpec as P

MESH = pl.DeviceIdType.MESH
BF = jnp.bfloat16
F32 = jnp.float32
C = 128
K9 = 9 * C
SIDES = 16


def dot(a, b):
    return jnp.dot(a, b, preferred_element_type=F32)


def dot_t(a, b):
    return lax.dot_general(a, b, (((0,), (0,)), ((), ())), preferred_element_type=F32)


def iota(shape, dim):
    return lax.broadcasted_iota(jnp.int32, shape, dim)


def onehot(mask):
    return jnp.where(mask, 1.0, 0.0).astype(BF)


def kernel(
    n,
    ny,
    nz,
    u_ref,
    v_ref,
    c_ref,
    w1_ref,
    w2_ref,
    t1_ref,
    t2_ref,
    nb_ref,
    next_ref,
    adj_ref,
    adt_ref,
    out_ref,
    rb,
    mb,
    ebuf,
    hm,
    zs,
    rx,
    mt,
    sel,
    selh,
    amat,
    bmat,
    c0mat,
    c2mat,
    wraw,
    wf1,
    ws1,
    ws2,
    padz,
    tu,
    tv,
    ts,
    tx,
    aext,
    pext,
    front,
    field,
    gsum,
    gs,
    gr,
    pf,
    ps,
    pr,
    qf,
    qs,
    qr,
    pz,
    pzf,
    pzr,
    qy,
    qyf,
    qyr,
    nbm,
    res,
    fin_p,
    fin_q,
    osem,
    lsem,
    bulk_s,
    bulk_r,
    e_s,
    e_r,
    hm_s,
    rx_r,
    z_s,
    z_r,
    mt_s,
    mt_r,
    ar_s,
    ar_r,
):
    F = n
    cells = 6 * F
    rep = lax.axis_index("rep")
    r = lax.axis_index("tile") * 2 + lax.axis_index("sub")
    core = lax.rem(lax.div(r, 2), 2)
    z = lax.rem(lax.div(r, 4), nz)
    yhi = lax.div(r, 4 * nz)
    ylo = lax.rem(r, 2)
    y = yhi * 2 + ylo

    def dev(p):
        return (lax.div(p, 2), lax.rem(p, 2), rep)

    def make(hi, zc, co, lo):
        return ((hi * nz + zc) * 2 + co) * 2 + lo

    up = lax.rem(r + n - 1, n)
    dn = lax.rem(r + 1, n)
    mirror = n - 1 - r
    odd = lax.rem(r, 2)
    beside = r + 1 - 2 * odd
    beyond = lax.rem(r + n - 1 + 2 * odd, n)
    outer = jnp.logical_or(lax.rem(r, 4) == 0, lax.rem(r, 4) == 3)
    slot_in = 2 - 2 * odd
    slot_out = 2 * odd
    partner = make(yhi, z, 1 - core, ylo)

    def ypeer(d):
        q = lax.rem(y + d, ny)
        return q, make(lax.div(q, 2), z, core, lax.rem(q, 2))

    def zpeer(d):
        q = lax.rem(z + d, nz)
        return q, make(yhi, q, core, ylo)

    is0 = r == 0
    is1 = r == n - 1
    ishub = jnp.logical_or(is0, is1)

    def rcopy(src, dst, ssem, rsem, p):
        return pltpu.make_async_remote_copy(
            src_ref=src,
            dst_ref=dst,
            send_sem=ssem,
            recv_sem=rsem,
            device_id=dev(p),
            device_id_type=MESH,
        )

    nbload = pltpu.make_async_copy(nb_ref, nbm, lsem.at[7])
    nbload.start()
    loads = [pltpu.make_async_copy(ref, rb.at[0, i, 1], lsem.at[i]) for i, ref in enumerate((u_ref, v_ref, c_ref))]
    wloads = [pltpu.make_async_copy(ref, wraw.at[i], lsem.at[3 + i]) for i, ref in enumerate((w1_ref, t1_ref, w2_ref, t2_ref))]
    for cp in loads + wloads:
        cp.start()

    barrier = pltpu.get_barrier_semaphore()

    def greet(p):
        pl.semaphore_signal(barrier, inc=1, device_id=dev(p), device_id_type=MESH)

    @pl.when(ishub)
    def _():
        def body(i, carry):
            greet(lax.rem(r + i, n))
            return carry

        lax.fori_loop(1, n, body, 0)

    @pl.when(r != 0)
    def _():
        greet(0)

    @pl.when(r != n - 1)
    def _():
        greet(n - 1)

    for p in (up, dn, mirror, partner):
        greet(p)
    for d in range(1, ny):
        greet(ypeer(d)[1])
    for d in range(1, nz):
        greet(zpeer(d)[1])

    nbload.wait()
    nbs = [[nbm[s, f] for s in range(4)] for f in range(6)]
    x = iota((48, 160), 0)
    yy = iota((48, 160), 1)
    xs = x & 15
    xsd = jnp.where(xs < 8, 1, 3)
    xnb = jnp.full((48, 160), -1, jnp.int32)
    for f in range(6):
        xnb = jnp.where(xs == f, nbs[f][1], xnb)
        xnb = jnp.where(xs == 8 + f, nbs[f][3], xnb)
    ym = jnp.where(yy >= 48, yy - 48, yy)
    ysd = jnp.where((ym & 15) < 8, 1, 3)
    yz = (yy - 96) & 31
    isz = yy >= 96
    yg = jnp.where(isz, yz & 7, ym & 7)
    yt = jnp.where(isz, jnp.where(yy >= 128, 2, 0), ysd)
    yfield = jnp.where(isz, yz >> 3, ym >> 4)
    way = jnp.where(isz, 1, jnp.where(yy >= 48, jnp.where(xsd == ysd, 1, 0), jnp.where(xsd == ysd, 0, 1)))
    sel[...] = onehot((xnb == 4 * yg + yt) & ((x >> 4) == yfield) & (yg < 6) & (way == 1))
    x = iota((64, 48), 0)
    yy = iota((64, 48), 1)
    xnb = jnp.full((64, 48), -1, jnp.int32)
    for f in range(6):
        xnb = jnp.where((x & 7) == f, jnp.where(x < 32, nbs[f][0], nbs[f][2]), xnb)
    yt = jnp.where((yy & 15) < 8, 1, 3)
    selh[...] = onehot((xnb == 4 * (yy & 7) + yt) & (((x & 31) >> 3) == (yy >> 4)) & ((yy & 7) < 6))

    def chosen(s, code, offset):
        t = code & 3
        flipped = (s < 2) == (t < 2)
        along = jnp.where(flipped, 1 - offset, offset - 1)
        row_tap = jnp.where(t == 0, 0, jnp.where(t == 2, 2, 1 - along))
        col_tap = jnp.where(t == 1, 2, jnp.where(t == 3, 0, 1 - along))
        return 3 * row_tap + col_tap

    xs = iota((SIDES, C), 0)
    code = jnp.full((SIDES, C), 0, jnp.int32)
    for f in range(6):
        code = jnp.where(xs == f, nbs[f][1], code)
        code = jnp.where(xs == 8 + f, nbs[f][3], code)
    side_taps = [chosen(jnp.where(xs < 8, 1, 3), code, o) for o in range(3)]

    hub_side = jnp.where(is0, 0, 2)
    hub_nb = [jnp.where(is0, nbs[f][0], nbs[f][2]) for f in range(6)]
    hub_flip = [((hub_side < 2) == ((code_f & 3) < 2)).astype(jnp.int32) for code_f in hub_nb]

    def per_face(face, values, start):
        result = jnp.full(face.shape, start, jnp.int32)
        for f in range(6):
            result = jnp.where(face == f, values[f], result)
        return result

    @pl.when(ishub)
    def _():
        a = iota((8 * F, cells), 0)
        b = iota((8 * F, cells), 1)
        g = a & 7
        pos = a >> 3
        target = g * F + jnp.where(per_face(g, hub_flip, 0) == 1, F - 1 - pos, pos)
        amat[...] = onehot((b == target) & (g < 6))

    def edges(ph, i):
        row = rb[ph, i, 1].astype(F32)
        zero = jnp.zeros((2, C), F32)
        return jnp.concatenate([row[:, F - 1], zero, row[:, 0], zero], axis=0).astype(BF)

    def prepare(ph):
        for i in range(3):
            ebuf[ph, 16 * i : 16 * i + 16] = edges(ph, i)
        hm[ph] = dot(selh[...], ebuf[ph, 0:48]).astype(BF)

        @pl.when(ishub)
        def _():
            parts = []
            for i in range(3):
                parts.append(dot(amat[...], rb[ph, i, 1].reshape(cells, C)).reshape(F, 8, C))
            parts.append(jnp.zeros((F, 8, C), F32))
            zs[ph] = jnp.concatenate(parts, axis=1).astype(BF)

        @pl.when(is0)
        def _():
            rx[ph, 0] = hm[ph, 0:32]
            ebuf[ph, 96:128] = zs[ph, 0]

        @pl.when(is1)
        def _():
            rx[ph, n - 1] = hm[ph, 32:64]
            ebuf[ph, 128:160] = zs[ph, n - 1]

    def e_copy(ph):
        return rcopy(ebuf.at[ph, pl.ds(0, 48)], ebuf.at[ph, pl.ds(48, 48)], e_s.at[ph], e_r.at[ph], mirror)

    def hm_copy(ph, h):
        return rcopy(
            hm.at[ph, pl.ds(32 * h, 32)],
            rx.at[ph, r],
            hm_s.at[ph, h],
            rx_r.at[ph],
            (n - 1) * h,
        )

    def z_copy(ph, h, p):
        return rcopy(zs.at[ph, p], ebuf.at[ph, pl.ds(96 + 32 * h, 32)], z_s.at[ph], z_r.at[ph, h], p)

    def row_beside(ph, i, out):
        slot = slot_out if out else slot_in
        return rcopy(rb.at[ph, i, 1], rb.at[ph, i, slot], bulk_s.at[ph, 0], bulk_r.at[ph, i, 0], beside)

    def row_beyond(ph, i, out):
        slot = slot_in if out else slot_out
        return rcopy(rb.at[ph, i, 1], rb.at[ph, i, slot], bulk_s.at[ph, 1], bulk_r.at[ph, i, 1], beyond)

    def row_inward(ph, i):
        return rcopy(rb.at[ph, i, slot_in], rb.at[ph, i, slot_out], bulk_s.at[ph, 2], bulk_r.at[ph, i, 1], partner)

    def send_rows(ph, fields=(0, 1, 2)):
        for i in fields:
            row_beside(ph, i, True).start()

            @pl.when(outer)
            def _():
                row_beyond(ph, i, True).start()

    def hand_row(ph, i):
        @pl.when(outer)
        def _():
            row_beside(ph, i, False).wait_recv()
            row_inward(ph, i).start()

    def receive_row(ph, i):
        @pl.when(jnp.logical_not(outer))
        def _():
            row_beside(ph, i, False).wait_recv()

        row_beyond(ph, i, False).wait_recv()

    def finish_rows(ph):
        three = rb.at[ph, :, 1]

        def sent(kind):
            rcopy(three, three, bulk_s.at[ph, kind], bulk_r.at[ph, 0, 0], beside).wait_send()

        sent(0)

        @pl.when(outer)
        def _():
            sent(1)
            sent(2)

    def mt_copy(ph, way):
        return rcopy(
            mt.at[ph, 1],
            mt.at[ph, 2 if way == 0 else 0],
            mt_s.at[ph, way],
            mt_r.at[ph, way],
            up if way == 0 else dn,
        )

    def hub_loop(step):
        def body(i, carry):
            step(lax.rem(r + i, n))
            return carry

        lax.fori_loop(1, n, body, 0)

    def send(ph):
        for h, here in ((0, is0), (1, is1)):

            @pl.when(here)
            def _():
                hub_loop(lambda p: z_copy(ph, h, p).start())

            @pl.when(jnp.logical_not(here))
            def _():
                hm_copy(ph, h).start()

        e_copy(ph).start()

    def margins(ph):
        e_copy(ph).wait()
        for h, here in ((0, is0), (1, is1)):

            @pl.when(jnp.logical_not(here))
            def _():
                z_copy(ph, h, 0).wait_recv()

        mt[ph, 1] = dot(sel[...], ebuf[ph]).astype(BF)
        for way in range(2):
            mt_copy(ph, way).start()

    def hub_wait(ph):
        @pl.when(ishub)
        def _():
            start = jnp.where(is0, 1, 0)
            rcopy(zs.at[ph, pl.ds(0, n - 1)], rx.at[ph, pl.ds(start, n - 1)], z_s.at[ph], rx_r.at[ph], mirror).wait_recv()

    def hub_row(ph, i, spreads):
        @pl.when(ishub)
        def _():
            slot = jnp.where(is0, 0, 2)
            piece = rx[ph].astype(F32)[:, 8 * i : 8 * i + 8].reshape(8 * F, C).astype(BF)
            row = dot(bmat[...], piece)
            row = row + dot(c0mat[...], rb[ph, i, 1].reshape(cells, C))
            row = row + dot(c2mat[...], rb[ph, i, slot].reshape(cells, C))
            row = row.astype(BF).reshape(6, F, C)
            if spreads:
                mb[ph, i] = row
                rb[ph, i, slot] = jnp.zeros((6, F, C), BF)
            else:
                rb[ph, i, slot] = row

    def receive_margins(ph):
        for way in range(2):
            mt_copy(ph, way).wait()

        @pl.when(is0)
        def _():
            mt[ph, 0] = jnp.zeros((48, C), BF)

        @pl.when(is1)
        def _():
            mt[ph, 2] = jnp.zeros((48, C), BF)

    def finish_sends(ph):
        for h, here in ((0, is0), (1, is1)):

            @pl.when(here)
            def _():
                rcopy(zs.at[ph, pl.ds(0, n - 1)], rx.at[ph, pl.ds(0, n - 1)], z_s.at[ph], rx_r.at[ph], mirror).wait_send()

            @pl.when(jnp.logical_not(here))
            def _():
                hm_copy(ph, h).wait_send()

    def row_taps(ph, i, a, dst, spreads, scale):
        padz[:, 8 : 8 + F] = rb[ph, i, a].astype(F32) * scale
        for b in range(3):
            k = 3 * a + b
            k = 8 - k if spreads else k
            dst[0:cells, k * C : k * C + C] = padz[:, 7 + b : 7 + b + F].reshape(cells, C).astype(BF)

    def forward_sides(ph, i, dst):
        for a in range(3):
            line = mt[ph, a, 16 * i : 16 * i + 16].astype(F32)
            zero = jnp.zeros((SIDES, C), F32)
            for b, part in enumerate((jnp.where(xs < 8, zero, line), zero, jnp.where(xs < 8, line, zero))):
                k = 3 * a + b
                dst[cells : cells + SIDES, k * C : k * C + C] = part.astype(BF)

    def spread_sides(ph, i, dst, scale):
        lines = [mt[ph, o, 16 * i : 16 * i + 16].astype(F32) * scale for o in range(3)]
        for k in range(9):
            total = jnp.zeros((SIDES, C), F32)
            for o in range(3):
                total = jnp.where(side_taps[o] == k, lines[o], total)
            dst[cells : cells + SIDES, k * C : k * C + C] = total.astype(BF)

    def hub_taps(ph, i, extra, scale):
        padz[:, 8 : 8 + F] = mb[ph, i].astype(F32) * scale
        for f in range(6):
            picks = [chosen(hub_side, hub_nb[f], o) for o in range(3)]
            shifted = [padz[f, 7 + o : 7 + o + F] for o in range(3)]
            for k in range(9):
                total = jnp.zeros((F, C), F32)
                for o in range(3):
                    total = jnp.where(picks[o] == k, shifted[o], total)
                extra[f * F : f * F + F, k * C : k * C + C] = total.astype(BF)

    def add_sides(ref, lanes, side):
        for f in range(6):
            ref[f, F - 1 : F, lanes] += side[f : f + 1]
            ref[f, 0:1, lanes] += side[8 + f : 9 + f]

    def main_spread(ph, i, dst, extra, weights, scale, ref, lanes):
        width = lanes.stop - lanes.start
        ref[:, :, lanes] = dot(dst[0:cells], weights).reshape(6, F, width)

        @pl.when(ishub)
        def _():
            hub_taps(ph, i, extra, scale)
            ref[:, :, lanes] += dot(extra[...], weights).reshape(6, F, width)

    for cp in loads:
        cp.wait()
    prepare(0)
    base = 4 + (ny - 1) + (nz - 1)
    pl.semaphore_wait(barrier, base + 2 + jnp.where(ishub, n - 2, 0))
    send(0)
    send_rows(0)

    padz[...] = jnp.zeros(padz.shape, F32)
    for cp in wloads:
        cp.wait()
    wf1[:, 0:C] = wraw[0]
    wf1[:, C : 2 * C] = wraw[1]
    for k in range(9):
        rows = slice(k * C, k * C + C)
        ws1[rows, 0:C] = wraw[0, rows].astype(F32).T.astype(BF)
        ws1[rows, C : 2 * C] = wraw[1, rows].astype(F32).T.astype(BF)
        ws2[rows, 0:C] = wraw[2, rows].astype(F32).T.astype(BF)
        ws2[rows, C : 2 * C] = wraw[3, rows].astype(F32).T.astype(BF)

    @pl.when(ishub)
    def _():
        a = iota((cells, 8 * F), 0)
        b = iota((cells, 8 * F), 1)
        face = lax.div(a, F)
        pos = a - face * F
        pos = jnp.where(per_face(face, hub_flip, 0) == 1, F - 1 - pos, pos)
        column = per_face(face, [code_f & 1 for code_f in hub_nb], 0)
        bmat[...] = onehot((b == 8 * pos + face) & (column == 1))
        a = iota((cells, cells), 0)
        b = iota((cells, cells), 1)
        face = lax.div(a, F)
        pos = a - face * F
        code_a = per_face(face, hub_nb, 0)
        other = (code_a >> 2) * F
        c0mat[...] = onehot(((code_a & 3) == hub_side) & (b == other + F - 1 - pos))
        c2mat[...] = onehot(((code_a & 3) == 2 - hub_side) & (b == other + pos))

    inputs = ((0, tu, False, 1.0), (1, tv, False, 1.0), (2, ts, True, 0.5))
    for i, dst, spreads, scale in inputs:
        row_taps(0, i, 1, dst, spreads, scale)
    both = slice(0, 2 * C)
    left = slice(0, C)
    right = slice(C, 2 * C)

    def field_rows(i):
        receive_row(0, i)
        _, dst, spreads, scale = inputs[i]
        hub_row(0, i, spreads)
        row_taps(0, i, 0, dst, spreads, scale)
        row_taps(0, i, 2, dst, spreads, scale)

    hand_row(0, 0)
    margins(0)
    hand_row(0, 1)
    hub_wait(0)
    field_rows(0)
    front[...] = dot(tu[0:cells], wf1[...]).reshape(6, F, 2 * C)
    hand_row(0, 2)
    field_rows(1)
    front[:, :, right] += dot(tv[0:cells], wraw[0]).reshape(6, F, C)
    field_rows(2)
    main_spread(0, 2, ts, tx, ws2[...], 0.5, field, both)
    receive_margins(0)
    forward_sides(0, 0, tu)
    forward_sides(0, 1, tv)
    spread_sides(0, 2, ts, 0.5)
    side = dot(tu[cells:], wf1[...])
    more = dot(tv[cells:], wraw[0])
    add_sides(front, both, side)
    add_sides(front, right, more)
    add_sides(field, both, dot(ts[cells:], ws2[...]))
    squash = jnp.tanh(front[:, :, left])
    derivative = 1.0 - squash * squash
    hidden_tangent = front[:, :, right]
    act_tangent = (derivative * hidden_tangent).astype(BF)
    backward = field[:, :, left]
    scaled = derivative * backward
    rb[1, 0, 1] = squash.astype(BF)
    rb[1, 1, 1] = scaled.astype(BF)
    rb[1, 2, 1] = (derivative * field[:, :, right] - 2.0 * squash * scaled * hidden_tangent).astype(BF)
    aext[0:cells, right] = act_tangent.reshape(cells, C)

    send_rows(1, (0,))

    aext[0:cells, left] = rb[1, 0, 1].reshape(cells, C)
    aext[cells:, left] = edges(1, 0)
    zero = jnp.zeros((2, C), F32)
    wide = act_tangent.astype(F32)
    aext[cells:, right] = jnp.concatenate([wide[:, F - 1], zero, wide[:, 0], zero], axis=0).astype(BF)
    for i, lanes in ((1, left), (2, right)):
        pext[0:cells, lanes] = rb[1, i, 1].reshape(cells, C)
        pext[cells:, lanes] = edges(1, i)
    first = dot_t(tu[...], pext[...])
    gsum[0:K9] = first[:, 0:C]
    gsum[2 * K9 : 3 * K9] = first[:, C : 2 * C] + dot_t(tv[...], pext[:, left])
    second = dot_t(aext[...], ts[...])
    for k in range(9):
        gsum[K9 + k * C : K9 + k * C + C] = second[0:C, k * C : k * C + C]
        gsum[3 * K9 + k * C : 3 * K9 + k * C + C] = second[C : 2 * C, k * C : k * C + C]

    @pl.when(ishub)
    def _():
        more = dot_t(aext[0:cells], tx[...])
        for k in range(9):
            gsum[K9 + k * C : K9 + k * C + C] += more[0:C, k * C : k * C + C]
            gsum[3 * K9 + k * C : 3 * K9 + k * C + C] += more[C : 2 * C, k * C : k * C + C]

    outs = [pltpu.make_async_copy(res.at[i], ref, osem.at[i]) for i, ref in enumerate((next_ref, adj_ref, adt_ref))]

    shard, p0, p1, qn = split_rows(ny, nz)
    qoff = p0 + p1 + qn * core
    qother = p0 + p1 + qn * (1 - core)
    def by_core(fn):
        @pl.when(core == 0)
        def _():
            fn(0, p0, p0, p1)

        @pl.when(core == 1)
        def _():
            fn(p0, p1, 0, p0)

    def ar(name, src, dst, p, extra=None):
        at = STEPS.index(name)
        return rcopy(src, dst, ar_s.at[at], ar_r.at[at if extra is None else len(STEPS) + extra], p)

    def sent(name, src):
        ar(name, src, src, partner).wait_send()

    def arrived(name, dst):
        ar(name, dst, dst, partner).wait_recv()

    ypeers = [ypeer(d) for d in range(1, ny)]
    zpeers = [zpeer(d) for d in range(1, nz)]
    whole = gsum[...].reshape(ny, nz, shard, C)
    gs[...] = whole.astype(BF)

    def core_p(off, size, ooff, osize):
        return ar("cp", gs.at[:, :, pl.ds(ooff, osize)], gr.at[:, :, pl.ds(ooff, osize)], partner)

    def core_p_in(off, size, ooff, osize):
        return ar("cp", gs.at[:, :, pl.ds(off, size)], gr.at[:, :, pl.ds(off, size)], partner)

    def core_q(o):
        return ar("cq", gs.at[:, :, pl.ds(o, qn)], gr.at[:, :, pl.ds(o, qn)], partner)

    core_q(qother).start()
    by_core(lambda *a: core_p(*a).start())

    def q1(d):
        q, p = zpeers[d]
        return ar("q1", qs.at[:, q], qr.at[z], p)

    def p1_copy(d, size):
        q, p = ypeers[d]
        return ar("p1", ps.at[q, :, pl.ds(0, size)], pr.at[y, :, pl.ds(0, size)], p)

    core_q(qother).wait_send()
    core_q(qoff).wait_recv()

    def stage(qo):
        part = gsum[...].reshape(ny, nz, shard, C)[:, :, qo : qo + qn] + gr[:, :, qo : qo + qn].astype(F32)
        qf[...] = part
        qs[...] = part.astype(BF)

    by_core(lambda off, size, ooff, osize: stage(p0 + p1 if off == 0 else p0 + p1 + qn))
    for d in range(nz - 1):
        q1(d).start()

    def stage(off, size, ooff, osize):
        core_p(off, size, ooff, osize).wait_send()
        core_p_in(off, size, ooff, osize).wait_recv()
        part = gsum[...].reshape(ny, nz, shard, C)[:, :, off : off + size] + gr[:, :, off : off + size].astype(F32)
        pf[:, :, 0:size] = part
        ps[:, :, 0:size] = part.astype(BF)
        for d in range(ny - 1):
            p1_copy(d, size).start()

    by_core(stage)
    prepare(1)
    send(1)
    send_rows(1, (1, 2))

    def p2_copy(d, size):
        q, p = zpeers[d]
        return ar("p2", pz.at[q, pl.ds(0, size)], pzr.at[z, pl.ds(0, size)], p)

    def stage(off, size, ooff, osize):
        arrived("p1", pr.at[pl.ds(0, ny - 1), :, pl.ds(0, size)])
        part = pf[y, :, 0:size]
        for q, p in ypeers:
            part = part + pr[q, :, 0:size].astype(F32)
        pzf[:, 0:size] = part
        pz[:, 0:size] = part.astype(BF)
        for d in range(nz - 1):
            p2_copy(d, size).start()

    by_core(stage)

    def q2(d):
        q, p = ypeers[d]
        return ar("q2", qy.at[q], qyr.at[y], p)

    arrived("q1", qr.at[pl.ds(0, nz - 1)])
    part = qf[:, z]
    for q, p in zpeers:
        part = part + qr[q].astype(F32)
    qyf[...] = part
    qy[...] = part.astype(BF)
    for d in range(ny - 1):
        q2(d).start()

    scale = 1.0 / F

    def p3(d, size, off):
        q, p = zpeers[d]
        return ar("p3", fin_p.at[pl.ds(0, size)], out_ref.at[y, z, pl.ds(off, size)], p)

    def own_p(size, off):
        return pltpu.make_async_copy(fin_p.at[pl.ds(0, size)], out_ref.at[y, z, pl.ds(off, size)], osem.at[3])

    own_q = pltpu.make_async_copy(fin_q, out_ref.at[y, z, pl.ds(qoff, qn)], osem.at[4])

    def stage(off, size, ooff, osize):
        arrived("p2", pzr.at[pl.ds(0, nz - 1), pl.ds(0, size)])
        part = pzf[z, 0:size]
        for q, p in zpeers:
            part = part + pzr[q, 0:size].astype(F32)
        fin_p[0:size] = (part * scale).astype(BF)
        own_p(size, off).start()
        for d in range(nz - 1):
            p3(d, size, off).start()

    by_core(stage)

    def q3(d):
        q, p = ypeers[d]
        return ar("q3", fin_q, out_ref.at[y, z, pl.ds(qoff, qn)], p)

    arrived("q2", qyr.at[pl.ds(0, ny - 1)])
    part = qyf[y]
    for q, p in ypeers:
        part = part + qyr[q].astype(F32)
    fin_q[...] = (part * scale).astype(BF)
    own_q.start()
    for d in range(ny - 1):
        q3(d).start()

    for i in range(3):
        hand_row(1, i)
    margins(1)
    hub_wait(1)
    for i in range(3):
        receive_row(1, i)
        hub_row(1, i, i > 0)
    for a in range(3):
        row_taps(1, 0, a, tu, False, 1.0)
    field[:, :, left] = dot(tu[0:cells], wraw[2]).reshape(6, F, C)

    def p4(d, size, off, out):
        q, p = ypeers[d]
        qq = y if out else q
        ref = out_ref.at[qq, :, pl.ds(off, size)]
        return ar("p4", ref, ref, p, qq)

    def cpy_p(q, size, off):
        ref = out_ref.at[q, :, pl.ds(off, size)]
        return ar("c4", ref, ref, partner)

    def stage(off, size, ooff, osize):
        arrived("p3", out_ref.at[y, pl.ds(0, nz - 1), pl.ds(off, size)])
        own_p(size, off).wait()
        for d in range(ny - 1):
            p4(d, size, off, True).start()
        cpy_p(y, size, off).start()

    by_core(stage)

    def q4(d, out):
        q, p = zpeers[d]
        qq = z if out else q
        ref = out_ref.at[:, qq, pl.ds(qoff, qn)]
        return ar("q4", ref, ref, p, ny + qq)

    def cpy_q(q, o):
        ref = out_ref.at[:, q, pl.ds(o, qn)]
        return ar("d4", ref, ref, partner)

    arrived("q3", out_ref.at[pl.ds(0, ny - 1), z, pl.ds(qoff, qn)])
    own_q.wait()
    for d in range(nz - 1):
        q4(d, True).start()
    cpy_q(z, qoff).start()

    receive_margins(1)
    forward_sides(1, 0, tu)
    add_sides(field, left, dot(tu[cells:], wraw[2]))
    res[0] = (rb[0, 0, 1].astype(F32) + 0.5 * field[:, :, left]).astype(BF)
    outs[0].start()

    def adjoint_of(i, dst, weights, ref, lanes):
        for a in range(3):
            row_taps(1, i, a, dst, True, 1.0)
        spread_sides(1, i, dst, 1.0)
        main_spread(1, i, dst, tx, weights, 1.0, ref, lanes)
        add_sides(ref, lanes, dot(dst[cells:], weights))

    adjoint_of(1, ts, ws1[...], front, both)
    res[1] = (rb[0, 2, 1].astype(F32) + front[:, :, left]).astype(BF)
    outs[1].start()

    adjoint_of(2, ts, ws1[:, 0:C], field, left)
    res[2] = (front[:, :, right] + field[:, :, left]).astype(BF)
    outs[2].start()

    def stage(off, size, ooff, osize):
        for d in range(ny - 1):
            p4(d, size, off, False).wait_recv()
            cpy_p(ypeers[d][0], size, off).start()

    by_core(stage)
    for d in range(nz - 1):
        q4(d, False).wait_recv()
        cpy_q(zpeers[d][0], qoff).start()

    def stage(off, size, ooff, osize):
        sent("p1", pr.at[pl.ds(0, ny - 1), :, pl.ds(0, size)])
        sent("p2", pzr.at[pl.ds(0, nz - 1), pl.ds(0, size)])
        sent("p3", out_ref.at[y, pl.ds(0, nz - 1), pl.ds(off, size)])
        sent("p4", out_ref.at[pl.ds(0, ny - 1), :, pl.ds(off, size)])
        sent("c4", out_ref.at[:, :, pl.ds(off, size)])
        arrived("c4", out_ref.at[:, :, pl.ds(ooff, osize)])

    by_core(stage)
    sent("q1", qr.at[pl.ds(0, nz - 1)])
    sent("q2", qyr.at[pl.ds(0, ny - 1)])
    sent("q3", out_ref.at[pl.ds(0, ny - 1), z, pl.ds(qoff, qn)])
    sent("q4", out_ref.at[:, pl.ds(0, nz - 1), pl.ds(qoff, qn)])
    sent("d4", out_ref.at[:, :, pl.ds(qoff, qn)])
    arrived("d4", out_ref.at[:, :, pl.ds(qother, qn)])
    for cp in outs:
        cp.wait()
    for ph in range(2):
        finish_sends(ph)
        finish_rows(ph)


STEPS = ("cp", "cq", "q1", "p1", "p2", "q2", "p3", "q3", "p4", "c4", "q4", "d4")


def split_rows(ny, nz):
    tiles = 4 * K9 // (16 * ny * nz)
    qn = 2 * tiles // 9
    p1 = (tiles - 2 * qn) // 2
    return 16 * tiles, 16 * (tiles - 2 * qn - p1), 16 * p1, 16 * qn


CHUNKS = 8


def finish(n_ref, a_ref, t_ref, g_ref, n_out, a_out, t_out, w_out, h_out, packed, wide, held, in_sem, out_sem, row_in, row_out):
    size = packed.shape[1]
    row_ins = [pltpu.make_async_copy(src, held.at[i], row_in.at[i]) for i, src in enumerate((n_ref, a_ref, t_ref))]
    row_outs = [pltpu.make_async_copy(held.at[i], dst, row_out.at[i]) for i, dst in enumerate((n_out, a_out, t_out))]
    half = CHUNKS // 2
    ins = [pltpu.make_async_copy(g_ref.at[pl.ds(i * size, size)], packed.at[i], in_sem.at[i]) for i in range(CHUNKS)]
    outs = [
        pltpu.make_async_copy(wide.at[i], (w_out, h_out)[i // half].at[pl.ds(i % half * size, size)], out_sem.at[i])
        for i in range(CHUNKS)
    ]
    for cp in ins + row_ins:
        cp.start()
    for i in range(CHUNKS):
        ins[i].wait()
        wide[i] = packed[i].astype(F32)
        outs[i].start()
    for i in range(3):
        row_ins[i].wait()
        row_outs[i].start()
    for cp in outs + row_outs:
        cp.wait()


def on_device(n, ny, nz, u, v, c, w1, w2, t1, t2, nb):
    F = n
    cells = 6 * F
    shard, p0, p1, qn = split_rows(ny, nz)
    u, v, c = (a.reshape(6, F, C) for a in (u, v, c))
    w1, w2, t1, t2 = (a.reshape(K9, C) for a in (w1, w2, t1, t2))
    vm = pltpu.VMEM
    dma = pltpu.SemaphoreType.DMA
    anywhere = pl.BlockSpec(memory_space=pl.ANY)
    inside = pl.BlockSpec(memory_space=pltpu.VMEM)
    row = jax.ShapeDtypeStruct((6, F, C), BF)
    nxt, adj, adt, out = pl.pallas_call(
        functools.partial(kernel, n, ny, nz),
        out_shape=(row, row, row, jax.ShapeDtypeStruct((ny, nz, shard, C), BF)),
        in_specs=[anywhere] * 8,
        out_specs=(anywhere,) * 4,
        scratch_shapes=[
            vm((2, 3, 3, 6, F, C), BF),
            vm((2, 3, 6, F, C), BF),
            vm((2, 160, C), BF),
            vm((2, 64, C), BF),
            vm((2, F, 32, C), BF),
            vm((2, F, 32, C), BF),
            vm((2, 3, 48, C), BF),
            vm((48, 160), BF),
            vm((64, 48), BF),
            vm((8 * F, cells), BF),
            vm((cells, 8 * F), BF),
            vm((cells, cells), BF),
            vm((cells, cells), BF),
            vm((4, K9, C), BF),
            vm((K9, 2 * C), BF),
            vm((K9, 2 * C), BF),
            vm((K9, 2 * C), BF),
            vm((6, F + 16, C), F32),
            vm((cells + SIDES, K9), BF),
            vm((cells + SIDES, K9), BF),
            vm((cells + SIDES, K9), BF),
            vm((cells, K9), BF),
            vm((cells + SIDES, 2 * C), BF),
            vm((cells + SIDES, 2 * C), BF),
            vm((6, F, 2 * C), F32),
            vm((6, F, 2 * C), F32),
            vm((4 * K9, C), F32),
            vm((ny, nz, shard, C), BF),
            vm((ny, nz, shard, C), BF),
            vm((ny, nz, p0, C), F32),
            vm((ny, nz, p0, C), BF),
            vm((ny, nz, p0, C), BF),
            vm((ny, nz, qn, C), F32),
            vm((ny, nz, qn, C), BF),
            vm((nz, ny, qn, C), BF),
            vm((nz, p0, C), BF),
            vm((nz, p0, C), F32),
            vm((nz, p0, C), BF),
            vm((ny, qn, C), BF),
            vm((ny, qn, C), F32),
            vm((ny, qn, C), BF),
            pltpu.SMEM((4, 6), jnp.int32),
            vm((3, 6, F, C), BF),
            vm((p0, C), BF),
            vm((qn, C), BF),
            dma((5,)),
            dma((8,)),
            dma((2, 3)),
            dma((2, 3, 2)),
            dma((2,)),
            dma((2,)),
            dma((2, 2)),
            dma((2,)),
            dma((2,)),
            dma((2, 2)),
            dma((2, 2)),
            dma((2, 2)),
            dma((len(STEPS),)),
            dma((len(STEPS) + ny + nz,)),
        ],
        compiler_params=pltpu.CompilerParams(
            collective_id=0, has_side_effects=True, vmem_limit_bytes=56 * 2**20
        ),
    )(u, v, c, w1, w2, t1, t2, nb.T)
    half = 2 * K9
    grad = jax.ShapeDtypeStruct((half, C), F32)
    nxt, adj, adt, wg, hp = pl.pallas_call(
        finish,
        out_shape=(row, row, row, grad, grad),
        in_specs=[anywhere] * 4,
        out_specs=(anywhere,) * 5,
        scratch_shapes=[vm((CHUNKS, 2 * half // CHUNKS, C), BF), vm((CHUNKS, 2 * half // CHUNKS, C), F32), vm((3, 6, F, C), BF), dma((CHUNKS,)), dma((CHUNKS,)), dma((3,)), dma((3,))],
        compiler_params=pltpu.CompilerParams(vmem_limit_bytes=56 * 2**20),
    )(nxt, adj, adt, out.reshape(2 * half, C))
    shape4 = (2, 9, C, C)
    shape = (6, 1, F, C)
    return nxt.reshape(shape), adj.reshape(shape), adt.reshape(shape), wg.reshape(shape4), hp.reshape(shape4)


def solution(mesh):
    n = mesh.shape["tile"] * mesh.shape["sub"]
    nz = 8 if n == 64 else 2
    ny = n // (2 * nz)
    field = P("rep", ("tile", "sub"), None, None)
    grads = P("rep", None, None, None)
    return jax.shard_map(
        functools.partial(on_device, n, ny, nz),
        mesh=mesh,
        in_specs=(field, field, field, P(), P(), P(), P(), P()),
        out_specs=(field, field, field, grads, grads),
        check_vma=False,
    )
```

```python
import functools

import jax
import jax.numpy as jnp
from jax import lax
from jax.experimental import pallas as pl
from jax.experimental.pallas import tpu as pltpu
from jax.sharding import PartitionSpec as P

MESH = pl.DeviceIdType.MESH
BF = jnp.bfloat16
F32 = jnp.float32
C = 128
K9 = 9 * C
SIDES = 16


def dot(a, b):
    return jnp.dot(a, b, preferred_element_type=F32)


def dot_t(a, b):
    return lax.dot_general(a, b, (((0,), (0,)), ((), ())), preferred_element_type=F32)


def iota(shape, dim):
    return lax.broadcasted_iota(jnp.int32, shape, dim)


def onehot(mask):
    return jnp.where(mask, 1.0, 0.0).astype(BF)


def kernel(
    n,
    ny,
    nz,
    u_ref,
    v_ref,
    c_ref,
    w1_ref,
    w2_ref,
    t1_ref,
    t2_ref,
    nb_ref,
    next_ref,
    adj_ref,
    adt_ref,
    out_ref,
    rb,
    mb,
    ebuf,
    hm,
    zs,
    rx,
    mt,
    sel,
    selh,
    amat,
    bmat,
    c0mat,
    c2mat,
    wraw,
    wf1,
    ws1,
    ws2,
    padz,
    tu,
    tv,
    ts,
    tx,
    aext,
    pext,
    front,
    field,
    gsum,
    gs,
    gr,
    pf,
    ps,
    pr,
    qf,
    qs,
    qr,
    pz,
    pzf,
    pzr,
    qy,
    qyf,
    qyr,
    nbm,
    res,
    fin_p,
    fin_q,
    osem,
    lsem,
    bulk_s,
    bulk_r,
    e_s,
    e_r,
    hm_s,
    rx_r,
    z_s,
    z_r,
    mt_s,
    mt_r,
    ar_s,
    ar_r,
):
    F = n
    cells = 6 * F
    rep = lax.axis_index("rep")
    r = lax.axis_index("tile") * 2 + lax.axis_index("sub")
    core = lax.rem(lax.div(r, 2), 2)
    z = lax.rem(lax.div(r, 4), nz)
    yhi = lax.div(r, 4 * nz)
    ylo = lax.rem(r, 2)
    y = yhi * 2 + ylo

    def dev(p):
        return (lax.div(p, 2), lax.rem(p, 2), rep)

    def make(hi, zc, co, lo):
        return ((hi * nz + zc) * 2 + co) * 2 + lo

    up = lax.rem(r + n - 1, n)
    dn = lax.rem(r + 1, n)
    mirror = n - 1 - r
    odd = lax.rem(r, 2)
    beside = r + 1 - 2 * odd
    beyond = lax.rem(r + n - 1 + 2 * odd, n)
    outer = jnp.logical_or(lax.rem(r, 4) == 0, lax.rem(r, 4) == 3)
    slot_in = 2 - 2 * odd
    slot_out = 2 * odd
    partner = make(yhi, z, 1 - core, ylo)

    def ypeer(d):
        q = lax.rem(y + d, ny)
        return q, make(lax.div(q, 2), z, core, lax.rem(q, 2))

    def zpeer(d):
        q = lax.rem(z + d, nz)
        return q, make(yhi, q, core, ylo)

    is0 = r == 0
    is1 = r == n - 1
    ishub = jnp.logical_or(is0, is1)

    def rcopy(src, dst, ssem, rsem, p):
        return pltpu.make_async_remote_copy(
            src_ref=src,
            dst_ref=dst,
            send_sem=ssem,
            recv_sem=rsem,
            device_id=dev(p),
            device_id_type=MESH,
        )

    nbload = pltpu.make_async_copy(nb_ref, nbm, lsem.at[7])
    nbload.start()
    loads = [pltpu.make_async_copy(ref, rb.at[0, i, 1], lsem.at[i]) for i, ref in enumerate((u_ref, v_ref, c_ref))]
    wloads = [pltpu.make_async_copy(ref, wraw.at[i], lsem.at[3 + i]) for i, ref in enumerate((w1_ref, t1_ref, w2_ref, t2_ref))]
    for cp in loads + wloads:
        cp.start()

    barrier = pltpu.get_barrier_semaphore()

    def greet(p):
        pl.semaphore_signal(barrier, inc=1, device_id=dev(p), device_id_type=MESH)

    @pl.when(ishub)
    def _():
        def body(i, carry):
            greet(lax.rem(r + i, n))
            return carry

        lax.fori_loop(1, n, body, 0)

    @pl.when(r != 0)
    def _():
        greet(0)

    @pl.when(r != n - 1)
    def _():
        greet(n - 1)

    for p in (up, dn, mirror, partner):
        greet(p)
    for d in range(1, ny):
        greet(ypeer(d)[1])
    for d in range(1, nz):
        greet(zpeer(d)[1])

    nbload.wait()
    nbs = [[nbm[s, f] for s in range(4)] for f in range(6)]
    x = iota((48, 160), 0)
    yy = iota((48, 160), 1)
    xs = x & 15
    xsd = jnp.where(xs < 8, 1, 3)
    xnb = jnp.full((48, 160), -1, jnp.int32)
    for f in range(6):
        xnb = jnp.where(xs == f, nbs[f][1], xnb)
        xnb = jnp.where(xs == 8 + f, nbs[f][3], xnb)
    ym = jnp.where(yy >= 48, yy - 48, yy)
    ysd = jnp.where((ym & 15) < 8, 1, 3)
    yz = (yy - 96) & 31
    isz = yy >= 96
    yg = jnp.where(isz, yz & 7, ym & 7)
    yt = jnp.where(isz, jnp.where(yy >= 128, 2, 0), ysd)
    yfield = jnp.where(isz, yz >> 3, ym >> 4)
    way = jnp.where(isz, 1, jnp.where(yy >= 48, jnp.where(xsd == ysd, 1, 0), jnp.where(xsd == ysd, 0, 1)))
    sel[...] = onehot((xnb == 4 * yg + yt) & ((x >> 4) == yfield) & (yg < 6) & (way == 1))
    x = iota((64, 48), 0)
    yy = iota((64, 48), 1)
    xnb = jnp.full((64, 48), -1, jnp.int32)
    for f in range(6):
        xnb = jnp.where((x & 7) == f, jnp.where(x < 32, nbs[f][0], nbs[f][2]), xnb)
    yt = jnp.where((yy & 15) < 8, 1, 3)
    selh[...] = onehot((xnb == 4 * (yy & 7) + yt) & (((x & 31) >> 3) == (yy >> 4)) & ((yy & 7) < 6))

    def chosen(s, code, offset):
        t = code & 3
        flipped = (s < 2) == (t < 2)
        along = jnp.where(flipped, 1 - offset, offset - 1)
        row_tap = jnp.where(t == 0, 0, jnp.where(t == 2, 2, 1 - along))
        col_tap = jnp.where(t == 1, 2, jnp.where(t == 3, 0, 1 - along))
        return 3 * row_tap + col_tap

    xs = iota((SIDES, C), 0)
    code = jnp.full((SIDES, C), 0, jnp.int32)
    for f in range(6):
        code = jnp.where(xs == f, nbs[f][1], code)
        code = jnp.where(xs == 8 + f, nbs[f][3], code)
    side_taps = [chosen(jnp.where(xs < 8, 1, 3), code, o) for o in range(3)]

    hub_side = jnp.where(is0, 0, 2)
    hub_nb = [jnp.where(is0, nbs[f][0], nbs[f][2]) for f in range(6)]
    hub_flip = [((hub_side < 2) == ((code_f & 3) < 2)).astype(jnp.int32) for code_f in hub_nb]

    def per_face(face, values, start):
        result = jnp.full(face.shape, start, jnp.int32)
        for f in range(6):
            result = jnp.where(face == f, values[f], result)
        return result

    @pl.when(ishub)
    def _():
        a = iota((8 * F, cells), 0)
        b = iota((8 * F, cells), 1)
        g = a & 7
        pos = a >> 3
        target = g * F + jnp.where(per_face(g, hub_flip, 0) == 1, F - 1 - pos, pos)
        amat[...] = onehot((b == target) & (g < 6))

    def edges(ph, i):
        row = rb[ph, i, 1].astype(F32)
        zero = jnp.zeros((2, C), F32)
        return jnp.concatenate([row[:, F - 1], zero, row[:, 0], zero], axis=0).astype(BF)

    def prepare(ph):
        for i in range(3):
            ebuf[ph, 16 * i : 16 * i + 16] = edges(ph, i)
        hm[ph] = dot(selh[...], ebuf[ph, 0:48]).astype(BF)

        @pl.when(ishub)
        def _():
            parts = []
            for i in range(3):
                parts.append(dot(amat[...], rb[ph, i, 1].reshape(cells, C)).reshape(F, 8, C))
            parts.append(jnp.zeros((F, 8, C), F32))
            zs[ph] = jnp.concatenate(parts, axis=1).astype(BF)

        @pl.when(is0)
        def _():
            rx[ph, 0] = hm[ph, 0:32]
            ebuf[ph, 96:128] = zs[ph, 0]

        @pl.when(is1)
        def _():
            rx[ph, n - 1] = hm[ph, 32:64]
            ebuf[ph, 128:160] = zs[ph, n - 1]

    def e_copy(ph):
        return rcopy(ebuf.at[ph, pl.ds(0, 48)], ebuf.at[ph, pl.ds(48, 48)], e_s.at[ph], e_r.at[ph], mirror)

    def hm_copy(ph, h):
        return rcopy(
            hm.at[ph, pl.ds(32 * h, 32)],
            rx.at[ph, r],
            hm_s.at[ph, h],
            rx_r.at[ph],
            (n - 1) * h,
        )

    def z_copy(ph, h, p):
        return rcopy(zs.at[ph, p], ebuf.at[ph, pl.ds(96 + 32 * h, 32)], z_s.at[ph], z_r.at[ph, h], p)

    def row_beside(ph, i, out):
        slot = slot_out if out else slot_in
        return rcopy(rb.at[ph, i, 1], rb.at[ph, i, slot], bulk_s.at[ph, 0], bulk_r.at[ph, i, 0], beside)

    def row_beyond(ph, i, out):
        slot = slot_in if out else slot_out
        return rcopy(rb.at[ph, i, 1], rb.at[ph, i, slot], bulk_s.at[ph, 1], bulk_r.at[ph, i, 1], beyond)

    def row_inward(ph, i):
        return rcopy(rb.at[ph, i, slot_in], rb.at[ph, i, slot_out], bulk_s.at[ph, 2], bulk_r.at[ph, i, 1], partner)

    def send_rows(ph, fields=(0, 1, 2)):
        for i in fields:
            row_beside(ph, i, True).start()

            @pl.when(outer)
            def _():
                row_beyond(ph, i, True).start()

    def hand_row(ph, i):
        @pl.when(outer)
        def _():
            row_beside(ph, i, False).wait_recv()
            row_inward(ph, i).start()

    def receive_row(ph, i):
        @pl.when(jnp.logical_not(outer))
        def _():
            row_beside(ph, i, False).wait_recv()

        row_beyond(ph, i, False).wait_recv()

    def finish_rows(ph):
        three = rb.at[ph, :, 1]

        def sent(kind):
            rcopy(three, three, bulk_s.at[ph, kind], bulk_r.at[ph, 0, 0], beside).wait_send()

        sent(0)

        @pl.when(outer)
        def _():
            sent(1)
            sent(2)

    def mt_copy(ph, way):
        return rcopy(
            mt.at[ph, 1],
            mt.at[ph, 2 if way == 0 else 0],
            mt_s.at[ph, way],
            mt_r.at[ph, way],
            up if way == 0 else dn,
        )

    def hub_loop(step):
        def body(i, carry):
            step(lax.rem(r + i, n))
            return carry

        lax.fori_loop(1, n, body, 0)

    def send(ph):
        for h, here in ((0, is0), (1, is1)):

            @pl.when(here)
            def _():
                hub_loop(lambda p: z_copy(ph, h, p).start())

            @pl.when(jnp.logical_not(here))
            def _():
                hm_copy(ph, h).start()

        e_copy(ph).start()

    def margins(ph):
        e_copy(ph).wait()
        for h, here in ((0, is0), (1, is1)):

            @pl.when(jnp.logical_not(here))
            def _():
                z_copy(ph, h, 0).wait_recv()

        mt[ph, 1] = dot(sel[...], ebuf[ph]).astype(BF)
        for way in range(2):
            mt_copy(ph, way).start()

    def hub_wait(ph):
        @pl.when(ishub)
        def _():
            start = jnp.where(is0, 1, 0)
            rcopy(zs.at[ph, pl.ds(0, n - 1)], rx.at[ph, pl.ds(start, n - 1)], z_s.at[ph], rx_r.at[ph], mirror).wait_recv()

    def hub_row(ph, i, spreads):
        @pl.when(ishub)
        def _():
            slot = jnp.where(is0, 0, 2)
            piece = rx[ph].astype(F32)[:, 8 * i : 8 * i + 8].reshape(8 * F, C).astype(BF)
            row = dot(bmat[...], piece)
            row = row + dot(c0mat[...], rb[ph, i, 1].reshape(cells, C))
            row = row + dot(c2mat[...], rb[ph, i, slot].reshape(cells, C))
            row = row.astype(BF).reshape(6, F, C)
            if spreads:
                mb[ph, i] = row
                rb[ph, i, slot] = jnp.zeros((6, F, C), BF)
            else:
                rb[ph, i, slot] = row

    def receive_margins(ph):
        for way in range(2):
            mt_copy(ph, way).wait()

        @pl.when(is0)
        def _():
            mt[ph, 0] = jnp.zeros((48, C), BF)

        @pl.when(is1)
        def _():
            mt[ph, 2] = jnp.zeros((48, C), BF)

    def finish_sends(ph):
        for h, here in ((0, is0), (1, is1)):

            @pl.when(here)
            def _():
                rcopy(zs.at[ph, pl.ds(0, n - 1)], rx.at[ph, pl.ds(0, n - 1)], z_s.at[ph], rx_r.at[ph], mirror).wait_send()

            @pl.when(jnp.logical_not(here))
            def _():
                hm_copy(ph, h).wait_send()

    def row_taps(ph, i, a, dst, spreads, scale):
        padz[:, 8 : 8 + F] = rb[ph, i, a].astype(F32) * scale
        for b in range(3):
            k = 3 * a + b
            k = 8 - k if spreads else k
            dst[0:cells, k * C : k * C + C] = padz[:, 7 + b : 7 + b + F].reshape(cells, C).astype(BF)

    def forward_sides(ph, i, dst):
        for a in range(3):
            line = mt[ph, a, 16 * i : 16 * i + 16].astype(F32)
            zero = jnp.zeros((SIDES, C), F32)
            for b, part in enumerate((jnp.where(xs < 8, zero, line), zero, jnp.where(xs < 8, line, zero))):
                k = 3 * a + b
                dst[cells : cells + SIDES, k * C : k * C + C] = part.astype(BF)

    def spread_sides(ph, i, dst, scale):
        lines = [mt[ph, o, 16 * i : 16 * i + 16].astype(F32) * scale for o in range(3)]
        for k in range(9):
            total = jnp.zeros((SIDES, C), F32)
            for o in range(3):
                total = jnp.where(side_taps[o] == k, lines[o], total)
            dst[cells : cells + SIDES, k * C : k * C + C] = total.astype(BF)

    def hub_taps(ph, i, extra, scale):
        padz[:, 8 : 8 + F] = mb[ph, i].astype(F32) * scale
        for f in range(6):
            picks = [chosen(hub_side, hub_nb[f], o) for o in range(3)]
            shifted = [padz[f, 7 + o : 7 + o + F] for o in range(3)]
            for k in range(9):
                total = jnp.zeros((F, C), F32)
                for o in range(3):
                    total = jnp.where(picks[o] == k, shifted[o], total)
                extra[f * F : f * F + F, k * C : k * C + C] = total.astype(BF)

    def add_sides(ref, lanes, side):
        for f in range(6):
            ref[f, F - 1 : F, lanes] += side[f : f + 1]
            ref[f, 0:1, lanes] += side[8 + f : 9 + f]

    def main_spread(ph, i, dst, extra, weights, scale, ref, lanes):
        width = lanes.stop - lanes.start
        ref[:, :, lanes] = dot(dst[0:cells], weights).reshape(6, F, width)

        @pl.when(ishub)
        def _():
            hub_taps(ph, i, extra, scale)
            ref[:, :, lanes] += dot(extra[...], weights).reshape(6, F, width)

    for cp in loads:
        cp.wait()
    prepare(0)
    base = 4 + (ny - 1) + (nz - 1)
    pl.semaphore_wait(barrier, base + 2 + jnp.where(ishub, n - 2, 0))
    send(0)
    send_rows(0)

    padz[...] = jnp.zeros(padz.shape, F32)
    for cp in wloads:
        cp.wait()
    wf1[:, 0:C] = wraw[0]
    wf1[:, C : 2 * C] = wraw[1]
    for k in range(9):
        rows = slice(k * C, k * C + C)
        ws1[rows, 0:C] = wraw[0, rows].astype(F32).T.astype(BF)
        ws1[rows, C : 2 * C] = wraw[1, rows].astype(F32).T.astype(BF)
        ws2[rows, 0:C] = wraw[2, rows].astype(F32).T.astype(BF)
        ws2[rows, C : 2 * C] = wraw[3, rows].astype(F32).T.astype(BF)

    @pl.when(ishub)
    def _():
        a = iota((cells, 8 * F), 0)
        b = iota((cells, 8 * F), 1)
        face = lax.div(a, F)
        pos = a - face * F
        pos = jnp.where(per_face(face, hub_flip, 0) == 1, F - 1 - pos, pos)
        column = per_face(face, [code_f & 1 for code_f in hub_nb], 0)
        bmat[...] = onehot((b == 8 * pos + face) & (column == 1))
        a = iota((cells, cells), 0)
        b = iota((cells, cells), 1)
        face = lax.div(a, F)
        pos = a - face * F
        code_a = per_face(face, hub_nb, 0)
        other = (code_a >> 2) * F
        c0mat[...] = onehot(((code_a & 3) == hub_side) & (b == other + F - 1 - pos))
        c2mat[...] = onehot(((code_a & 3) == 2 - hub_side) & (b == other + pos))

    inputs = ((0, tu, False, 1.0), (1, tv, False, 1.0), (2, ts, True, 0.5))
    for i, dst, spreads, scale in inputs:
        row_taps(0, i, 1, dst, spreads, scale)
    both = slice(0, 2 * C)
    left = slice(0, C)
    right = slice(C, 2 * C)

    def field_rows(i):
        receive_row(0, i)
        _, dst, spreads, scale = inputs[i]
        hub_row(0, i, spreads)
        row_taps(0, i, 0, dst, spreads, scale)
        row_taps(0, i, 2, dst, spreads, scale)

    hand_row(0, 0)
    margins(0)
    hand_row(0, 1)
    hub_wait(0)
    field_rows(0)
    front[...] = dot(tu[0:cells], wf1[...]).reshape(6, F, 2 * C)
    hand_row(0, 2)
    field_rows(1)
    front[:, :, right] += dot(tv[0:cells], wraw[0]).reshape(6, F, C)
    field_rows(2)
    main_spread(0, 2, ts, tx, ws2[...], 0.5, field, both)
    receive_margins(0)
    forward_sides(0, 0, tu)
    forward_sides(0, 1, tv)
    spread_sides(0, 2, ts, 0.5)
    side = dot(tu[cells:], wf1[...])
    more = dot(tv[cells:], wraw[0])
    add_sides(front, both, side)
    add_sides(front, right, more)
    add_sides(field, both, dot(ts[cells:], ws2[...]))
    squash = jnp.tanh(front[:, :, left])
    derivative = 1.0 - squash * squash
    hidden_tangent = front[:, :, right]
    act_tangent = (derivative * hidden_tangent).astype(BF)
    backward = field[:, :, left]
    scaled = derivative * backward
    rb[1, 0, 1] = squash.astype(BF)
    rb[1, 1, 1] = scaled.astype(BF)
    rb[1, 2, 1] = (derivative * field[:, :, right] - 2.0 * squash * scaled * hidden_tangent).astype(BF)
    aext[0:cells, right] = act_tangent.reshape(cells, C)

    send_rows(1, (0,))

    prepare(1)
    send(1)

    aext[0:cells, left] = rb[1, 0, 1].reshape(cells, C)
    aext[cells:, left] = edges(1, 0)
    zero = jnp.zeros((2, C), F32)
    wide = act_tangent.astype(F32)
    aext[cells:, right] = jnp.concatenate([wide[:, F - 1], zero, wide[:, 0], zero], axis=0).astype(BF)
    second = dot_t(aext[...], ts[...])
    for k in range(9):
        gsum[k * C : k * C + C] = second[0:C, k * C : k * C + C]
        gsum[K9 + k * C : K9 + k * C + C] = second[C : 2 * C, k * C : k * C + C]

    @pl.when(ishub)
    def _():
        more = dot_t(aext[0:cells], tx[...])
        for k in range(9):
            gsum[k * C : k * C + C] += more[0:C, k * C : k * C + C]
            gsum[K9 + k * C : K9 + k * C + C] += more[C : 2 * C, k * C : k * C + C]

    shard, p0, p1, qn = split_rows(ny, nz)
    qoff = p0 + p1 + qn * core
    qother = p0 + p1 + qn * (1 - core)
    def by_core(fn):
        @pl.when(core == 0)
        def _():
            fn(0, p0, p0, p1)

        @pl.when(core == 1)
        def _():
            fn(p0, p1, 0, p0)

    def ar(name, src, dst, p, extra=None):
        at = STEPS.index(name)
        return rcopy(src, dst, ar_s.at[at], ar_r.at[at if extra is None else len(STEPS) + extra], p)

    def sent(name, src):
        ar(name, src, src, partner).wait_send()

    def arrived(name, dst):
        ar(name, dst, dst, partner).wait_recv()

    ypeers = [ypeer(d) for d in sorted(range(1, ny), key=lambda d: -min(d, ny - d))]
    zpeers = [zpeer(d) for d in sorted(range(1, nz), key=lambda d: -min(d, nz - d))]
    hy = ny // 2

    def rows_of(h):
        return pl.ds(h * hy, hy)

    def core_p(h, off, size):
        at = (rows_of(h), slice(None), pl.ds(off, size))
        return ar(("cp0", "cp1")[h], gs.at[at], gr.at[at], partner)

    def core_q(h, o):
        at = (rows_of(h), slice(None), pl.ds(o, qn))
        return ar(("cq0", "cq1")[h], gs.at[at], gr.at[at], partner)

    def swap_cores(h):
        half = gsum[h * 2 * K9 : (h + 1) * 2 * K9]
        gs[h * hy : (h + 1) * hy] = half.astype(BF).reshape(hy, nz, shard, C)
        core_q(h, qother).start()
        by_core(lambda off, size, ooff, osize: core_p(h, ooff, osize).start())

    def own_half(h, off, size):
        half = gsum[h * 2 * K9 : (h + 1) * 2 * K9].reshape(hy, nz, shard, C)
        return half[:, :, off : off + size] + gr[h * hy : (h + 1) * hy, :, off : off + size].astype(F32)

    def q1(h, d):
        q, p = zpeers[d]
        return ar("q1", qs.at[rows_of(h), q], qr.at[z, rows_of(h)], p)

    def p1_copy(d, size):
        q, p = ypeers[d]
        return ar("p1", ps.at[q, :, pl.ds(0, size)], pr.at[y, :, pl.ds(0, size)], p)

    def first_step(h):
        rows = slice(h * hy, (h + 1) * hy)
        core_q(h, qother).wait_send()
        core_q(h, qoff).wait_recv()

        def stage(qo):
            part = own_half(h, qo, qn)
            qf[rows] = part
            qs[rows] = part.astype(BF)

        by_core(lambda off, size, ooff, osize: stage(p0 + p1 if off == 0 else p0 + p1 + qn))
        for d in range(nz - 1):
            q1(h, d).start()

        def stage(off, size, ooff, osize):
            core_p(h, ooff, osize).wait_send()
            core_p(h, off, size).wait_recv()
            part = own_half(h, off, size)
            pf[rows, :, 0:size] = part
            ps[rows, :, 0:size] = part.astype(BF)
            for d in range(ny - 1):

                @pl.when(lax.div(ypeers[d][0], hy) == h)
                def _():
                    p1_copy(d, size).start()

        by_core(stage)

    swap_cores(0)
    for i, lanes in ((1, left), (2, right)):
        pext[0:cells, lanes] = rb[1, i, 1].reshape(cells, C)
        pext[cells:, lanes] = edges(1, i)
    first = dot_t(tu[...], pext[...])
    gsum[2 * K9 : 3 * K9] = first[:, 0:C]
    gsum[3 * K9 : 4 * K9] = first[:, C : 2 * C] + dot_t(tv[...], pext[:, left])
    swap_cores(1)
    first_step(0)
    first_step(1)
    send_rows(1, (1,))

    def p2_copy(d, size):
        q, p = zpeers[d]
        return ar("p2", pz.at[q, pl.ds(0, size)], pzr.at[z, pl.ds(0, size)], p)

    def stage(off, size, ooff, osize):
        arrived("p1", pr.at[pl.ds(0, ny - 1), :, pl.ds(0, size)])
        part = pf[y, :, 0:size]
        for q, p in ypeers:
            part = part + pr[q, :, 0:size].astype(F32)
        pzf[:, 0:size] = part
        pz[:, 0:size] = part.astype(BF)
        for d in range(nz - 1):
            p2_copy(d, size).start()

    by_core(stage)

    def q2(d):
        q, p = ypeers[d]
        return ar("q2", qy.at[q], qyr.at[y], p)

    send_rows(1, (2,))
    arrived("q1", qr.at[pl.ds(0, nz - 1)])
    part = qf[:, z]
    for q, p in zpeers:
        part = part + qr[q].astype(F32)
    qyf[...] = part
    qy[...] = part.astype(BF)
    for d in range(ny - 1):
        q2(d).start()

    scale = 1.0 / F

    def p3(d, size, off):
        q, p = zpeers[d]
        return ar("p3", fin_p.at[pl.ds(0, size)], out_ref.at[y, z, pl.ds(off, size)], p)

    def own_p(size, off):
        return pltpu.make_async_copy(fin_p.at[pl.ds(0, size)], out_ref.at[y, z, pl.ds(off, size)], osem.at[3])

    own_q = pltpu.make_async_copy(fin_q, out_ref.at[y, z, pl.ds(qoff, qn)], osem.at[4])

    def stage(off, size, ooff, osize):
        arrived("p2", pzr.at[pl.ds(0, nz - 1), pl.ds(0, size)])
        part = pzf[z, 0:size]
        for q, p in zpeers:
            part = part + pzr[q, 0:size].astype(F32)
        fin_p[0:size] = (part * scale).astype(BF)
        own_p(size, off).start()
        for d in range(nz - 1):
            p3(d, size, off).start()

    by_core(stage)

    def q3(d):
        q, p = ypeers[d]
        return ar("q3", fin_q, out_ref.at[y, z, pl.ds(qoff, qn)], p)

    arrived("q2", qyr.at[pl.ds(0, ny - 1)])
    part = qyf[y]
    for q, p in ypeers:
        part = part + qyr[q].astype(F32)
    fin_q[...] = (part * scale).astype(BF)
    own_q.start()
    for d in range(ny - 1):
        q3(d).start()
    for q, p in zpeers:
        ar("q4", fin_q, out_ref.at[y, z, pl.ds(qoff, qn)], p, ny + z).start()

    outs = [pltpu.make_async_copy(res.at[i], ref, osem.at[i]) for i, ref in enumerate((next_ref, adj_ref, adt_ref))]

    for i in range(3):
        hand_row(1, i)
    margins(1)
    hub_wait(1)
    for i in range(3):
        receive_row(1, i)
        hub_row(1, i, i > 0)
    for a in range(3):
        row_taps(1, 0, a, tu, False, 1.0)
    field[:, :, left] = dot(tu[0:cells], wraw[2]).reshape(6, F, C)

    def p4(d, size, off, out):
        q, p = ypeers[d]
        qq = y if out else q
        ref = out_ref.at[qq, :, pl.ds(off, size)]
        return ar("p4", ref, ref, p, qq)

    def cpy_p(q, size, off):
        ref = out_ref.at[q, :, pl.ds(off, size)]
        return ar("c4", ref, ref, partner)

    def stage(off, size, ooff, osize):
        arrived("p3", out_ref.at[y, pl.ds(0, nz - 1), pl.ds(off, size)])
        own_p(size, off).wait()
        for d in range(ny - 1):
            p4(d, size, off, True).start()
        cpy_p(y, size, off).start()

    by_core(stage)

    def q4_in(q):
        ref = out_ref.at[:, q, pl.ds(qoff, qn)]
        return ar("q4", ref, ref, partner, ny + q)

    def q4_rest(d, qq):
        ref = out_ref.at[qq, z, pl.ds(qoff, qn)]
        return ar("q4", ref, ref, zpeers[d][1], ny + z)

    def cpy_q(q, o):
        ref = out_ref.at[:, q, pl.ds(o, qn)]
        return ar("d4", ref, ref, partner)

    arrived("q3", out_ref.at[pl.ds(0, ny - 1), z, pl.ds(qoff, qn)])
    own_q.wait()
    for d in range(nz - 1):
        for q, p in ypeers:
            q4_rest(d, q).start()
    cpy_q(z, qoff).start()

    receive_margins(1)
    forward_sides(1, 0, tu)
    add_sides(field, left, dot(tu[cells:], wraw[2]))
    res[0] = (rb[0, 0, 1].astype(F32) + 0.5 * field[:, :, left]).astype(BF)
    outs[0].start()

    def adjoint_of(i, dst, weights, ref, lanes):
        for a in range(3):
            row_taps(1, i, a, dst, True, 1.0)
        spread_sides(1, i, dst, 1.0)
        main_spread(1, i, dst, tx, weights, 1.0, ref, lanes)
        add_sides(ref, lanes, dot(dst[cells:], weights))

    adjoint_of(1, ts, ws1[...], front, both)
    res[1] = (rb[0, 2, 1].astype(F32) + front[:, :, left]).astype(BF)
    outs[1].start()

    adjoint_of(2, ts, ws1[:, 0:C], field, left)
    res[2] = (front[:, :, right] + field[:, :, left]).astype(BF)
    outs[2].start()

    def stage(off, size, ooff, osize):
        for d in range(ny - 1):
            p4(d, size, off, False).wait_recv()
            cpy_p(ypeers[d][0], size, off).start()

    by_core(stage)
    for d in range(nz - 1):
        q4_in(zpeers[d][0]).wait_recv()
        cpy_q(zpeers[d][0], qoff).start()

    def stage(off, size, ooff, osize):
        sent("p1", pr.at[pl.ds(0, ny - 1), :, pl.ds(0, size)])
        sent("p2", pzr.at[pl.ds(0, nz - 1), pl.ds(0, size)])
        sent("p3", out_ref.at[y, pl.ds(0, nz - 1), pl.ds(off, size)])
        sent("p4", out_ref.at[pl.ds(0, ny - 1), :, pl.ds(off, size)])
        sent("c4", out_ref.at[:, :, pl.ds(off, size)])
        arrived("c4", out_ref.at[:, :, pl.ds(ooff, osize)])

    by_core(stage)
    sent("q1", qr.at[pl.ds(0, nz - 1)])
    sent("q2", qyr.at[pl.ds(0, ny - 1)])
    sent("q3", out_ref.at[pl.ds(0, ny - 1), z, pl.ds(qoff, qn)])
    sent("q4", out_ref.at[:, pl.ds(0, nz - 1), pl.ds(qoff, qn)])
    sent("d4", out_ref.at[:, :, pl.ds(qoff, qn)])
    arrived("d4", out_ref.at[:, :, pl.ds(qother, qn)])
    for cp in outs:
        cp.wait()
    for ph in range(2):
        finish_sends(ph)
        finish_rows(ph)


STEPS = ("cp0", "cq0", "cp1", "cq1", "q1", "p1", "p2", "q2", "p3", "q3", "p4", "c4", "q4", "d4")


def split_rows(ny, nz):
    tiles = 4 * K9 // (16 * ny * nz)
    qn = 2 * tiles // 9
    p1 = (tiles - 2 * qn) // 2
    return 16 * tiles, 16 * (tiles - 2 * qn - p1), 16 * p1, 16 * qn


CHUNKS = 8


def finish(n_ref, a_ref, t_ref, g_ref, n_out, a_out, t_out, w_out, h_out, packed, wide, held, in_sem, out_sem, row_in, row_out):
    size = packed.shape[1]
    row_ins = [pltpu.make_async_copy(src, held.at[i], row_in.at[i]) for i, src in enumerate((n_ref, a_ref, t_ref))]
    row_outs = [pltpu.make_async_copy(held.at[i], dst, row_out.at[i]) for i, dst in enumerate((n_out, a_out, t_out))]
    quarter = CHUNKS // 4
    ins = [pltpu.make_async_copy(g_ref.at[pl.ds(i * size, size)], packed.at[i], in_sem.at[i]) for i in range(CHUNKS)]
    outs = [
        pltpu.make_async_copy(
            wide.at[i],
            (w_out, h_out)[i // quarter % 2].at[pl.ds((i % quarter + (quarter if i < 2 * quarter else 0)) * size, size)],
            out_sem.at[i],
        )
        for i in range(CHUNKS)
    ]
    for cp in ins + row_ins:
        cp.start()
    for i in range(CHUNKS):
        ins[i].wait()
        wide[i] = packed[i].astype(F32)
        outs[i].start()
    for i in range(3):
        row_ins[i].wait()
        row_outs[i].start()
    for cp in outs + row_outs:
        cp.wait()


def on_device(n, ny, nz, u, v, c, w1, w2, t1, t2, nb):
    F = n
    cells = 6 * F
    shard, p0, p1, qn = split_rows(ny, nz)
    u, v, c = (a.reshape(6, F, C) for a in (u, v, c))
    w1, w2, t1, t2 = (a.reshape(K9, C) for a in (w1, w2, t1, t2))
    vm = pltpu.VMEM
    dma = pltpu.SemaphoreType.DMA
    anywhere = pl.BlockSpec(memory_space=pl.ANY)
    inside = pl.BlockSpec(memory_space=pltpu.VMEM)
    row = jax.ShapeDtypeStruct((6, F, C), BF)
    nxt, adj, adt, out = pl.pallas_call(
        functools.partial(kernel, n, ny, nz),
        out_shape=(row, row, row, jax.ShapeDtypeStruct((ny, nz, shard, C), BF)),
        in_specs=[anywhere] * 8,
        out_specs=(anywhere,) * 4,
        scratch_shapes=[
            vm((2, 3, 3, 6, F, C), BF),
            vm((2, 3, 6, F, C), BF),
            vm((2, 160, C), BF),
            vm((2, 64, C), BF),
            vm((2, F, 32, C), BF),
            vm((2, F, 32, C), BF),
            vm((2, 3, 48, C), BF),
            vm((48, 160), BF),
            vm((64, 48), BF),
            vm((8 * F, cells), BF),
            vm((cells, 8 * F), BF),
            vm((cells, cells), BF),
            vm((cells, cells), BF),
            vm((4, K9, C), BF),
            vm((K9, 2 * C), BF),
            vm((K9, 2 * C), BF),
            vm((K9, 2 * C), BF),
            vm((6, F + 16, C), F32),
            vm((cells + SIDES, K9), BF),
            vm((cells + SIDES, K9), BF),
            vm((cells + SIDES, K9), BF),
            vm((cells, K9), BF),
            vm((cells + SIDES, 2 * C), BF),
            vm((cells + SIDES, 2 * C), BF),
            vm((6, F, 2 * C), F32),
            vm((6, F, 2 * C), F32),
            vm((4 * K9, C), F32),
            vm((ny, nz, shard, C), BF),
            vm((ny, nz, shard, C), BF),
            vm((ny, nz, p0, C), F32),
            vm((ny, nz, p0, C), BF),
            vm((ny, nz, p0, C), BF),
            vm((ny, nz, qn, C), F32),
            vm((ny, nz, qn, C), BF),
            vm((nz, ny, qn, C), BF),
            vm((nz, p0, C), BF),
            vm((nz, p0, C), F32),
            vm((nz, p0, C), BF),
            vm((ny, qn, C), BF),
            vm((ny, qn, C), F32),
            vm((ny, qn, C), BF),
            pltpu.SMEM((4, 6), jnp.int32),
            vm((3, 6, F, C), BF),
            vm((p0, C), BF),
            vm((qn, C), BF),
            dma((5,)),
            dma((8,)),
            dma((2, 3)),
            dma((2, 3, 2)),
            dma((2,)),
            dma((2,)),
            dma((2, 2)),
            dma((2,)),
            dma((2,)),
            dma((2, 2)),
            dma((2, 2)),
            dma((2, 2)),
            dma((len(STEPS),)),
            dma((len(STEPS) + ny + nz,)),
        ],
        compiler_params=pltpu.CompilerParams(
            collective_id=0, has_side_effects=True, vmem_limit_bytes=56 * 2**20
        ),
    )(u, v, c, w1, w2, t1, t2, nb.T)
    half = 2 * K9
    grad = jax.ShapeDtypeStruct((half, C), F32)
    nxt, adj, adt, wg, hp = pl.pallas_call(
        finish,
        out_shape=(row, row, row, grad, grad),
        in_specs=[anywhere] * 4,
        out_specs=(anywhere,) * 5,
        scratch_shapes=[vm((CHUNKS, 2 * half // CHUNKS, C), BF), vm((CHUNKS, 2 * half // CHUNKS, C), F32), vm((3, 6, F, C), BF), dma((CHUNKS,)), dma((CHUNKS,)), dma((3,)), dma((3,))],
        compiler_params=pltpu.CompilerParams(vmem_limit_bytes=56 * 2**20),
    )(nxt, adj, adt, out.reshape(2 * half, C))
    shape4 = (2, 9, C, C)
    shape = (6, 1, F, C)
    return nxt.reshape(shape), adj.reshape(shape), adt.reshape(shape), wg.reshape(shape4), hp.reshape(shape4)


def solution(mesh):
    n = mesh.shape["tile"] * mesh.shape["sub"]
    nz = 8 if n == 64 else 2
    ny = n // (2 * nz)
    field = P("rep", ("tile", "sub"), None, None)
    grads = P("rep", None, None, None)
    return jax.shard_map(
        functools.partial(on_device, n, ny, nz),
        mesh=mesh,
        in_specs=(field, field, field, P(), P(), P(), P(), P()),
        out_specs=(field, field, field, grads, grads),
        check_vma=False,
    )
```

```python
import functools

import jax
import jax.numpy as jnp
from jax import lax
from jax.experimental import pallas as pl
from jax.experimental.pallas import tpu as pltpu
from jax.sharding import PartitionSpec as P

MESH = pl.DeviceIdType.MESH
BF = jnp.bfloat16
F32 = jnp.float32
C = 128
K9 = 9 * C
SIDES = 16


def dot(a, b):
    return jnp.dot(a, b, preferred_element_type=F32)


def dot_t(a, b):
    return lax.dot_general(a, b, (((0,), (0,)), ((), ())), preferred_element_type=F32)


def iota(shape, dim):
    return lax.broadcasted_iota(jnp.int32, shape, dim)


def onehot(mask):
    return jnp.where(mask, 1.0, 0.0).astype(BF)


def kernel(
    n,
    ny,
    nz,
    u_ref,
    v_ref,
    c_ref,
    w1_ref,
    w2_ref,
    t1_ref,
    t2_ref,
    nb_ref,
    next_ref,
    adj_ref,
    adt_ref,
    out_ref,
    rb,
    mb,
    ebuf,
    hm,
    zs,
    rx,
    mt,
    sel,
    selh,
    amat,
    bmat,
    c0mat,
    c2mat,
    wraw,
    wf1,
    ws1,
    ws2,
    padz,
    tu,
    tv,
    ts,
    tx,
    aext,
    pext,
    front,
    field,
    gsum,
    gs,
    gr,
    pf,
    ps,
    pr,
    qf,
    qs,
    qr,
    pz,
    pzf,
    pzr,
    qy,
    qyf,
    qyr,
    nbm,
    res,
    fin_p,
    fin_q,
    osem,
    lsem,
    bulk_s,
    bulk_r,
    e_s,
    e_r,
    hm_s,
    rx_r,
    z_s,
    z_r,
    mt_s,
    mt_r,
    ar_s,
    ar_r,
):
    F = n
    cells = 6 * F
    rep = lax.axis_index("rep")
    r = lax.axis_index("tile") * 2 + lax.axis_index("sub")
    core = lax.rem(lax.div(r, 2), 2)
    z = lax.rem(lax.div(r, 4), nz)
    yhi = lax.div(r, 4 * nz)
    ylo = lax.rem(r, 2)
    y = yhi * 2 + ylo

    def dev(p):
        return (lax.div(p, 2), lax.rem(p, 2), rep)

    def make(hi, zc, co, lo):
        return ((hi * nz + zc) * 2 + co) * 2 + lo

    up = lax.rem(r + n - 1, n)
    dn = lax.rem(r + 1, n)
    mirror = n - 1 - r
    odd = lax.rem(r, 2)
    beside = r + 1 - 2 * odd
    beyond = lax.rem(r + n - 1 + 2 * odd, n)
    outer = jnp.logical_or(lax.rem(r, 4) == 0, lax.rem(r, 4) == 3)
    slot_in = 2 - 2 * odd
    slot_out = 2 * odd
    partner = make(yhi, z, 1 - core, ylo)

    def ypeer(d):
        q = lax.rem(y + d, ny)
        return q, make(lax.div(q, 2), z, core, lax.rem(q, 2))

    def zpeer(d):
        q = lax.rem(z + d, nz)
        return q, make(yhi, q, core, ylo)

    is0 = r == 0
    is1 = r == n - 1
    ishub = jnp.logical_or(is0, is1)

    def rcopy(src, dst, ssem, rsem, p):
        return pltpu.make_async_remote_copy(
            src_ref=src,
            dst_ref=dst,
            send_sem=ssem,
            recv_sem=rsem,
            device_id=dev(p),
            device_id_type=MESH,
        )

    nbload = pltpu.make_async_copy(nb_ref, nbm, lsem.at[7])
    nbload.start()
    loads = [pltpu.make_async_copy(ref, rb.at[0, i, 1], lsem.at[i]) for i, ref in enumerate((u_ref, v_ref, c_ref))]
    wloads = [pltpu.make_async_copy(ref, wraw.at[i], lsem.at[3 + i]) for i, ref in enumerate((w1_ref, t1_ref, w2_ref, t2_ref))]
    for cp in loads + wloads:
        cp.start()

    barrier = pltpu.get_barrier_semaphore()

    def greet(p):
        pl.semaphore_signal(barrier, inc=1, device_id=dev(p), device_id_type=MESH)

    @pl.when(ishub)
    def _():
        def body(i, carry):
            greet(lax.rem(r + i, n))
            return carry

        lax.fori_loop(1, n, body, 0)

    @pl.when(r != 0)
    def _():
        greet(0)

    @pl.when(r != n - 1)
    def _():
        greet(n - 1)

    for p in (up, dn, mirror, partner):
        greet(p)
    for d in range(1, ny):
        greet(ypeer(d)[1])
    for d in range(1, nz):
        greet(zpeer(d)[1])

    nbload.wait()
    nbs = [[nbm[s, f] for s in range(4)] for f in range(6)]
    x = iota((48, 160), 0)
    yy = iota((48, 160), 1)
    xs = x & 15
    xsd = jnp.where(xs < 8, 1, 3)
    xnb = jnp.full((48, 160), -1, jnp.int32)
    for f in range(6):
        xnb = jnp.where(xs == f, nbs[f][1], xnb)
        xnb = jnp.where(xs == 8 + f, nbs[f][3], xnb)
    ym = jnp.where(yy >= 48, yy - 48, yy)
    ysd = jnp.where((ym & 15) < 8, 1, 3)
    yz = (yy - 96) & 31
    isz = yy >= 96
    yg = jnp.where(isz, yz & 7, ym & 7)
    yt = jnp.where(isz, jnp.where(yy >= 128, 2, 0), ysd)
    yfield = jnp.where(isz, yz >> 3, ym >> 4)
    way = jnp.where(isz, 1, jnp.where(yy >= 48, jnp.where(xsd == ysd, 1, 0), jnp.where(xsd == ysd, 0, 1)))
    sel[...] = onehot((xnb == 4 * yg + yt) & ((x >> 4) == yfield) & (yg < 6) & (way == 1))
    x = iota((64, 48), 0)
    yy = iota((64, 48), 1)
    xnb = jnp.full((64, 48), -1, jnp.int32)
    for f in range(6):
        xnb = jnp.where((x & 7) == f, jnp.where(x < 32, nbs[f][0], nbs[f][2]), xnb)
    yt = jnp.where((yy & 15) < 8, 1, 3)
    selh[...] = onehot((xnb == 4 * (yy & 7) + yt) & (((x & 31) >> 3) == (yy >> 4)) & ((yy & 7) < 6))

    def chosen(s, code, offset):
        t = code & 3
        flipped = (s < 2) == (t < 2)
        along = jnp.where(flipped, 1 - offset, offset - 1)
        row_tap = jnp.where(t == 0, 0, jnp.where(t == 2, 2, 1 - along))
        col_tap = jnp.where(t == 1, 2, jnp.where(t == 3, 0, 1 - along))
        return 3 * row_tap + col_tap

    xs = iota((SIDES, C), 0)
    code = jnp.full((SIDES, C), 0, jnp.int32)
    for f in range(6):
        code = jnp.where(xs == f, nbs[f][1], code)
        code = jnp.where(xs == 8 + f, nbs[f][3], code)
    side_taps = [chosen(jnp.where(xs < 8, 1, 3), code, o) for o in range(3)]

    hub_side = jnp.where(is0, 0, 2)
    hub_nb = [jnp.where(is0, nbs[f][0], nbs[f][2]) for f in range(6)]
    hub_flip = [((hub_side < 2) == ((code_f & 3) < 2)).astype(jnp.int32) for code_f in hub_nb]

    def per_face(face, values, start):
        result = jnp.full(face.shape, start, jnp.int32)
        for f in range(6):
            result = jnp.where(face == f, values[f], result)
        return result

    @pl.when(ishub)
    def _():
        a = iota((8 * F, cells), 0)
        b = iota((8 * F, cells), 1)
        g = a & 7
        pos = a >> 3
        target = g * F + jnp.where(per_face(g, hub_flip, 0) == 1, F - 1 - pos, pos)
        amat[...] = onehot((b == target) & (g < 6))

    def edges(ph, i):
        row = rb[ph, i, 1].astype(F32)
        zero = jnp.zeros((2, C), F32)
        return jnp.concatenate([row[:, F - 1], zero, row[:, 0], zero], axis=0).astype(BF)

    def prepare(ph):
        for i in range(3):
            ebuf[ph, 16 * i : 16 * i + 16] = edges(ph, i)
        hm[ph] = dot(selh[...], ebuf[ph, 0:48]).astype(BF)

        @pl.when(ishub)
        def _():
            parts = []
            for i in range(3):
                parts.append(dot(amat[...], rb[ph, i, 1].reshape(cells, C)).reshape(F, 8, C))
            parts.append(jnp.zeros((F, 8, C), F32))
            zs[ph] = jnp.concatenate(parts, axis=1).astype(BF)

        @pl.when(is0)
        def _():
            rx[ph, 0] = hm[ph, 0:32]
            ebuf[ph, 96:128] = zs[ph, 0]

        @pl.when(is1)
        def _():
            rx[ph, n - 1] = hm[ph, 32:64]
            ebuf[ph, 128:160] = zs[ph, n - 1]

    def e_copy(ph):
        return rcopy(ebuf.at[ph, pl.ds(0, 48)], ebuf.at[ph, pl.ds(48, 48)], e_s.at[ph], e_r.at[ph], mirror)

    def hm_copy(ph, h):
        return rcopy(
            hm.at[ph, pl.ds(32 * h, 32)],
            rx.at[ph, r],
            hm_s.at[ph, h],
            rx_r.at[ph],
            (n - 1) * h,
        )

    def z_copy(ph, h, p):
        return rcopy(zs.at[ph, p], ebuf.at[ph, pl.ds(96 + 32 * h, 32)], z_s.at[ph], z_r.at[ph, h], p)

    def row_beside(ph, i, out):
        slot = slot_out if out else slot_in
        return rcopy(rb.at[ph, i, 1], rb.at[ph, i, slot], bulk_s.at[ph, 0], bulk_r.at[ph, i, 0], beside)

    def row_beyond(ph, i, out):
        slot = slot_in if out else slot_out
        return rcopy(rb.at[ph, i, 1], rb.at[ph, i, slot], bulk_s.at[ph, 1], bulk_r.at[ph, i, 1], beyond)

    def row_inward(ph, i):
        return rcopy(rb.at[ph, i, slot_in], rb.at[ph, i, slot_out], bulk_s.at[ph, 2], bulk_r.at[ph, i, 1], partner)

    def send_rows(ph, fields=(0, 1, 2)):
        for i in fields:
            row_beside(ph, i, True).start()

            @pl.when(outer)
            def _():
                row_beyond(ph, i, True).start()

    def hand_row(ph, i):
        @pl.when(outer)
        def _():
            row_beside(ph, i, False).wait_recv()
            row_inward(ph, i).start()

    def receive_row(ph, i):
        @pl.when(jnp.logical_not(outer))
        def _():
            row_beside(ph, i, False).wait_recv()

        row_beyond(ph, i, False).wait_recv()

    def finish_rows(ph):
        three = rb.at[ph, :, 1]

        def sent(kind):
            rcopy(three, three, bulk_s.at[ph, kind], bulk_r.at[ph, 0, 0], beside).wait_send()

        sent(0)

        @pl.when(outer)
        def _():
            sent(1)
            sent(2)

    def mt_copy(ph, way):
        return rcopy(
            mt.at[ph, 1],
            mt.at[ph, 2 if way == 0 else 0],
            mt_s.at[ph, way],
            mt_r.at[ph, way],
            up if way == 0 else dn,
        )

    def hub_loop(step):
        def body(i, carry):
            step(lax.rem(r + i, n))
            return carry

        lax.fori_loop(1, n, body, 0)

    def send(ph):
        for h, here in ((0, is0), (1, is1)):

            @pl.when(here)
            def _():
                hub_loop(lambda p: z_copy(ph, h, p).start())

            @pl.when(jnp.logical_not(here))
            def _():
                hm_copy(ph, h).start()

        e_copy(ph).start()

    def margins(ph):
        e_copy(ph).wait()
        for h, here in ((0, is0), (1, is1)):

            @pl.when(jnp.logical_not(here))
            def _():
                z_copy(ph, h, 0).wait_recv()

        mt[ph, 1] = dot(sel[...], ebuf[ph]).astype(BF)
        for way in range(2):
            mt_copy(ph, way).start()

    def hub_wait(ph):
        @pl.when(ishub)
        def _():
            start = jnp.where(is0, 1, 0)
            rcopy(zs.at[ph, pl.ds(0, n - 1)], rx.at[ph, pl.ds(start, n - 1)], z_s.at[ph], rx_r.at[ph], mirror).wait_recv()

    def hub_row(ph, i, spreads):
        @pl.when(ishub)
        def _():
            slot = jnp.where(is0, 0, 2)
            piece = rx[ph].astype(F32)[:, 8 * i : 8 * i + 8].reshape(8 * F, C).astype(BF)
            row = dot(bmat[...], piece)
            row = row + dot(c0mat[...], rb[ph, i, 1].reshape(cells, C))
            row = row + dot(c2mat[...], rb[ph, i, slot].reshape(cells, C))
            row = row.astype(BF).reshape(6, F, C)
            if spreads:
                mb[ph, i] = row
                rb[ph, i, slot] = jnp.zeros((6, F, C), BF)
            else:
                rb[ph, i, slot] = row

    def receive_margins(ph):
        for way in range(2):
            mt_copy(ph, way).wait()

        @pl.when(is0)
        def _():
            mt[ph, 0] = jnp.zeros((48, C), BF)

        @pl.when(is1)
        def _():
            mt[ph, 2] = jnp.zeros((48, C), BF)

    def finish_sends(ph):
        for h, here in ((0, is0), (1, is1)):

            @pl.when(here)
            def _():
                rcopy(zs.at[ph, pl.ds(0, n - 1)], rx.at[ph, pl.ds(0, n - 1)], z_s.at[ph], rx_r.at[ph], mirror).wait_send()

            @pl.when(jnp.logical_not(here))
            def _():
                hm_copy(ph, h).wait_send()

    def row_taps(ph, i, a, dst, spreads, scale):
        padz[:, 8 : 8 + F] = rb[ph, i, a].astype(F32) * scale
        for b in range(3):
            k = 3 * a + b
            k = 8 - k if spreads else k
            dst[0:cells, k * C : k * C + C] = padz[:, 7 + b : 7 + b + F].reshape(cells, C).astype(BF)

    def forward_sides(ph, i, dst):
        for a in range(3):
            line = mt[ph, a, 16 * i : 16 * i + 16].astype(F32)
            zero = jnp.zeros((SIDES, C), F32)
            for b, part in enumerate((jnp.where(xs < 8, zero, line), zero, jnp.where(xs < 8, line, zero))):
                k = 3 * a + b
                dst[cells : cells + SIDES, k * C : k * C + C] = part.astype(BF)

    def spread_sides(ph, i, dst, scale):
        lines = [mt[ph, o, 16 * i : 16 * i + 16].astype(F32) * scale for o in range(3)]
        for k in range(9):
            total = jnp.zeros((SIDES, C), F32)
            for o in range(3):
                total = jnp.where(side_taps[o] == k, lines[o], total)
            dst[cells : cells + SIDES, k * C : k * C + C] = total.astype(BF)

    def hub_taps(ph, i, extra, scale):
        padz[:, 8 : 8 + F] = mb[ph, i].astype(F32) * scale
        for f in range(6):
            picks = [chosen(hub_side, hub_nb[f], o) for o in range(3)]
            shifted = [padz[f, 7 + o : 7 + o + F] for o in range(3)]
            for k in range(9):
                total = jnp.zeros((F, C), F32)
                for o in range(3):
                    total = jnp.where(picks[o] == k, shifted[o], total)
                extra[f * F : f * F + F, k * C : k * C + C] = total.astype(BF)

    def add_sides(ref, lanes, side):
        for f in range(6):
            ref[f, F - 1 : F, lanes] += side[f : f + 1]
            ref[f, 0:1, lanes] += side[8 + f : 9 + f]

    def main_spread(ph, i, dst, extra, weights, scale, ref, lanes):
        width = lanes.stop - lanes.start
        ref[:, :, lanes] = dot(dst[0:cells], weights).reshape(6, F, width)

        @pl.when(ishub)
        def _():
            hub_taps(ph, i, extra, scale)
            ref[:, :, lanes] += dot(extra[...], weights).reshape(6, F, width)

    for cp in loads:
        cp.wait()
    prepare(0)
    base = 4 + (ny - 1) + (nz - 1)
    pl.semaphore_wait(barrier, base + 2 + jnp.where(ishub, n - 2, 0))
    send(0)
    send_rows(0)

    padz[...] = jnp.zeros(padz.shape, F32)
    for cp in wloads:
        cp.wait()
    wf1[:, 0:C] = wraw[0]
    wf1[:, C : 2 * C] = wraw[1]
    for k in range(9):
        rows = slice(k * C, k * C + C)
        ws1[rows, 0:C] = wraw[0, rows].astype(F32).T.astype(BF)
        ws1[rows, C : 2 * C] = wraw[1, rows].astype(F32).T.astype(BF)
        ws2[rows, 0:C] = wraw[2, rows].astype(F32).T.astype(BF)
        ws2[rows, C : 2 * C] = wraw[3, rows].astype(F32).T.astype(BF)

    @pl.when(ishub)
    def _():
        a = iota((cells, 8 * F), 0)
        b = iota((cells, 8 * F), 1)
        face = lax.div(a, F)
        pos = a - face * F
        pos = jnp.where(per_face(face, hub_flip, 0) == 1, F - 1 - pos, pos)
        column = per_face(face, [code_f & 1 for code_f in hub_nb], 0)
        bmat[...] = onehot((b == 8 * pos + face) & (column == 1))
        a = iota((cells, cells), 0)
        b = iota((cells, cells), 1)
        face = lax.div(a, F)
        pos = a - face * F
        code_a = per_face(face, hub_nb, 0)
        other = (code_a >> 2) * F
        c0mat[...] = onehot(((code_a & 3) == hub_side) & (b == other + F - 1 - pos))
        c2mat[...] = onehot(((code_a & 3) == 2 - hub_side) & (b == other + pos))

    inputs = ((0, tu, False, 1.0), (1, tv, False, 1.0), (2, ts, True, 0.5))
    for i, dst, spreads, scale in inputs:
        row_taps(0, i, 1, dst, spreads, scale)
    both = slice(0, 2 * C)
    left = slice(0, C)
    right = slice(C, 2 * C)

    def field_rows(i):
        receive_row(0, i)
        _, dst, spreads, scale = inputs[i]
        hub_row(0, i, spreads)
        row_taps(0, i, 0, dst, spreads, scale)
        row_taps(0, i, 2, dst, spreads, scale)

    hand_row(0, 0)
    margins(0)
    hand_row(0, 1)
    hub_wait(0)
    field_rows(0)
    front[...] = dot(tu[0:cells], wf1[...]).reshape(6, F, 2 * C)
    hand_row(0, 2)
    field_rows(1)
    front[:, :, right] += dot(tv[0:cells], wraw[0]).reshape(6, F, C)
    field_rows(2)
    main_spread(0, 2, ts, tx, ws2[...], 0.5, field, both)
    receive_margins(0)
    forward_sides(0, 0, tu)
    forward_sides(0, 1, tv)
    spread_sides(0, 2, ts, 0.5)
    side = dot(tu[cells:], wf1[...])
    more = dot(tv[cells:], wraw[0])
    add_sides(front, both, side)
    add_sides(front, right, more)
    add_sides(field, both, dot(ts[cells:], ws2[...]))
    squash = jnp.tanh(front[:, :, left])
    derivative = 1.0 - squash * squash
    hidden_tangent = front[:, :, right]
    act_tangent = (derivative * hidden_tangent).astype(BF)
    backward = field[:, :, left]
    scaled = derivative * backward
    rb[1, 0, 1] = squash.astype(BF)
    rb[1, 1, 1] = scaled.astype(BF)
    rb[1, 2, 1] = (derivative * field[:, :, right] - 2.0 * squash * scaled * hidden_tangent).astype(BF)
    aext[0:cells, right] = act_tangent.reshape(cells, C)

    send_rows(1, (0,))

    aext[0:cells, left] = rb[1, 0, 1].reshape(cells, C)
    aext[cells:, left] = edges(1, 0)
    zero = jnp.zeros((2, C), F32)
    wide = act_tangent.astype(F32)
    aext[cells:, right] = jnp.concatenate([wide[:, F - 1], zero, wide[:, 0], zero], axis=0).astype(BF)
    second = dot_t(aext[...], ts[...])
    for k in range(9):
        gsum[k * C : k * C + C] = second[0:C, k * C : k * C + C]
        gsum[K9 + k * C : K9 + k * C + C] = second[C : 2 * C, k * C : k * C + C]

    @pl.when(ishub)
    def _():
        more = dot_t(aext[0:cells], tx[...])
        for k in range(9):
            gsum[k * C : k * C + C] += more[0:C, k * C : k * C + C]
            gsum[K9 + k * C : K9 + k * C + C] += more[C : 2 * C, k * C : k * C + C]

    shard, p0, p1, qn = split_rows(ny, nz)
    qoff = p0 + p1 + qn * core
    qother = p0 + p1 + qn * (1 - core)
    def by_core(fn):
        @pl.when(core == 0)
        def _():
            fn(0, p0, p0, p1)

        @pl.when(core == 1)
        def _():
            fn(p0, p1, 0, p0)

    def ar(name, src, dst, p, extra=None):
        at = STEPS.index(name)
        return rcopy(src, dst, ar_s.at[at], ar_r.at[at if extra is None else len(STEPS) + extra], p)

    def sent(name, src):
        ar(name, src, src, partner).wait_send()

    def arrived(name, dst):
        ar(name, dst, dst, partner).wait_recv()

    ypeers = [ypeer(d) for d in sorted(range(1, ny), key=lambda d: -min(d, ny - d))]
    zpeers = [zpeer(d) for d in sorted(range(1, nz), key=lambda d: -min(d, nz - d))]
    hy = ny // 2

    def rows_of(h):
        return pl.ds(h * hy, hy)

    def core_p(h, off, size):
        at = (rows_of(h), slice(None), pl.ds(off, size))
        return ar(("cp0", "cp1")[h], gs.at[at], gr.at[at], partner)

    def core_q(h, o):
        at = (rows_of(h), slice(None), pl.ds(o, qn))
        return ar(("cq0", "cq1")[h], gs.at[at], gr.at[at], partner)

    def swap_cores(h):
        half = gsum[h * 2 * K9 : (h + 1) * 2 * K9]
        gs[h * hy : (h + 1) * hy] = half.astype(BF).reshape(hy, nz, shard, C)
        core_q(h, qother).start()
        by_core(lambda off, size, ooff, osize: core_p(h, ooff, osize).start())

    def own_half(h, off, size):
        half = gsum[h * 2 * K9 : (h + 1) * 2 * K9].reshape(hy, nz, shard, C)
        return half[:, :, off : off + size] + gr[h * hy : (h + 1) * hy, :, off : off + size].astype(F32)

    def q1(h, d):
        q, p = zpeers[d]
        return ar("q1", qs.at[rows_of(h), q], qr.at[z, rows_of(h)], p)

    def p1_copy(d, size):
        q, p = ypeers[d]
        return ar("p1", ps.at[q, :, pl.ds(0, size)], pr.at[y, :, pl.ds(0, size)], p)

    def first_step(h):
        rows = slice(h * hy, (h + 1) * hy)
        core_q(h, qother).wait_send()
        core_q(h, qoff).wait_recv()

        def stage(qo):
            part = own_half(h, qo, qn)
            qf[rows] = part
            qs[rows] = part.astype(BF)

        by_core(lambda off, size, ooff, osize: stage(p0 + p1 if off == 0 else p0 + p1 + qn))
        for d in range(nz - 1):
            q1(h, d).start()

        def stage(off, size, ooff, osize):
            core_p(h, ooff, osize).wait_send()
            core_p(h, off, size).wait_recv()
            part = own_half(h, off, size)
            pf[rows, :, 0:size] = part
            ps[rows, :, 0:size] = part.astype(BF)
            for d in range(ny - 1):

                @pl.when(lax.div(ypeers[d][0], hy) == h)
                def _():
                    p1_copy(d, size).start()

        by_core(stage)

    swap_cores(0)
    for i, lanes in ((1, left), (2, right)):
        pext[0:cells, lanes] = rb[1, i, 1].reshape(cells, C)
        pext[cells:, lanes] = edges(1, i)
    first = dot_t(tu[...], pext[...])
    gsum[2 * K9 : 3 * K9] = first[:, 0:C]
    gsum[3 * K9 : 4 * K9] = first[:, C : 2 * C] + dot_t(tv[...], pext[:, left])
    swap_cores(1)
    first_step(0)
    first_step(1)
    prepare(1)
    send(1)
    send_rows(1, (1,))

    def p2_copy(d, size):
        q, p = zpeers[d]
        return ar("p2", pz.at[q, pl.ds(0, size)], pzr.at[z, pl.ds(0, size)], p)

    def stage(off, size, ooff, osize):
        arrived("p1", pr.at[pl.ds(0, ny - 1), :, pl.ds(0, size)])
        part = pf[y, :, 0:size]
        for q, p in ypeers:
            part = part + pr[q, :, 0:size].astype(F32)
        pzf[:, 0:size] = part
        pz[:, 0:size] = part.astype(BF)
        for d in range(nz - 1):
            p2_copy(d, size).start()

    by_core(stage)

    def q2(d):
        q, p = ypeers[d]
        return ar("q2", qy.at[q], qyr.at[y], p)

    arrived("q1", qr.at[pl.ds(0, nz - 1)])
    part = qf[:, z]
    for q, p in zpeers:
        part = part + qr[q].astype(F32)
    qyf[...] = part
    qy[...] = part.astype(BF)
    for d in range(ny - 1):
        q2(d).start()
    send_rows(1, (2,))

    scale = 1.0 / F

    def p3(d, size, off):
        q, p = zpeers[d]
        return ar("p3", fin_p.at[pl.ds(0, size)], out_ref.at[y, z, pl.ds(off, size)], p)

    def own_p(size, off):
        return pltpu.make_async_copy(fin_p.at[pl.ds(0, size)], out_ref.at[y, z, pl.ds(off, size)], osem.at[3])

    own_q = pltpu.make_async_copy(fin_q, out_ref.at[y, z, pl.ds(qoff, qn)], osem.at[4])

    def stage(off, size, ooff, osize):
        arrived("p2", pzr.at[pl.ds(0, nz - 1), pl.ds(0, size)])
        part = pzf[z, 0:size]
        for q, p in zpeers:
            part = part + pzr[q, 0:size].astype(F32)
        fin_p[0:size] = (part * scale).astype(BF)
        own_p(size, off).start()
        for d in range(nz - 1):
            p3(d, size, off).start()

    by_core(stage)

    def q3(d):
        q, p = ypeers[d]
        return ar("q3", fin_q, out_ref.at[y, z, pl.ds(qoff, qn)], p)

    arrived("q2", qyr.at[pl.ds(0, ny - 1)])
    part = qyf[y]
    for q, p in ypeers:
        part = part + qyr[q].astype(F32)
    fin_q[...] = (part * scale).astype(BF)
    own_q.start()
    for d in range(ny - 1):
        q3(d).start()
    for q, p in zpeers:
        ar("q4", fin_q, out_ref.at[y, z, pl.ds(qoff, qn)], p, ny + z).start()

    outs = [pltpu.make_async_copy(res.at[i], ref, osem.at[i]) for i, ref in enumerate((next_ref, adj_ref, adt_ref))]

    for i in range(3):
        hand_row(1, i)
    margins(1)
    hub_wait(1)
    for i in range(3):
        receive_row(1, i)
        hub_row(1, i, i > 0)
    for a in range(3):
        row_taps(1, 0, a, tu, False, 1.0)
    field[:, :, left] = dot(tu[0:cells], wraw[2]).reshape(6, F, C)

    def p4(d, size, off, out):
        q, p = ypeers[d]
        qq = y if out else q
        ref = out_ref.at[qq, :, pl.ds(off, size)]
        return ar("p4", ref, ref, p, qq)

    def cpy_p(q, size, off):
        ref = out_ref.at[q, :, pl.ds(off, size)]
        return ar("c4", ref, ref, partner)

    def stage(off, size, ooff, osize):
        arrived("p3", out_ref.at[y, pl.ds(0, nz - 1), pl.ds(off, size)])
        own_p(size, off).wait()
        for d in range(ny - 1):
            p4(d, size, off, True).start()
        cpy_p(y, size, off).start()

    by_core(stage)

    def q4_in(q):
        ref = out_ref.at[:, q, pl.ds(qoff, qn)]
        return ar("q4", ref, ref, partner, ny + q)

    def q4_rest(d, qq):
        ref = out_ref.at[qq, z, pl.ds(qoff, qn)]
        return ar("q4", ref, ref, zpeers[d][1], ny + z)

    def cpy_q(q, o):
        ref = out_ref.at[:, q, pl.ds(o, qn)]
        return ar("d4", ref, ref, partner)

    arrived("q3", out_ref.at[pl.ds(0, ny - 1), z, pl.ds(qoff, qn)])
    own_q.wait()
    for d in range(nz - 1):
        for q, p in ypeers:
            q4_rest(d, q).start()
    cpy_q(z, qoff).start()

    receive_margins(1)
    forward_sides(1, 0, tu)
    add_sides(field, left, dot(tu[cells:], wraw[2]))
    res[0] = (rb[0, 0, 1].astype(F32) + 0.5 * field[:, :, left]).astype(BF)
    outs[0].start()

    def adjoint_of(i, dst, weights, ref, lanes):
        for a in range(3):
            row_taps(1, i, a, dst, True, 1.0)
        spread_sides(1, i, dst, 1.0)
        main_spread(1, i, dst, tx, weights, 1.0, ref, lanes)
        add_sides(ref, lanes, dot(dst[cells:], weights))

    adjoint_of(1, ts, ws1[...], front, both)
    res[1] = (rb[0, 2, 1].astype(F32) + front[:, :, left]).astype(BF)
    outs[1].start()

    adjoint_of(2, ts, ws1[:, 0:C], field, left)
    res[2] = (front[:, :, right] + field[:, :, left]).astype(BF)
    outs[2].start()

    def stage(off, size, ooff, osize):
        for d in range(ny - 1):
            p4(d, size, off, False).wait_recv()
            cpy_p(ypeers[d][0], size, off).start()

    by_core(stage)
    for d in range(nz - 1):
        q4_in(zpeers[d][0]).wait_recv()
        cpy_q(zpeers[d][0], qoff).start()

    def stage(off, size, ooff, osize):
        sent("p1", pr.at[pl.ds(0, ny - 1), :, pl.ds(0, size)])
        sent("p2", pzr.at[pl.ds(0, nz - 1), pl.ds(0, size)])
        sent("p3", out_ref.at[y, pl.ds(0, nz - 1), pl.ds(off, size)])
        sent("p4", out_ref.at[pl.ds(0, ny - 1), :, pl.ds(off, size)])
        sent("c4", out_ref.at[:, :, pl.ds(off, size)])
        arrived("c4", out_ref.at[:, :, pl.ds(ooff, osize)])

    by_core(stage)
    sent("q1", qr.at[pl.ds(0, nz - 1)])
    sent("q2", qyr.at[pl.ds(0, ny - 1)])
    sent("q3", out_ref.at[pl.ds(0, ny - 1), z, pl.ds(qoff, qn)])
    sent("q4", out_ref.at[:, pl.ds(0, nz - 1), pl.ds(qoff, qn)])
    sent("d4", out_ref.at[:, :, pl.ds(qoff, qn)])
    arrived("d4", out_ref.at[:, :, pl.ds(qother, qn)])
    for cp in outs:
        cp.wait()
    for ph in range(2):
        finish_sends(ph)
        finish_rows(ph)


STEPS = ("cp0", "cq0", "cp1", "cq1", "q1", "p1", "p2", "q2", "p3", "q3", "p4", "c4", "q4", "d4")


def split_rows(ny, nz):
    tiles = 4 * K9 // (16 * ny * nz)
    qn = 2 * tiles // 9
    p1 = (tiles - 2 * qn) // 2
    return 16 * tiles, 16 * (tiles - 2 * qn - p1), 16 * p1, 16 * qn


CHUNKS = 8


def finish(n_ref, a_ref, t_ref, g_ref, n_out, a_out, t_out, w_out, h_out, packed, wide, held, in_sem, out_sem, row_in, row_out):
    size = packed.shape[1]
    row_ins = [pltpu.make_async_copy(src, held.at[i], row_in.at[i]) for i, src in enumerate((n_ref, a_ref, t_ref))]
    row_outs = [pltpu.make_async_copy(held.at[i], dst, row_out.at[i]) for i, dst in enumerate((n_out, a_out, t_out))]
    quarter = CHUNKS // 4
    ins = [pltpu.make_async_copy(g_ref.at[pl.ds(i * size, size)], packed.at[i], in_sem.at[i]) for i in range(CHUNKS)]
    outs = [
        pltpu.make_async_copy(
            wide.at[i],
            (w_out, h_out)[i // quarter % 2].at[pl.ds((i % quarter + (quarter if i < 2 * quarter else 0)) * size, size)],
            out_sem.at[i],
        )
        for i in range(CHUNKS)
    ]
    for cp in ins + row_ins:
        cp.start()
    for i in range(CHUNKS):
        ins[i].wait()
        wide[i] = packed[i].astype(F32)
        outs[i].start()
    for i in range(3):
        row_ins[i].wait()
        row_outs[i].start()
    for cp in outs + row_outs:
        cp.wait()


def on_device(n, ny, nz, u, v, c, w1, w2, t1, t2, nb):
    F = n
    cells = 6 * F
    shard, p0, p1, qn = split_rows(ny, nz)
    u, v, c = (a.reshape(6, F, C) for a in (u, v, c))
    w1, w2, t1, t2 = (a.reshape(K9, C) for a in (w1, w2, t1, t2))
    vm = pltpu.VMEM
    dma = pltpu.SemaphoreType.DMA
    anywhere = pl.BlockSpec(memory_space=pl.ANY)
    inside = pl.BlockSpec(memory_space=pltpu.VMEM)
    row = jax.ShapeDtypeStruct((6, F, C), BF)
    nxt, adj, adt, out = pl.pallas_call(
        functools.partial(kernel, n, ny, nz),
        out_shape=(row, row, row, jax.ShapeDtypeStruct((ny, nz, shard, C), BF)),
        in_specs=[anywhere] * 8,
        out_specs=(anywhere,) * 4,
        scratch_shapes=[
            vm((2, 3, 3, 6, F, C), BF),
            vm((2, 3, 6, F, C), BF),
            vm((2, 160, C), BF),
            vm((2, 64, C), BF),
            vm((2, F, 32, C), BF),
            vm((2, F, 32, C), BF),
            vm((2, 3, 48, C), BF),
            vm((48, 160), BF),
            vm((64, 48), BF),
            vm((8 * F, cells), BF),
            vm((cells, 8 * F), BF),
            vm((cells, cells), BF),
            vm((cells, cells), BF),
            vm((4, K9, C), BF),
            vm((K9, 2 * C), BF),
            vm((K9, 2 * C), BF),
            vm((K9, 2 * C), BF),
            vm((6, F + 16, C), F32),
            vm((cells + SIDES, K9), BF),
            vm((cells + SIDES, K9), BF),
            vm((cells + SIDES, K9), BF),
            vm((cells, K9), BF),
            vm((cells + SIDES, 2 * C), BF),
            vm((cells + SIDES, 2 * C), BF),
            vm((6, F, 2 * C), F32),
            vm((6, F, 2 * C), F32),
            vm((4 * K9, C), F32),
            vm((ny, nz, shard, C), BF),
            vm((ny, nz, shard, C), BF),
            vm((ny, nz, p0, C), F32),
            vm((ny, nz, p0, C), BF),
            vm((ny, nz, p0, C), BF),
            vm((ny, nz, qn, C), F32),
            vm((ny, nz, qn, C), BF),
            vm((nz, ny, qn, C), BF),
            vm((nz, p0, C), BF),
            vm((nz, p0, C), F32),
            vm((nz, p0, C), BF),
            vm((ny, qn, C), BF),
            vm((ny, qn, C), F32),
            vm((ny, qn, C), BF),
            pltpu.SMEM((4, 6), jnp.int32),
            vm((3, 6, F, C), BF),
            vm((p0, C), BF),
            vm((qn, C), BF),
            dma((5,)),
            dma((8,)),
            dma((2, 3)),
            dma((2, 3, 2)),
            dma((2,)),
            dma((2,)),
            dma((2, 2)),
            dma((2,)),
            dma((2,)),
            dma((2, 2)),
            dma((2, 2)),
            dma((2, 2)),
            dma((len(STEPS),)),
            dma((len(STEPS) + ny + nz,)),
        ],
        compiler_params=pltpu.CompilerParams(
            collective_id=0, has_side_effects=True, vmem_limit_bytes=56 * 2**20
        ),
    )(u, v, c, w1, w2, t1, t2, nb.T)
    half = 2 * K9
    grad = jax.ShapeDtypeStruct((half, C), F32)
    nxt, adj, adt, wg, hp = pl.pallas_call(
        finish,
        out_shape=(row, row, row, grad, grad),
        in_specs=[anywhere] * 4,
        out_specs=(anywhere,) * 5,
        scratch_shapes=[vm((CHUNKS, 2 * half // CHUNKS, C), BF), vm((CHUNKS, 2 * half // CHUNKS, C), F32), vm((3, 6, F, C), BF), dma((CHUNKS,)), dma((CHUNKS,)), dma((3,)), dma((3,))],
        compiler_params=pltpu.CompilerParams(vmem_limit_bytes=56 * 2**20),
    )(nxt, adj, adt, out.reshape(2 * half, C))
    shape4 = (2, 9, C, C)
    shape = (6, 1, F, C)
    return nxt.reshape(shape), adj.reshape(shape), adt.reshape(shape), wg.reshape(shape4), hp.reshape(shape4)


def solution(mesh):
    n = mesh.shape["tile"] * mesh.shape["sub"]
    nz = 8 if n == 64 else 2
    ny = n // (2 * nz)
    field = P("rep", ("tile", "sub"), None, None)
    grads = P("rep", None, None, None)
    return jax.shard_map(
        functools.partial(on_device, n, ny, nz),
        mesh=mesh,
        in_specs=(field, field, field, P(), P(), P(), P(), P()),
        out_specs=(field, field, field, grads, grads),
        check_vma=False,
    )
```

```python
import functools

import jax
import jax.numpy as jnp
from jax import lax
from jax.experimental import pallas as pl
from jax.experimental.pallas import tpu as pltpu
from jax.sharding import PartitionSpec as P

MESH = pl.DeviceIdType.MESH
BF = jnp.bfloat16
F32 = jnp.float32
C = 128
K9 = 9 * C
SIDES = 16


def dot(a, b):
    return jnp.dot(a, b, preferred_element_type=F32)


def dot_t(a, b):
    return lax.dot_general(a, b, (((0,), (0,)), ((), ())), preferred_element_type=F32)


def iota(shape, dim):
    return lax.broadcasted_iota(jnp.int32, shape, dim)


def onehot(mask):
    return jnp.where(mask, 1.0, 0.0).astype(BF)


def kernel(
    n,
    ny,
    nz,
    u_ref,
    v_ref,
    c_ref,
    w1_ref,
    w2_ref,
    t1_ref,
    t2_ref,
    nb_ref,
    next_ref,
    adj_ref,
    adt_ref,
    out_ref,
    rb,
    mb,
    ebuf,
    hm,
    zs,
    rx,
    mt,
    sel,
    selh,
    amat,
    bmat,
    c0mat,
    c2mat,
    wraw,
    wf1,
    ws1,
    ws2,
    padz,
    tu,
    tv,
    ts,
    tx,
    aext,
    pext,
    front,
    field,
    gsum,
    gs,
    gr,
    pf,
    ps,
    pr,
    qf,
    qs,
    qr,
    pz,
    pzf,
    pzr,
    qy,
    qyf,
    qyr,
    nbm,
    res,
    fin_p,
    fin_q,
    osem,
    lsem,
    bulk_s,
    bulk_r,
    e_s,
    e_r,
    hm_s,
    rx_r,
    z_s,
    z_r,
    mt_s,
    mt_r,
    ar_s,
    ar_r,
):
    F = n
    cells = 6 * F
    rep = lax.axis_index("rep")
    r = lax.axis_index("tile") * 2 + lax.axis_index("sub")
    core = lax.rem(lax.div(r, 2), 2)
    z = lax.rem(lax.div(r, 4), nz)
    yhi = lax.div(r, 4 * nz)
    ylo = lax.rem(r, 2)
    y = yhi * 2 + ylo

    def dev(p):
        return (lax.div(p, 2), lax.rem(p, 2), rep)

    def make(hi, zc, co, lo):
        return ((hi * nz + zc) * 2 + co) * 2 + lo

    up = lax.rem(r + n - 1, n)
    dn = lax.rem(r + 1, n)
    mirror = n - 1 - r
    odd = lax.rem(r, 2)
    beside = r + 1 - 2 * odd
    beyond = lax.rem(r + n - 1 + 2 * odd, n)
    outer = jnp.logical_or(lax.rem(r, 4) == 0, lax.rem(r, 4) == 3)
    slot_in = 2 - 2 * odd
    slot_out = 2 * odd
    partner = make(yhi, z, 1 - core, ylo)

    def ypeer(d):
        q = lax.rem(y + d, ny)
        return q, make(lax.div(q, 2), z, core, lax.rem(q, 2))

    def zpeer(d):
        q = lax.rem(z + d, nz)
        return q, make(yhi, q, core, ylo)

    is0 = r == 0
    is1 = r == n - 1
    ishub = jnp.logical_or(is0, is1)

    def rcopy(src, dst, ssem, rsem, p):
        return pltpu.make_async_remote_copy(
            src_ref=src,
            dst_ref=dst,
            send_sem=ssem,
            recv_sem=rsem,
            device_id=dev(p),
            device_id_type=MESH,
        )

    nbload = pltpu.make_async_copy(nb_ref, nbm, lsem.at[7])
    nbload.start()
    loads = [pltpu.make_async_copy(ref, rb.at[0, i, 1], lsem.at[i]) for i, ref in enumerate((u_ref, v_ref, c_ref))]
    wloads = [pltpu.make_async_copy(ref, wraw.at[i], lsem.at[3 + i]) for i, ref in enumerate((w1_ref, t1_ref, w2_ref, t2_ref))]
    for cp in loads + wloads:
        cp.start()

    barrier = pltpu.get_barrier_semaphore()

    def greet(p):
        pl.semaphore_signal(barrier, inc=1, device_id=dev(p), device_id_type=MESH)

    @pl.when(ishub)
    def _():
        def body(i, carry):
            greet(lax.rem(r + i, n))
            return carry

        lax.fori_loop(1, n, body, 0)

    @pl.when(r != 0)
    def _():
        greet(0)

    @pl.when(r != n - 1)
    def _():
        greet(n - 1)

    for p in (up, dn, mirror, partner):
        greet(p)
    for d in range(1, ny):
        greet(ypeer(d)[1])
    for d in range(1, nz):
        greet(zpeer(d)[1])

    nbload.wait()
    nbs = [[nbm[s, f] for s in range(4)] for f in range(6)]
    x = iota((48, 160), 0)
    yy = iota((48, 160), 1)
    xs = x & 15
    xsd = jnp.where(xs < 8, 1, 3)
    xnb = jnp.full((48, 160), -1, jnp.int32)
    for f in range(6):
        xnb = jnp.where(xs == f, nbs[f][1], xnb)
        xnb = jnp.where(xs == 8 + f, nbs[f][3], xnb)
    ym = jnp.where(yy >= 48, yy - 48, yy)
    ysd = jnp.where((ym & 15) < 8, 1, 3)
    yz = (yy - 96) & 31
    isz = yy >= 96
    yg = jnp.where(isz, yz & 7, ym & 7)
    yt = jnp.where(isz, jnp.where(yy >= 128, 2, 0), ysd)
    yfield = jnp.where(isz, yz >> 3, ym >> 4)
    way = jnp.where(isz, 1, jnp.where(yy >= 48, jnp.where(xsd == ysd, 1, 0), jnp.where(xsd == ysd, 0, 1)))
    sel[...] = onehot((xnb == 4 * yg + yt) & ((x >> 4) == yfield) & (yg < 6) & (way == 1))
    x = iota((64, 48), 0)
    yy = iota((64, 48), 1)
    xnb = jnp.full((64, 48), -1, jnp.int32)
    for f in range(6):
        xnb = jnp.where((x & 7) == f, jnp.where(x < 32, nbs[f][0], nbs[f][2]), xnb)
    yt = jnp.where((yy & 15) < 8, 1, 3)
    selh[...] = onehot((xnb == 4 * (yy & 7) + yt) & (((x & 31) >> 3) == (yy >> 4)) & ((yy & 7) < 6))

    def chosen(s, code, offset):
        t = code & 3
        flipped = (s < 2) == (t < 2)
        along = jnp.where(flipped, 1 - offset, offset - 1)
        row_tap = jnp.where(t == 0, 0, jnp.where(t == 2, 2, 1 - along))
        col_tap = jnp.where(t == 1, 2, jnp.where(t == 3, 0, 1 - along))
        return 3 * row_tap + col_tap

    xs = iota((SIDES, C), 0)
    code = jnp.full((SIDES, C), 0, jnp.int32)
    for f in range(6):
        code = jnp.where(xs == f, nbs[f][1], code)
        code = jnp.where(xs == 8 + f, nbs[f][3], code)
    side_taps = [chosen(jnp.where(xs < 8, 1, 3), code, o) for o in range(3)]

    hub_side = jnp.where(is0, 0, 2)
    hub_nb = [jnp.where(is0, nbs[f][0], nbs[f][2]) for f in range(6)]
    hub_flip = [((hub_side < 2) == ((code_f & 3) < 2)).astype(jnp.int32) for code_f in hub_nb]

    def per_face(face, values, start):
        result = jnp.full(face.shape, start, jnp.int32)
        for f in range(6):
            result = jnp.where(face == f, values[f], result)
        return result

    @pl.when(ishub)
    def _():
        a = iota((8 * F, cells), 0)
        b = iota((8 * F, cells), 1)
        g = a & 7
        pos = a >> 3
        target = g * F + jnp.where(per_face(g, hub_flip, 0) == 1, F - 1 - pos, pos)
        amat[...] = onehot((b == target) & (g < 6))

    def edges(ph, i):
        row = rb[ph, i, 1].astype(F32)
        zero = jnp.zeros((2, C), F32)
        return jnp.concatenate([row[:, F - 1], zero, row[:, 0], zero], axis=0).astype(BF)

    def prepare(ph):
        for i in range(3):
            ebuf[ph, 16 * i : 16 * i + 16] = edges(ph, i)
        hm[ph] = dot(selh[...], ebuf[ph, 0:48]).astype(BF)

        @pl.when(ishub)
        def _():
            parts = []
            for i in range(3):
                parts.append(dot(amat[...], rb[ph, i, 1].reshape(cells, C)).reshape(F, 8, C))
            parts.append(jnp.zeros((F, 8, C), F32))
            zs[ph] = jnp.concatenate(parts, axis=1).astype(BF)

        @pl.when(is0)
        def _():
            rx[ph, 0] = hm[ph, 0:32]
            ebuf[ph, 96:128] = zs[ph, 0]

        @pl.when(is1)
        def _():
            rx[ph, n - 1] = hm[ph, 32:64]
            ebuf[ph, 128:160] = zs[ph, n - 1]

    def e_copy(ph):
        return rcopy(ebuf.at[ph, pl.ds(0, 48)], ebuf.at[ph, pl.ds(48, 48)], e_s.at[ph], e_r.at[ph], mirror)

    def hm_copy(ph, h):
        return rcopy(
            hm.at[ph, pl.ds(32 * h, 32)],
            rx.at[ph, r],
            hm_s.at[ph, h],
            rx_r.at[ph],
            (n - 1) * h,
        )

    def z_copy(ph, h, p):
        return rcopy(zs.at[ph, p], ebuf.at[ph, pl.ds(96 + 32 * h, 32)], z_s.at[ph], z_r.at[ph, h], p)

    def row_beside(ph, i, out):
        slot = slot_out if out else slot_in
        return rcopy(rb.at[ph, i, 1], rb.at[ph, i, slot], bulk_s.at[ph, 0], bulk_r.at[ph, i, 0], beside)

    def row_beyond(ph, i, out):
        slot = slot_in if out else slot_out
        return rcopy(rb.at[ph, i, 1], rb.at[ph, i, slot], bulk_s.at[ph, 1], bulk_r.at[ph, i, 1], beyond)

    def row_inward(ph, i):
        return rcopy(rb.at[ph, i, slot_in], rb.at[ph, i, slot_out], bulk_s.at[ph, 2], bulk_r.at[ph, i, 1], partner)

    def send_rows(ph, fields=(0, 1, 2)):
        for i in fields:
            row_beside(ph, i, True).start()

            @pl.when(outer)
            def _():
                row_beyond(ph, i, True).start()

    def hand_row(ph, i):
        @pl.when(outer)
        def _():
            row_beside(ph, i, False).wait_recv()
            row_inward(ph, i).start()

    def receive_row(ph, i):
        @pl.when(jnp.logical_not(outer))
        def _():
            row_beside(ph, i, False).wait_recv()

        row_beyond(ph, i, False).wait_recv()

    def finish_rows(ph):
        three = rb.at[ph, :, 1]

        def sent(kind):
            rcopy(three, three, bulk_s.at[ph, kind], bulk_r.at[ph, 0, 0], beside).wait_send()

        sent(0)

        @pl.when(outer)
        def _():
            sent(1)
            sent(2)

    def mt_copy(ph, way):
        return rcopy(
            mt.at[ph, 1],
            mt.at[ph, 2 if way == 0 else 0],
            mt_s.at[ph, way],
            mt_r.at[ph, way],
            up if way == 0 else dn,
        )

    def hub_loop(step):
        def body(i, carry):
            step(lax.rem(r + i, n))
            return carry

        lax.fori_loop(1, n, body, 0)

    def send(ph):
        for h, here in ((0, is0), (1, is1)):

            @pl.when(here)
            def _():
                hub_loop(lambda p: z_copy(ph, h, p).start())

            @pl.when(jnp.logical_not(here))
            def _():
                hm_copy(ph, h).start()

        e_copy(ph).start()

    def margins(ph):
        e_copy(ph).wait()
        for h, here in ((0, is0), (1, is1)):

            @pl.when(jnp.logical_not(here))
            def _():
                z_copy(ph, h, 0).wait_recv()

        mt[ph, 1] = dot(sel[...], ebuf[ph]).astype(BF)
        for way in range(2):
            mt_copy(ph, way).start()

    def hub_wait(ph):
        @pl.when(ishub)
        def _():
            start = jnp.where(is0, 1, 0)
            rcopy(zs.at[ph, pl.ds(0, n - 1)], rx.at[ph, pl.ds(start, n - 1)], z_s.at[ph], rx_r.at[ph], mirror).wait_recv()

    def hub_row(ph, i, spreads):
        @pl.when(ishub)
        def _():
            slot = jnp.where(is0, 0, 2)
            piece = rx[ph].astype(F32)[:, 8 * i : 8 * i + 8].reshape(8 * F, C).astype(BF)
            row = dot(bmat[...], piece)
            row = row + dot(c0mat[...], rb[ph, i, 1].reshape(cells, C))
            row = row + dot(c2mat[...], rb[ph, i, slot].reshape(cells, C))
            row = row.astype(BF).reshape(6, F, C)
            if spreads:
                mb[ph, i] = row
                rb[ph, i, slot] = jnp.zeros((6, F, C), BF)
            else:
                rb[ph, i, slot] = row

    def receive_margins(ph):
        for way in range(2):
            mt_copy(ph, way).wait()

        @pl.when(is0)
        def _():
            mt[ph, 0] = jnp.zeros((48, C), BF)

        @pl.when(is1)
        def _():
            mt[ph, 2] = jnp.zeros((48, C), BF)

    def finish_sends(ph):
        for h, here in ((0, is0), (1, is1)):

            @pl.when(here)
            def _():
                rcopy(zs.at[ph, pl.ds(0, n - 1)], rx.at[ph, pl.ds(0, n - 1)], z_s.at[ph], rx_r.at[ph], mirror).wait_send()

            @pl.when(jnp.logical_not(here))
            def _():
                hm_copy(ph, h).wait_send()

    def row_taps(ph, i, a, dst, spreads, scale):
        padz[:, 8 : 8 + F] = rb[ph, i, a].astype(F32) * scale
        for b in range(3):
            k = 3 * a + b
            k = 8 - k if spreads else k
            dst[0:cells, k * C : k * C + C] = padz[:, 7 + b : 7 + b + F].reshape(cells, C).astype(BF)

    def forward_sides(ph, i, dst):
        for a in range(3):
            line = mt[ph, a, 16 * i : 16 * i + 16].astype(F32)
            zero = jnp.zeros((SIDES, C), F32)
            for b, part in enumerate((jnp.where(xs < 8, zero, line), zero, jnp.where(xs < 8, line, zero))):
                k = 3 * a + b
                dst[cells : cells + SIDES, k * C : k * C + C] = part.astype(BF)

    def spread_sides(ph, i, dst, scale):
        lines = [mt[ph, o, 16 * i : 16 * i + 16].astype(F32) * scale for o in range(3)]
        for k in range(9):
            total = jnp.zeros((SIDES, C), F32)
            for o in range(3):
                total = jnp.where(side_taps[o] == k, lines[o], total)
            dst[cells : cells + SIDES, k * C : k * C + C] = total.astype(BF)

    def hub_taps(ph, i, extra, scale):
        padz[:, 8 : 8 + F] = mb[ph, i].astype(F32) * scale
        for f in range(6):
            picks = [chosen(hub_side, hub_nb[f], o) for o in range(3)]
            shifted = [padz[f, 7 + o : 7 + o + F] for o in range(3)]
            for k in range(9):
                total = jnp.zeros((F, C), F32)
                for o in range(3):
                    total = jnp.where(picks[o] == k, shifted[o], total)
                extra[f * F : f * F + F, k * C : k * C + C] = total.astype(BF)

    def add_sides(ref, lanes, side):
        for f in range(6):
            ref[f, F - 1 : F, lanes] += side[f : f + 1]
            ref[f, 0:1, lanes] += side[8 + f : 9 + f]

    def main_spread(ph, i, dst, extra, weights, scale, ref, lanes):
        width = lanes.stop - lanes.start
        ref[:, :, lanes] = dot(dst[0:cells], weights).reshape(6, F, width)

        @pl.when(ishub)
        def _():
            hub_taps(ph, i, extra, scale)
            ref[:, :, lanes] += dot(extra[...], weights).reshape(6, F, width)

    for cp in loads:
        cp.wait()
    prepare(0)
    base = 4 + (ny - 1) + (nz - 1)
    pl.semaphore_wait(barrier, base + 2 + jnp.where(ishub, n - 2, 0))
    send(0)
    send_rows(0)

    padz[...] = jnp.zeros(padz.shape, F32)
    for cp in wloads:
        cp.wait()
    wf1[:, 0:C] = wraw[0]
    wf1[:, C : 2 * C] = wraw[1]
    for k in range(9):
        rows = slice(k * C, k * C + C)
        ws1[rows, 0:C] = wraw[0, rows].astype(F32).T.astype(BF)
        ws1[rows, C : 2 * C] = wraw[1, rows].astype(F32).T.astype(BF)
        ws2[rows, 0:C] = wraw[2, rows].astype(F32).T.astype(BF)
        ws2[rows, C : 2 * C] = wraw[3, rows].astype(F32).T.astype(BF)

    @pl.when(ishub)
    def _():
        a = iota((cells, 8 * F), 0)
        b = iota((cells, 8 * F), 1)
        face = lax.div(a, F)
        pos = a - face * F
        pos = jnp.where(per_face(face, hub_flip, 0) == 1, F - 1 - pos, pos)
        column = per_face(face, [code_f & 1 for code_f in hub_nb], 0)
        bmat[...] = onehot((b == 8 * pos + face) & (column == 1))
        a = iota((cells, cells), 0)
        b = iota((cells, cells), 1)
        face = lax.div(a, F)
        pos = a - face * F
        code_a = per_face(face, hub_nb, 0)
        other = (code_a >> 2) * F
        c0mat[...] = onehot(((code_a & 3) == hub_side) & (b == other + F - 1 - pos))
        c2mat[...] = onehot(((code_a & 3) == 2 - hub_side) & (b == other + pos))

    inputs = ((0, tu, False, 1.0), (1, tv, False, 1.0), (2, ts, True, 0.5))
    for i, dst, spreads, scale in inputs:
        row_taps(0, i, 1, dst, spreads, scale)
    both = slice(0, 2 * C)
    left = slice(0, C)
    right = slice(C, 2 * C)

    def field_rows(i):
        receive_row(0, i)
        _, dst, spreads, scale = inputs[i]
        hub_row(0, i, spreads)
        row_taps(0, i, 0, dst, spreads, scale)
        row_taps(0, i, 2, dst, spreads, scale)

    hand_row(0, 0)
    margins(0)
    hand_row(0, 1)
    hub_wait(0)
    field_rows(0)
    front[...] = dot(tu[0:cells], wf1[...]).reshape(6, F, 2 * C)
    hand_row(0, 2)
    field_rows(1)
    front[:, :, right] += dot(tv[0:cells], wraw[0]).reshape(6, F, C)
    field_rows(2)
    main_spread(0, 2, ts, tx, ws2[...], 0.5, field, both)
    receive_margins(0)
    forward_sides(0, 0, tu)
    forward_sides(0, 1, tv)
    spread_sides(0, 2, ts, 0.5)
    side = dot(tu[cells:], wf1[...])
    more = dot(tv[cells:], wraw[0])
    add_sides(front, both, side)
    add_sides(front, right, more)
    add_sides(field, both, dot(ts[cells:], ws2[...]))
    squash = jnp.tanh(front[:, :, left])
    derivative = 1.0 - squash * squash
    hidden_tangent = front[:, :, right]
    act_tangent = (derivative * hidden_tangent).astype(BF)
    backward = field[:, :, left]
    scaled = derivative * backward
    rb[1, 0, 1] = squash.astype(BF)
    rb[1, 1, 1] = scaled.astype(BF)
    rb[1, 2, 1] = (derivative * field[:, :, right] - 2.0 * squash * scaled * hidden_tangent).astype(BF)
    aext[0:cells, right] = act_tangent.reshape(cells, C)

    send_rows(1, (0,))

    aext[0:cells, left] = rb[1, 0, 1].reshape(cells, C)
    aext[cells:, left] = edges(1, 0)
    zero = jnp.zeros((2, C), F32)
    wide = act_tangent.astype(F32)
    aext[cells:, right] = jnp.concatenate([wide[:, F - 1], zero, wide[:, 0], zero], axis=0).astype(BF)
    second = dot_t(aext[...], ts[...])
    for k in range(9):
        gsum[k * C : k * C + C] = second[0:C, k * C : k * C + C]
        gsum[K9 + k * C : K9 + k * C + C] = second[C : 2 * C, k * C : k * C + C]

    @pl.when(ishub)
    def _():
        more = dot_t(aext[0:cells], tx[...])
        for k in range(9):
            gsum[k * C : k * C + C] += more[0:C, k * C : k * C + C]
            gsum[K9 + k * C : K9 + k * C + C] += more[C : 2 * C, k * C : k * C + C]

    shard, p0, p1, qn = split_rows(ny, nz)
    qoff = p0 + p1 + qn * core
    qother = p0 + p1 + qn * (1 - core)
    def by_core(fn):
        @pl.when(core == 0)
        def _():
            fn(0, p0, p0, p1)

        @pl.when(core == 1)
        def _():
            fn(p0, p1, 0, p0)

    def ar(name, src, dst, p, extra=None):
        at = STEPS.index(name)
        return rcopy(src, dst, ar_s.at[at], ar_r.at[at if extra is None else len(STEPS) + extra], p)

    def sent(name, src):
        ar(name, src, src, partner).wait_send()

    def arrived(name, dst):
        ar(name, dst, dst, partner).wait_recv()

    ypeers = [ypeer(d) for d in sorted(range(1, ny), key=lambda d: -min(d, ny - d))]
    zpeers = [zpeer(d) for d in sorted(range(1, nz), key=lambda d: -min(d, nz - d))]
    hy = ny // 2

    def rows_of(h):
        return pl.ds(h * hy, hy)

    def core_p(h, off, size):
        at = (rows_of(h), slice(None), pl.ds(off, size))
        return ar(("cp0", "cp1")[h], gs.at[at], gr.at[at], partner)

    def core_q(h, o):
        at = (rows_of(h), slice(None), pl.ds(o, qn))
        return ar(("cq0", "cq1")[h], gs.at[at], gr.at[at], partner)

    def swap_cores(h):
        half = gsum[h * 2 * K9 : (h + 1) * 2 * K9]
        gs[h * hy : (h + 1) * hy] = half.astype(BF).reshape(hy, nz, shard, C)
        core_q(h, qother).start()
        by_core(lambda off, size, ooff, osize: core_p(h, ooff, osize).start())

    def own_half(h, off, size):
        half = gsum[h * 2 * K9 : (h + 1) * 2 * K9].reshape(hy, nz, shard, C)
        return half[:, :, off : off + size] + gr[h * hy : (h + 1) * hy, :, off : off + size].astype(F32)

    def q1(h, d):
        q, p = zpeers[d]
        return ar("q1", qs.at[rows_of(h), q], qr.at[z, rows_of(h)], p)

    def p1_copy(d, size):
        q, p = ypeers[d]
        return ar("p1", ps.at[q, :, pl.ds(0, size)], pr.at[y, :, pl.ds(0, size)], p)

    def first_step(h):
        rows = slice(h * hy, (h + 1) * hy)
        core_q(h, qother).wait_send()
        core_q(h, qoff).wait_recv()

        def stage(qo):
            part = own_half(h, qo, qn)
            qf[rows] = part
            qs[rows] = part.astype(BF)

        by_core(lambda off, size, ooff, osize: stage(p0 + p1 if off == 0 else p0 + p1 + qn))
        for d in range(nz - 1):
            q1(h, d).start()

        def stage(off, size, ooff, osize):
            core_p(h, ooff, osize).wait_send()
            core_p(h, off, size).wait_recv()
            part = own_half(h, off, size)
            pf[rows, :, 0:size] = part
            ps[rows, :, 0:size] = part.astype(BF)
            for d in range(ny - 1):

                @pl.when(lax.div(ypeers[d][0], hy) == h)
                def _():
                    p1_copy(d, size).start()

        by_core(stage)

    swap_cores(0)
    for i, lanes in ((1, left), (2, right)):
        pext[0:cells, lanes] = rb[1, i, 1].reshape(cells, C)
        pext[cells:, lanes] = edges(1, i)
    first = dot_t(tu[...], pext[...])
    gsum[2 * K9 : 3 * K9] = first[:, 0:C]
    gsum[3 * K9 : 4 * K9] = first[:, C : 2 * C] + dot_t(tv[...], pext[:, left])
    swap_cores(1)
    first_step(0)
    first_step(1)
    prepare(1)
    send(1)

    def p2_copy(d, size):
        q, p = zpeers[d]
        return ar("p2", pz.at[q, pl.ds(0, size)], pzr.at[z, pl.ds(0, size)], p)

    def stage(off, size, ooff, osize):
        arrived("p1", pr.at[pl.ds(0, ny - 1), :, pl.ds(0, size)])
        part = pf[y, :, 0:size]
        for q, p in ypeers:
            part = part + pr[q, :, 0:size].astype(F32)
        pzf[:, 0:size] = part
        pz[:, 0:size] = part.astype(BF)
        for d in range(nz - 1):
            p2_copy(d, size).start()

    by_core(stage)

    def q2(d):
        q, p = ypeers[d]
        return ar("q2", qy.at[q], qyr.at[y], p)

    send_rows(1, (1,))
    arrived("q1", qr.at[pl.ds(0, nz - 1)])
    part = qf[:, z]
    for q, p in zpeers:
        part = part + qr[q].astype(F32)
    qyf[...] = part
    qy[...] = part.astype(BF)
    for d in range(ny - 1):
        q2(d).start()
    send_rows(1, (2,))

    scale = 1.0 / F

    def p3(d, size, off):
        q, p = zpeers[d]
        return ar("p3", fin_p.at[pl.ds(0, size)], out_ref.at[y, z, pl.ds(off, size)], p)

    def own_p(size, off):
        return pltpu.make_async_copy(fin_p.at[pl.ds(0, size)], out_ref.at[y, z, pl.ds(off, size)], osem.at[3])

    own_q = pltpu.make_async_copy(fin_q, out_ref.at[y, z, pl.ds(qoff, qn)], osem.at[4])

    def stage(off, size, ooff, osize):
        arrived("p2", pzr.at[pl.ds(0, nz - 1), pl.ds(0, size)])
        part = pzf[z, 0:size]
        for q, p in zpeers:
            part = part + pzr[q, 0:size].astype(F32)
        fin_p[0:size] = (part * scale).astype(BF)
        own_p(size, off).start()
        for d in range(nz - 1):
            p3(d, size, off).start()
        for q, p in ypeers:
            ar("p4", fin_p.at[pl.ds(0, size)], out_ref.at[y, z, pl.ds(off, size)], p, y).start()

    by_core(stage)

    def q3(d):
        q, p = ypeers[d]
        return ar("q3", fin_q, out_ref.at[y, z, pl.ds(qoff, qn)], p)

    arrived("q2", qyr.at[pl.ds(0, ny - 1)])
    part = qyf[y]
    for q, p in ypeers:
        part = part + qyr[q].astype(F32)
    fin_q[...] = (part * scale).astype(BF)
    own_q.start()
    for d in range(ny - 1):
        q3(d).start()
    for q, p in zpeers:
        ar("q4", fin_q, out_ref.at[y, z, pl.ds(qoff, qn)], p, ny + z).start()

    outs = [pltpu.make_async_copy(res.at[i], ref, osem.at[i]) for i, ref in enumerate((next_ref, adj_ref, adt_ref))]

    for i in range(3):
        hand_row(1, i)
    margins(1)
    hub_wait(1)
    for i in range(3):
        receive_row(1, i)
        hub_row(1, i, i > 0)
    for a in range(3):
        row_taps(1, 0, a, tu, False, 1.0)
    field[:, :, left] = dot(tu[0:cells], wraw[2]).reshape(6, F, C)

    def p4(d, size, off, out):
        q, p = ypeers[d]
        qq = y if out else q
        ref = out_ref.at[qq, :, pl.ds(off, size)]
        return ar("p4", ref, ref, p, qq)

    def cpy_p(q, size, off):
        ref = out_ref.at[q, :, pl.ds(off, size)]
        return ar("c4", ref, ref, partner)

    def stage(off, size, ooff, osize):
        arrived("p3", out_ref.at[y, pl.ds(0, nz - 1), pl.ds(off, size)])
        own_p(size, off).wait()
        for d in range(ny - 1):
            for q, p in zpeers:
                ref = out_ref.at[y, q, pl.ds(off, size)]
                ar("p4", ref, ref, ypeers[d][1], y).start()
        cpy_p(y, size, off).start()

    by_core(stage)

    def q4_in(q):
        ref = out_ref.at[:, q, pl.ds(qoff, qn)]
        return ar("q4", ref, ref, partner, ny + q)

    def q4_rest(d, qq):
        ref = out_ref.at[qq, z, pl.ds(qoff, qn)]
        return ar("q4", ref, ref, zpeers[d][1], ny + z)

    def cpy_q(q, o):
        ref = out_ref.at[:, q, pl.ds(o, qn)]
        return ar("d4", ref, ref, partner)

    arrived("q3", out_ref.at[pl.ds(0, ny - 1), z, pl.ds(qoff, qn)])
    own_q.wait()
    for d in range(nz - 1):
        for q, p in ypeers:
            q4_rest(d, q).start()
    cpy_q(z, qoff).start()

    receive_margins(1)
    forward_sides(1, 0, tu)
    add_sides(field, left, dot(tu[cells:], wraw[2]))
    res[0] = (rb[0, 0, 1].astype(F32) + 0.5 * field[:, :, left]).astype(BF)
    outs[0].start()

    def adjoint_of(i, dst, weights, ref, lanes):
        for a in range(3):
            row_taps(1, i, a, dst, True, 1.0)
        spread_sides(1, i, dst, 1.0)
        main_spread(1, i, dst, tx, weights, 1.0, ref, lanes)
        add_sides(ref, lanes, dot(dst[cells:], weights))

    adjoint_of(1, ts, ws1[...], front, both)
    res[1] = (rb[0, 2, 1].astype(F32) + front[:, :, left]).astype(BF)
    outs[1].start()

    adjoint_of(2, ts, ws1[:, 0:C], field, left)
    res[2] = (front[:, :, right] + field[:, :, left]).astype(BF)
    outs[2].start()

    def stage(off, size, ooff, osize):
        for d in range(ny - 1):
            p4(d, size, off, False).wait_recv()
            cpy_p(ypeers[d][0], size, off).start()

    by_core(stage)
    for d in range(nz - 1):
        q4_in(zpeers[d][0]).wait_recv()
        cpy_q(zpeers[d][0], qoff).start()

    def stage(off, size, ooff, osize):
        sent("p1", pr.at[pl.ds(0, ny - 1), :, pl.ds(0, size)])
        sent("p2", pzr.at[pl.ds(0, nz - 1), pl.ds(0, size)])
        sent("p3", out_ref.at[y, pl.ds(0, nz - 1), pl.ds(off, size)])
        sent("p4", out_ref.at[pl.ds(0, ny - 1), :, pl.ds(off, size)])
        sent("c4", out_ref.at[:, :, pl.ds(off, size)])
        arrived("c4", out_ref.at[:, :, pl.ds(ooff, osize)])

    by_core(stage)
    sent("q1", qr.at[pl.ds(0, nz - 1)])
    sent("q2", qyr.at[pl.ds(0, ny - 1)])
    sent("q3", out_ref.at[pl.ds(0, ny - 1), z, pl.ds(qoff, qn)])
    sent("q4", out_ref.at[:, pl.ds(0, nz - 1), pl.ds(qoff, qn)])
    sent("d4", out_ref.at[:, :, pl.ds(qoff, qn)])
    arrived("d4", out_ref.at[:, :, pl.ds(qother, qn)])
    for cp in outs:
        cp.wait()
    for ph in range(2):
        finish_sends(ph)
        finish_rows(ph)


STEPS = ("cp0", "cq0", "cp1", "cq1", "q1", "p1", "p2", "q2", "p3", "q3", "p4", "c4", "q4", "d4")


def split_rows(ny, nz):
    tiles = 4 * K9 // (16 * ny * nz)
    qn = 2 * tiles // 9
    p1 = (tiles - 2 * qn) // 2
    return 16 * tiles, 16 * (tiles - 2 * qn - p1), 16 * p1, 16 * qn


CHUNKS = 8


def finish(n_ref, a_ref, t_ref, g_ref, n_out, a_out, t_out, w_out, h_out, packed, wide, held, in_sem, out_sem, row_in, row_out):
    size = packed.shape[1]
    row_ins = [pltpu.make_async_copy(src, held.at[i], row_in.at[i]) for i, src in enumerate((n_ref, a_ref, t_ref))]
    row_outs = [pltpu.make_async_copy(held.at[i], dst, row_out.at[i]) for i, dst in enumerate((n_out, a_out, t_out))]
    quarter = CHUNKS // 4
    ins = [pltpu.make_async_copy(g_ref.at[pl.ds(i * size, size)], packed.at[i], in_sem.at[i]) for i in range(CHUNKS)]
    outs = [
        pltpu.make_async_copy(
            wide.at[i],
            (w_out, h_out)[i // quarter % 2].at[pl.ds((i % quarter + (quarter if i < 2 * quarter else 0)) * size, size)],
            out_sem.at[i],
        )
        for i in range(CHUNKS)
    ]
    for cp in ins + row_ins:
        cp.start()
    for i in range(CHUNKS):
        ins[i].wait()
        wide[i] = packed[i].astype(F32)
        outs[i].start()
    for i in range(3):
        row_ins[i].wait()
        row_outs[i].start()
    for cp in outs + row_outs:
        cp.wait()


def on_device(n, ny, nz, u, v, c, w1, w2, t1, t2, nb):
    F = n
    cells = 6 * F
    shard, p0, p1, qn = split_rows(ny, nz)
    u, v, c = (a.reshape(6, F, C) for a in (u, v, c))
    w1, w2, t1, t2 = (a.reshape(K9, C) for a in (w1, w2, t1, t2))
    vm = pltpu.VMEM
    dma = pltpu.SemaphoreType.DMA
    anywhere = pl.BlockSpec(memory_space=pl.ANY)
    inside = pl.BlockSpec(memory_space=pltpu.VMEM)
    row = jax.ShapeDtypeStruct((6, F, C), BF)
    nxt, adj, adt, out = pl.pallas_call(
        functools.partial(kernel, n, ny, nz),
        out_shape=(row, row, row, jax.ShapeDtypeStruct((ny, nz, shard, C), BF)),
        in_specs=[anywhere] * 8,
        out_specs=(anywhere,) * 4,
        scratch_shapes=[
            vm((2, 3, 3, 6, F, C), BF),
            vm((2, 3, 6, F, C), BF),
            vm((2, 160, C), BF),
            vm((2, 64, C), BF),
            vm((2, F, 32, C), BF),
            vm((2, F, 32, C), BF),
            vm((2, 3, 48, C), BF),
            vm((48, 160), BF),
            vm((64, 48), BF),
            vm((8 * F, cells), BF),
            vm((cells, 8 * F), BF),
            vm((cells, cells), BF),
            vm((cells, cells), BF),
            vm((4, K9, C), BF),
            vm((K9, 2 * C), BF),
            vm((K9, 2 * C), BF),
            vm((K9, 2 * C), BF),
            vm((6, F + 16, C), F32),
            vm((cells + SIDES, K9), BF),
            vm((cells + SIDES, K9), BF),
            vm((cells + SIDES, K9), BF),
            vm((cells, K9), BF),
            vm((cells + SIDES, 2 * C), BF),
            vm((cells + SIDES, 2 * C), BF),
            vm((6, F, 2 * C), F32),
            vm((6, F, 2 * C), F32),
            vm((4 * K9, C), F32),
            vm((ny, nz, shard, C), BF),
            vm((ny, nz, shard, C), BF),
            vm((ny, nz, p0, C), F32),
            vm((ny, nz, p0, C), BF),
            vm((ny, nz, p0, C), BF),
            vm((ny, nz, qn, C), F32),
            vm((ny, nz, qn, C), BF),
            vm((nz, ny, qn, C), BF),
            vm((nz, p0, C), BF),
            vm((nz, p0, C), F32),
            vm((nz, p0, C), BF),
            vm((ny, qn, C), BF),
            vm((ny, qn, C), F32),
            vm((ny, qn, C), BF),
            pltpu.SMEM((4, 6), jnp.int32),
            vm((3, 6, F, C), BF),
            vm((p0, C), BF),
            vm((qn, C), BF),
            dma((5,)),
            dma((8,)),
            dma((2, 3)),
            dma((2, 3, 2)),
            dma((2,)),
            dma((2,)),
            dma((2, 2)),
            dma((2,)),
            dma((2,)),
            dma((2, 2)),
            dma((2, 2)),
            dma((2, 2)),
            dma((len(STEPS),)),
            dma((len(STEPS) + ny + nz,)),
        ],
        compiler_params=pltpu.CompilerParams(
            collective_id=0, has_side_effects=True, vmem_limit_bytes=56 * 2**20
        ),
    )(u, v, c, w1, w2, t1, t2, nb.T)
    half = 2 * K9
    grad = jax.ShapeDtypeStruct((half, C), F32)
    nxt, adj, adt, wg, hp = pl.pallas_call(
        finish,
        out_shape=(row, row, row, grad, grad),
        in_specs=[anywhere] * 4,
        out_specs=(anywhere,) * 5,
        scratch_shapes=[vm((CHUNKS, 2 * half // CHUNKS, C), BF), vm((CHUNKS, 2 * half // CHUNKS, C), F32), vm((3, 6, F, C), BF), dma((CHUNKS,)), dma((CHUNKS,)), dma((3,)), dma((3,))],
        compiler_params=pltpu.CompilerParams(vmem_limit_bytes=56 * 2**20),
    )(nxt, adj, adt, out.reshape(2 * half, C))
    shape4 = (2, 9, C, C)
    shape = (6, 1, F, C)
    return nxt.reshape(shape), adj.reshape(shape), adt.reshape(shape), wg.reshape(shape4), hp.reshape(shape4)


def solution(mesh):
    n = mesh.shape["tile"] * mesh.shape["sub"]
    nz = 8 if n == 64 else 2
    ny = n // (2 * nz)
    field = P("rep", ("tile", "sub"), None, None)
    grads = P("rep", None, None, None)
    return jax.shard_map(
        functools.partial(on_device, n, ny, nz),
        mesh=mesh,
        in_specs=(field, field, field, P(), P(), P(), P(), P()),
        out_specs=(field, field, field, grads, grads),
        check_vma=False,
    )
```
